32 devices in a mesh: groups: 2 (over y), tensor: 16 (over z, x, core).
Axes of the slice: x: 2, y: 2, z: 4, core: 2. Of those that a mesh axis runs over, the one named last changes fastest.
Arguments:
- tokens: bfloat16 [32, 8192], P(('groups', 'tensor')), parts along dimension 0, may hold values from -6 to 6
- norm_gain: bfloat16 [8192], replicated, may hold values from 0.5 to 1.5
- w_gate: bfloat16 [8192, 28672], P(None, 'tensor'), may hold values from -0.0625 to 0.0625
- w_up: bfloat16 [8192, 28672], P(None, 'tensor'), may hold values from -0.0625 to 0.0625
- w_down: bfloat16 [28672, 8192], P('tensor'), may hold values from -0.03125 to 0.03125
- lengths: int32 [16], P('groups'), parts along dimension 0, may hold values from 1 to 4, 16 in all
- hit_lengths: int32 [16], P('groups'), parts along dimension 0, may hold values from 0 to 4095, as said below
- start_positions: int32 [16], P('groups'), parts along dimension 0, may hold values from 0 to 4093
Outputs:
- block_out: bfloat16 [32, 8192], P(('groups', 'tensor')), parts along dimension 0
The draws below stay inside these ranges and needn't reach their ends.
There are 2 independent parts, one for each index of `groups`. The reference program is written for one: setup_inputs(seed, part) draws one part's arguments, and reference() takes and returns one part's arrays. A program takes and returns all parts, laid end to end along the dimension named above; an argument that names none is the same for every part. Nothing has to cross between parts.
Inputs may be any that keep to these rules, and one draw needn't show every extreme that they name: start_positions[r] <= hit_lengths[r] <= start_positions[r] + 2.
All inputs are finite; a program needn't handle non-finite values.
Results may differ from the reference program's by a relative error of at most 0.0071.
Values may be sent and summed in bfloat16 or wider, within the bound.
No kernel may reach another device: no remote copies, remote signals or barrier semaphores. Data moves between devices by JAX's collectives and lax.ppermute only.
A program may use at most 192 MiB of HBM per device.

```python
import math
import jax
import jax.numpy as jnp
import numpy as np
from jax import lax

D = 8192
FF = 28672
REQS = 8
HORIZON = 4096
TOKENS = 16
LMAX = 4
N_TENSOR = 16


def shared_positions(key):
    begin = jax.random.randint(jax.random.fold_in(key, 11), (REQS,), 0, HORIZON - 2).astype(jnp.int32)
    extra = jax.random.randint(jax.random.fold_in(key, 12), (REQS,), 0, 3).astype(jnp.int32)
    return (begin, extra)


def draw_start_positions(key, part):
    begin, extra = shared_positions(key)
    return begin


def draw_hit_lengths(key, part):
    begin, extra = shared_positions(key)
    return (begin + extra).astype(jnp.int32)


def block_scale(key, extent, shards, low, top_value):
    level = 1.0
    for axis_at, shards_of in shards:
        heights = jax.random.uniform(jax.random.fold_in(jax.random.fold_in(key, 6), axis_at), (shards_of,), jnp.float32, low / len(shards), top_value / len(shards))
        level = level * jnp.repeat(jnp.exp(heights), extent[axis_at] // shards_of).reshape((-1,) + (1,) * (len(extent) - 1 - axis_at))
    return level


def profile(amount, total, limit, lean):
    weights = [(1 << 20) // math.isqrt(rank ** lean) + 1 for rank in range(2, amount + 1)]
    surplus, given = total - limit - (amount - 1), [1] * (amount - 1)
    while surplus > 0:
        free = [i for i in range(amount - 1) if given[i] < limit]
        pool, budget = sum([weights[i] for i in free]), surplus
        for i in free:
            more = min(limit - given[i], max(1, budget * weights[i] // pool), surplus)
            given[i] = given[i] + more
            surplus = surplus - more
    return np.array([limit] + given)


def ragged_sizes(stream_key, count, total, reach, lean):
    if count == 2:
        one = jax.random.randint(stream_key, (), max(1, total - reach), min(reach, total - 1) + 1)
        return jnp.stack([one, total - one])
    tallies = jnp.asarray(profile(count, total, reach, lean), jnp.int32)
    couples = (count - 1) // 2
    giver, taker = tallies[1:1 + 2 * couples:2], tallies[2:2 + 2 * couples:2]
    room = jnp.minimum(giver - 1, reach - taker)
    moved = jax.random.randint(jax.random.fold_in(stream_key, 1), (couples,), 0, 1 << 20) % (room + 1)
    tallies = tallies.at[1:1 + 2 * couples:2].set(giver - moved).at[2:2 + 2 * couples:2].set(taker + moved)
    return tallies[jax.random.permutation(jax.random.fold_in(stream_key, 2), count)]


def scatter_about(own_key, shape, width, most, shards=(), kind=jnp.bfloat16):
    gain = block_scale(own_key, shape, shards, -0.22, 0.18) if shards else 1.0
    values = jax.random.normal(own_key, shape, jnp.float32) * width * gain
    return jnp.minimum(jnp.maximum(values, -most), most).astype(kind)


def setup_inputs(seed: int = 0, part: int = 0) -> dict:
    arg_keys = jax.random.split(jax.random.key(seed), 9)
    own_keys = jax.random.split(jax.random.fold_in(arg_keys[8], part), 9)
    return {
        "tokens": scatter_about(own_keys[0], (TOKENS, D), 1.0, 6.0, ((0, 16),)),
        "norm_gain": jnp.clip(jax.random.uniform(arg_keys[1], (D,), jnp.float32, 0.5, 1.5), 0.5, 1.5).astype(jnp.bfloat16),
        "w_gate": scatter_about(arg_keys[2], (D, FF), D ** -0.5, 0.0625, ((1, 16),)),
        "w_up": scatter_about(arg_keys[3], (D, FF), D ** -0.5, 0.0625, ((1, 16),)),
        "w_down": scatter_about(arg_keys[4], (FF, D), FF ** -0.5, 0.03125, ((0, 16),)),
        "lengths": ragged_sizes(own_keys[5], REQS, TOKENS, LMAX, 1).astype(jnp.int32),
        "hit_lengths": draw_hit_lengths(jax.random.fold_in(jax.random.fold_in(arg_keys[8], part), 71), part),
        "start_positions": draw_start_positions(jax.random.fold_in(jax.random.fold_in(arg_keys[8], part), 71), part),
    }


def normalize(tokens, norm_gain):
    values = tokens.astype(jnp.float32)
    mean_sq = lax.optimization_barrier(jnp.mean(values * values, axis=-1, keepdims=True))
    return (values * lax.rsqrt(mean_sq + 1e-05) * norm_gain.astype(jnp.float32)).astype(jnp.bfloat16)

def live_rows(lengths, hit_lengths, start_positions, token_index):
    ends = jnp.cumsum(lengths).astype(jnp.int32)
    begins = (ends - lengths).astype(jnp.int32)
    member = (token_index[:, None] >= begins[None, :]) & (token_index[:, None] < ends[None, :])
    member_int = member.astype(jnp.int32)
    offsets = token_index - lax.optimization_barrier(jnp.sum(member_int * begins[None, :], axis=1)).astype(jnp.int32)
    position = lax.optimization_barrier(jnp.sum(member_int * start_positions[None, :], axis=1)).astype(jnp.int32) + offsets
    covered = lax.optimization_barrier(jnp.sum(member_int * hit_lengths[None, :], axis=1)).astype(jnp.int32)
    return position >= covered

def reference(tokens, norm_gain, w_gate, w_up, w_down, lengths, hit_lengths, start_positions):
    normed = normalize(tokens, norm_gain)
    gate_out = jnp.dot(normed, w_gate, preferred_element_type=jnp.float32)
    up_out = jnp.dot(normed, w_up, preferred_element_type=jnp.float32)
    hidden = (jax.nn.silu(gate_out) * up_out).astype(jnp.bfloat16)
    unit_count = FF // N_TENSOR
    hidden_blocks = hidden.reshape(TOKENS, N_TENSOR, unit_count).transpose(1, 0, 2)
    down_blocks = w_down.reshape(N_TENSOR, unit_count, D)

    def accumulate(totals, operands):
        block_hidden, block_down = operands
        partial_value = jnp.dot(block_hidden, block_down, preferred_element_type=jnp.float32)
        rounded = lax.optimization_barrier(partial_value.astype(jnp.bfloat16))
        return (totals + rounded.astype(jnp.float32), None)
    start_totals = jnp.zeros((TOKENS, D), jnp.float32)
    totals, unused = lax.scan(accumulate, start_totals, (hidden_blocks, down_blocks))
    live = live_rows(lengths, hit_lengths, start_positions, jnp.arange(TOKENS, dtype=jnp.int32))
    return jnp.where(live[:, None], totals, jnp.zeros_like(totals)).astype(jnp.bfloat16)
```

```python
import functools

import jax
import jax.numpy as jnp
from jax import lax
from jax.experimental import pallas as pl
from jax.experimental.pallas import tpu as pltpu
from jax.sharding import PartitionSpec as P

LANES = 128
BOTH = ("groups", "tensor")


def normalize(tokens, norm_gain):
    values = tokens.astype(jnp.float32)
    mean_sq = jnp.mean(values * values, axis=-1, keepdims=True)
    return (values * lax.rsqrt(mean_sq + 1e-05) * norm_gain.astype(jnp.float32)).astype(
        jnp.bfloat16
    )


def live_rows(lengths, hit_lengths, start_positions, token_index):
    ends = jnp.cumsum(lengths)
    begins = ends - lengths
    member = (token_index[:, None] >= begins[None, :]) & (token_index[:, None] < ends[None, :])
    member_int = member.astype(jnp.int32)
    offsets = token_index - jnp.sum(member_int * begins[None, :], axis=1)
    position = jnp.sum(member_int * start_positions[None, :], axis=1) + offsets
    covered = jnp.sum(member_int * hit_lengths[None, :], axis=1)
    return position >= covered


def local(tokens, norm_gain, w_gate, w_up, w_down, lengths, hit_lengths, start_positions):
    row_count = tokens.shape[0]
    normed = normalize(tokens, norm_gain)
    piece_rows = lax.all_gather(normed, "tensor", axis=0, tiled=True)
    gate_out = jnp.dot(piece_rows, w_gate, preferred_element_type=jnp.float32)
    up_out = jnp.dot(piece_rows, w_up, preferred_element_type=jnp.float32)
    hidden = (jax.nn.silu(gate_out) * up_out).astype(jnp.bfloat16)
    partial_value = jnp.dot(hidden, w_down, preferred_element_type=jnp.float32)
    rounded = partial_value.astype(jnp.bfloat16)
    totals = jnp.sum(
        lax.all_to_all(rounded[None], "tensor", split_axis=1, concat_axis=0, tiled=True).astype(
            jnp.float32
        ),
        axis=0,
    )
    token_index = lax.axis_index("tensor") * row_count + jnp.arange(row_count, dtype=jnp.int32)
    live = live_rows(lengths, hit_lengths, start_positions, token_index)
    return jnp.where(live[:, None], totals, jnp.zeros_like(totals)).astype(jnp.bfloat16)


def load_kernel(half, gate_hbm, up_hbm, down_hbm, both_vmem, down_vmem, sems):
    own = pl.multiple_of(lax.axis_index("groups") * half, LANES)
    copies = [
        pltpu.make_async_copy(
            gate_hbm.at[:, pl.ds(own, half)], both_vmem.at[:, pl.ds(0, half)], sems.at[0]
        ),
        pltpu.make_async_copy(
            up_hbm.at[:, pl.ds(own, half)], both_vmem.at[:, pl.ds(half, half)], sems.at[1]
        ),
        pltpu.make_async_copy(down_hbm.at[pl.ds(own, half), :], down_vmem, sems.at[2]),
    ]
    for copy in copies:
        copy.start()
    for copy in copies:
        copy.wait()


def load_weights(w_gate, w_up, w_down, half):
    depth = w_gate.shape[0]
    width = w_down.shape[1]
    return pl.pallas_call(
        functools.partial(load_kernel, half),
        out_shape=(
            pltpu.VMEM((depth, 2 * half), w_gate.dtype),
            pltpu.VMEM((half, width), w_down.dtype),
        ),
        in_specs=[pl.BlockSpec(memory_space=pl.ANY)] * 3,
        out_specs=(
            pl.BlockSpec(memory_space=pltpu.VMEM),
            pl.BlockSpec(memory_space=pltpu.VMEM),
        ),
        scratch_shapes=[pltpu.SemaphoreType.DMA((3,))],
        compiler_params=pltpu.CompilerParams(vmem_limit_bytes=1 << 20),
        cost_estimate=pl.CostEstimate(
            flops=0, bytes_accessed=3 * depth * half * 2, transcendentals=0
        ),
        name="load_weights",
    )(w_gate, w_up, w_down)


def block_kernel(
    half, tokens_ref, gain_ref, both_ref, down_ref, out_ref, wide_ref, normed_ref, hidden_ref
):
    rows, lines, lanes = tokens_ref.shape
    depth = lines * lanes
    wide_ref[...] = tokens_ref[...].astype(jnp.float32)
    squares = wide_ref[:, 0, :] * wide_ref[:, 0, :]
    for line in range(1, lines):
        value = wide_ref[:, line, :]
        squares = squares + value * value
    scale = lax.rsqrt(jnp.sum(squares, axis=-1, keepdims=True) * (1.0 / depth) + 1e-05)
    for line in range(lines):
        columns = pl.ds(line * lanes, lanes)
        normed_ref[:, columns] = (
            wide_ref[:, line, :] * scale * gain_ref[:, columns].astype(jnp.float32)
        ).astype(jnp.bfloat16)
    tile = 256
    parts = []
    for at in range(0, 2 * half, tile):
        parts.append(
            jnp.dot(
                normed_ref[...], both_ref[:, pl.ds(at, tile)], preferred_element_type=jnp.float32
            )
        )
    product = jnp.concatenate(parts, axis=1)
    gate_out = product[:, :half]
    up_out = product[:, half:]
    hidden_ref[...] = (gate_out / (1.0 + jnp.exp(-gate_out)) * up_out).astype(jnp.bfloat16)
    for at in range(0, depth, tile):
        result = jnp.dot(
            hidden_ref[...], down_ref[:, pl.ds(at, tile)], preferred_element_type=jnp.float32
        )
        for step in range(tile // lanes):
            wide_ref[:, at // lanes + step, :] = result[:, step * lanes : (step + 1) * lanes]
    out_ref[...] = wide_ref[...].astype(jnp.bfloat16)


def block(tokens, gain, both, down, half):
    rows, lines, lanes = tokens.shape
    depth = lines * lanes
    vmem = pl.BlockSpec(memory_space=pltpu.VMEM)
    return pl.pallas_call(
        functools.partial(block_kernel, half),
        out_shape=jax.ShapeDtypeStruct(tokens.shape, jnp.bfloat16),
        in_specs=[vmem] * 4,
        out_specs=vmem,
        scratch_shapes=[
            pltpu.VMEM(tokens.shape, jnp.float32),
            pltpu.VMEM((rows, depth), jnp.bfloat16),
            pltpu.VMEM((rows, half), jnp.bfloat16),
        ],
        compiler_params=pltpu.CompilerParams(vmem_limit_bytes=12 << 20),
        cost_estimate=pl.CostEstimate(
            flops=6 * rows * depth * half, bytes_accessed=2 * rows * depth * 2, transcendentals=0
        ),
        name="block",
    )(
        tokens,
        gain,
        pltpu.with_memory_space_constraint(both, pltpu.VMEM),
        pltpu.with_memory_space_constraint(down, pltpu.VMEM),
    )


def shared(tokens, norm_gain, w_gate, w_up, w_down, lengths, hit_lengths, start_positions):
    row_count, depth = tokens.shape
    members = lax.axis_size("groups") * lax.axis_size("tensor")
    half = w_gate.shape[1] // lax.axis_size("groups")
    mine = tokens.reshape(1, row_count, depth // LANES, LANES)
    everywhere = jnp.broadcast_to(mine, (members,) + mine.shape[1:])
    gathered = lax.all_to_all(everywhere, BOTH, split_axis=0, concat_axis=0, tiled=True)
    both, down = load_weights(w_gate, w_up, w_down, half)
    partials = block(
        gathered.reshape(members * row_count, depth // LANES, LANES),
        norm_gain.reshape(1, depth),
        both,
        down,
        half,
    )
    arrived = lax.all_to_all(
        partials.reshape((members,) + mine.shape[1:]), BOTH, split_axis=0, concat_axis=0, tiled=True
    )
    totals = jnp.sum(arrived.astype(jnp.float32), axis=0)
    token_index = lax.axis_index("tensor") * row_count + jnp.arange(row_count, dtype=jnp.int32)
    live = live_rows(lengths, hit_lengths, start_positions, token_index)
    kept = jnp.where(live[:, None, None], totals, jnp.zeros_like(totals)).astype(jnp.bfloat16)
    return kept.reshape(row_count, depth)


def solution(mesh):
    placed = (
        P(("groups", "tensor"), None),
        P(),
        P(None, "tensor"),
        P(None, "tensor"),
        P("tensor", None),
        P("groups"),
        P("groups"),
        P("groups"),
    )

    def run(*arrays):
        units = arrays[2].shape[1] // mesh.shape["tensor"]
        halves = units % (LANES * mesh.shape["groups"]) == 0
        body = shared if halves else local
        return jax.shard_map(
            body,
            mesh=mesh,
            in_specs=placed,
            out_specs=P(("groups", "tensor"), None),
            check_vma=False,
        )(*arrays)

    return run
```

```python
import functools

import jax
import jax.numpy as jnp
from jax import lax
from jax.experimental import pallas as pl
from jax.experimental.pallas import tpu as pltpu
from jax.sharding import PartitionSpec as P

LANES = 128
BOTH = ("groups", "tensor")


def normalize(tokens, norm_gain):
    values = tokens.astype(jnp.float32)
    mean_sq = jnp.mean(values * values, axis=-1, keepdims=True)
    return (values * lax.rsqrt(mean_sq + 1e-05) * norm_gain.astype(jnp.float32)).astype(
        jnp.bfloat16
    )


def live_rows(lengths, hit_lengths, start_positions, token_index):
    ends = jnp.cumsum(lengths)
    begins = ends - lengths
    member = (token_index[:, None] >= begins[None, :]) & (token_index[:, None] < ends[None, :])
    member_int = member.astype(jnp.int32)
    offsets = token_index - jnp.sum(member_int * begins[None, :], axis=1)
    position = jnp.sum(member_int * start_positions[None, :], axis=1) + offsets
    covered = jnp.sum(member_int * hit_lengths[None, :], axis=1)
    return position >= covered


def local(tokens, norm_gain, w_gate, w_up, w_down, lengths, hit_lengths, start_positions):
    row_count = tokens.shape[0]
    normed = normalize(tokens, norm_gain)
    piece_rows = lax.all_gather(normed, "tensor", axis=0, tiled=True)
    gate_out = jnp.dot(piece_rows, w_gate, preferred_element_type=jnp.float32)
    up_out = jnp.dot(piece_rows, w_up, preferred_element_type=jnp.float32)
    hidden = (jax.nn.silu(gate_out) * up_out).astype(jnp.bfloat16)
    partial_value = jnp.dot(hidden, w_down, preferred_element_type=jnp.float32)
    rounded = partial_value.astype(jnp.bfloat16)
    totals = jnp.sum(
        lax.all_to_all(rounded[None], "tensor", split_axis=1, concat_axis=0, tiled=True).astype(
            jnp.float32
        ),
        axis=0,
    )
    token_index = lax.axis_index("tensor") * row_count + jnp.arange(row_count, dtype=jnp.int32)
    live = live_rows(lengths, hit_lengths, start_positions, token_index)
    return jnp.where(live[:, None], totals, jnp.zeros_like(totals)).astype(jnp.bfloat16)


def columns_of(tile, ref):
    return [pl.ds(at, tile) for at in range(0, ref.shape[1], tile)]


def load_kernel(half, gate_hbm, up_hbm, both_vmem, sems):
    own = pl.multiple_of(lax.axis_index("groups") * half, LANES)
    depth = both_vmem.shape[0]
    copies = [
        pltpu.make_async_copy(
            weight.at[pl.ds(0, depth), pl.ds(own, half)],
            both_vmem.at[:, pl.ds(at * half, half)],
            sems.at[at],
        )
        for at, weight in enumerate((gate_hbm, up_hbm))
    ]
    for copy in copies:
        copy.start()
    for copy in copies:
        copy.wait()


def load_weights(w_gate, w_up, half, depth):
    return pl.pallas_call(
        functools.partial(load_kernel, half),
        out_shape=pltpu.VMEM((depth, 2 * half), w_gate.dtype),
        in_specs=[pl.BlockSpec(memory_space=pltpu.HBM)] * 2,
        out_specs=pl.BlockSpec(memory_space=pltpu.VMEM),
        scratch_shapes=[pltpu.SemaphoreType.DMA((2,))],
        compiler_params=pltpu.CompilerParams(vmem_limit_bytes=1 << 20),
        cost_estimate=pl.CostEstimate(
            flops=0, bytes_accessed=2 * depth * half * 2, transcendentals=0
        ),
        name="load_weights",
    )(w_gate, w_up)


def block_kernel(
    half,
    chunk,
    near_ref,
    far_ref,
    gain_ref,
    first_ref,
    gate_hbm,
    up_hbm,
    down_hbm,
    out_ref,
    wide_ref,
    normed_ref,
    product_ref,
    hidden_ref,
    rest_ref,
    down_ref,
    both_sems,
    down_sems,
):
    tile = 256
    rows, lines, lanes = out_ref.shape
    depth = lines * lanes
    loaded = first_ref.shape[0]
    own = pl.multiple_of(lax.axis_index("groups") * half, LANES)
    both_copies = []
    for step, at in enumerate(range(0, depth - loaded, chunk)):
        both_copies.append(
            [
                pltpu.make_async_copy(
                    weight.at[pl.ds(loaded + at, chunk), pl.ds(own, half)],
                    rest_ref.at[pl.ds(at, chunk), pl.ds(side * half, half)],
                    both_sems.at[step, side],
                )
                for side, weight in enumerate((gate_hbm, up_hbm))
            ]
        )
    down_copies = [
        pltpu.make_async_copy(
            down_hbm.at[pl.ds(own, half), pl.ds(at, chunk)],
            down_ref.at[:, pl.ds(at, chunk)],
            down_sems.at[step],
        )
        for step, at in enumerate(range(0, depth, chunk))
    ]
    for pair in both_copies:
        for copy in pair:
            copy.start()
    for copy in down_copies:
        copy.start()

    wide_ref[: rows // 2] = near_ref[...].astype(jnp.float32)
    wide_ref[rows // 2 :] = far_ref[...].astype(jnp.float32)
    squares = wide_ref[:, 0, :] * wide_ref[:, 0, :]
    for line in range(1, lines):
        value = wide_ref[:, line, :]
        squares = squares + value * value
    scale = lax.rsqrt(jnp.sum(squares, axis=-1, keepdims=True) * (1.0 / depth) + 1e-05)
    for line in range(lines):
        columns = pl.ds(line * lanes, lanes)
        normed_ref[:, columns] = (
            wide_ref[:, line, :] * scale * gain_ref[:, columns].astype(jnp.float32)
        ).astype(jnp.bfloat16)

    for columns in columns_of(tile, product_ref):
        product_ref[:, columns] = jnp.dot(
            normed_ref[:, :loaded], first_ref[:, columns], preferred_element_type=jnp.float32
        )
    for step, pair in enumerate(both_copies):
        for copy in pair:
            copy.wait()
        at = step * chunk
        for columns in columns_of(tile, product_ref):
            product_ref[:, columns] += jnp.dot(
                normed_ref[:, loaded + at : loaded + at + chunk],
                rest_ref[at : at + chunk, columns],
                preferred_element_type=jnp.float32,
            )
    gate_out = product_ref[:, :half]
    up_out = product_ref[:, half:]
    hidden_ref[...] = (gate_out / (1.0 + jnp.exp(-gate_out)) * up_out).astype(jnp.bfloat16)
    for step, copy in enumerate(down_copies):
        copy.wait()
        for at in range(step * chunk, (step + 1) * chunk, tile):
            result = jnp.dot(
                hidden_ref[...], down_ref[:, pl.ds(at, tile)], preferred_element_type=jnp.float32
            )
            for line in range(tile // lanes):
                wide_ref[:, at // lanes + line, :] = result[:, line * lanes : (line + 1) * lanes]
        lines_done = pl.ds(step * chunk // lanes, chunk // lanes)
        out_ref[:, lines_done, :] = wide_ref[:, lines_done, :].astype(jnp.bfloat16)


def block(near, far, gain, first, w_gate, w_up, w_down, half):
    rows, lines, lanes = near.shape
    rows = 2 * rows
    depth = lines * lanes
    chunk = 1024
    rest = depth - first.shape[0]
    vmem = pl.BlockSpec(memory_space=pltpu.VMEM)
    hbm = pl.BlockSpec(memory_space=pltpu.HBM)
    return pl.pallas_call(
        functools.partial(block_kernel, half, chunk),
        out_shape=jax.ShapeDtypeStruct((rows, lines, lanes), jnp.bfloat16),
        in_specs=[vmem] * 4 + [hbm] * 3,
        out_specs=vmem,
        scratch_shapes=[
            pltpu.VMEM((rows, lines, lanes), jnp.float32),
            pltpu.VMEM((rows, depth), jnp.bfloat16),
            pltpu.VMEM((rows, 2 * half), jnp.float32),
            pltpu.VMEM((rows, half), jnp.bfloat16),
            pltpu.VMEM((rest, 2 * half), jnp.bfloat16),
            pltpu.VMEM((half, depth), jnp.bfloat16),
            pltpu.SemaphoreType.DMA((rest // chunk, 2)),
            pltpu.SemaphoreType.DMA((depth // chunk,)),
        ],
        compiler_params=pltpu.CompilerParams(
            vmem_limit_bytes=(rest * 2 + depth) * half * 2 + (6 << 20)
        ),
        cost_estimate=pl.CostEstimate(
            flops=6 * rows * depth * half,
            bytes_accessed=(rest * 2 + depth) * half * 2,
            transcendentals=0,
        ),
        name="block",
    )(near, far, gain, pltpu.with_memory_space_constraint(first, pltpu.VMEM), w_gate, w_up, w_down)


def swap(value, offset):
    members = lax.axis_size("groups") * lax.axis_size("tensor")
    return lax.ppermute(value, BOTH, [(place, place ^ offset) for place in range(members)])


def stages(members):
    bits = members.bit_length() - 1
    core, column, group = (0,), (1, bits - 1), tuple(range(2, bits - 1))
    return [[1 << bit for bit in stage] for stage in (group, column, core)]


def offsets(steps):
    found = [0]
    for step in steps:
        found = found + [at + step for at in found]
    return found


def gather(value, members):
    early, late, last = stages(members)
    for steps in (early, late):
        value = jnp.concatenate(
            [swap(value, at) if at else value for at in offsets(steps)], axis=0
        )
    return value, swap(value, last[0])


def scatter_sum(value, members):
    for steps in reversed(stages(members)):
        reach = offsets(steps)
        pieces = jnp.split(value, len(reach), axis=0)
        total = pieces[0].astype(jnp.float32)
        for at, piece in zip(reach[1:], pieces[1:]):
            total = total + swap(piece.astype(jnp.bfloat16), at).astype(jnp.float32)
        value = total.astype(jnp.bfloat16)
    return total


def shared(tokens, norm_gain, w_gate, w_up, w_down, lengths, hit_lengths, start_positions):
    row_count, depth = tokens.shape
    members = lax.axis_size("groups") * lax.axis_size("tensor")
    half = w_gate.shape[1] // lax.axis_size("groups")
    token_index = lax.axis_index("tensor") * row_count + jnp.arange(row_count, dtype=jnp.int32)
    live = live_rows(lengths, hit_lengths, start_positions, token_index)
    near, far = gather(tokens.reshape(row_count, depth // LANES, LANES), members)
    w_gate, w_up, w_down = (
        pltpu.with_memory_space_constraint(weight, pltpu.HBM) for weight in (w_gate, w_up, w_down)
    )
    first = load_weights(w_gate, w_up, half, depth // 2)
    partials = block(near, far, norm_gain.reshape(1, depth), first, w_gate, w_up, w_down, half)
    totals = scatter_sum(partials, members)
    kept = jnp.where(live[:, None, None], totals, jnp.zeros_like(totals)).astype(jnp.bfloat16)
    return kept.reshape(row_count, depth)


def solution(mesh):
    placed = (
        P(("groups", "tensor"), None),
        P(),
        P(None, "tensor"),
        P(None, "tensor"),
        P("tensor", None),
        P("groups"),
        P("groups"),
        P("groups"),
    )

    def run(*arrays):
        units = arrays[2].shape[1] // mesh.shape["tensor"]
        members = mesh.shape["groups"] * mesh.shape["tensor"]
        halves = (
            units % (LANES * mesh.shape["groups"]) == 0
            and arrays[0].shape[0] == members
            and mesh.shape["groups"] == 2
            and members & (members - 1) == 0
            and members >= 8
        )
        body = shared if halves else local
        return jax.shard_map(
            body,
            mesh=mesh,
            in_specs=placed,
            out_specs=P(("groups", "tensor"), None),
            check_vma=False,
        )(*arrays)

    return run
```

```python
import functools

import jax
import jax.numpy as jnp
from jax import lax
from jax.experimental import pallas as pl
from jax.experimental.pallas import tpu as pltpu
from jax.sharding import PartitionSpec as P

LANES = 128
ROW_LINES = ("groups", "z", "x", "core")


def normalize(tokens, norm_gain):
    values = tokens.astype(jnp.float32)
    mean_sq = jnp.mean(values * values, axis=-1, keepdims=True)
    return (values * lax.rsqrt(mean_sq + 1e-05) * norm_gain.astype(jnp.float32)).astype(
        jnp.bfloat16
    )


def live_rows(lengths, hit_lengths, start_positions, token_index):
    ends = jnp.cumsum(lengths)
    begins = ends - lengths
    member = (token_index[:, None] >= begins[None, :]) & (token_index[:, None] < ends[None, :])
    member_int = member.astype(jnp.int32)
    offsets = token_index - jnp.sum(member_int * begins[None, :], axis=1)
    position = jnp.sum(member_int * start_positions[None, :], axis=1) + offsets
    covered = jnp.sum(member_int * hit_lengths[None, :], axis=1)
    return position >= covered


def local(tokens, norm_gain, w_gate, w_up, w_down, lengths, hit_lengths, start_positions):
    row_count = tokens.shape[0]
    normed = normalize(tokens, norm_gain)
    piece_rows = lax.all_gather(normed, "tensor", axis=0, tiled=True)
    gate_out = jnp.dot(piece_rows, w_gate, preferred_element_type=jnp.float32)
    up_out = jnp.dot(piece_rows, w_up, preferred_element_type=jnp.float32)
    hidden = (jax.nn.silu(gate_out) * up_out).astype(jnp.bfloat16)
    partial_value = jnp.dot(hidden, w_down, preferred_element_type=jnp.float32)
    rounded = partial_value.astype(jnp.bfloat16)
    totals = jnp.sum(
        lax.all_to_all(rounded[None], "tensor", split_axis=1, concat_axis=0, tiled=True).astype(
            jnp.float32
        ),
        axis=0,
    )
    token_index = lax.axis_index("tensor") * row_count + jnp.arange(row_count, dtype=jnp.int32)
    live = live_rows(lengths, hit_lengths, start_positions, token_index)
    return jnp.where(live[:, None], totals, jnp.zeros_like(totals)).astype(jnp.bfloat16)


def live_flag(lengths, hit_lengths, start_positions, token):
    begin = 0
    live = False
    for request in range(lengths.shape[0]):
        end = begin + lengths[request]
        position = start_positions[request] + token - begin
        inside = (token >= begin) & (token < end)
        live = live | (inside & (position >= hit_lengths[request]))
        begin = end
    return live


def load_kernel(
    half, place, lengths, hit_lengths, start_positions, gate_hbm, up_hbm, both_vmem, keep_vmem, sems
):
    own = pl.multiple_of(lax.axis_index("groups") * half, LANES)
    depth = both_vmem.shape[0]
    copies = [
        pltpu.make_async_copy(
            weight.at[pl.ds(0, depth), pl.ds(own, half)],
            both_vmem.at[:, pl.ds(at * half, half)],
            sems.at[at],
        )
        for at, weight in enumerate((gate_hbm, up_hbm))
    ]
    for copy in copies:
        copy.start()
    live = live_flag(lengths, hit_lengths, start_positions, place())
    keep_vmem[...] = jnp.full(keep_vmem.shape, live.astype(jnp.float32), jnp.float32)
    for copy in copies:
        copy.wait()


def load_weights(requests, w_gate, w_up, half, depth, place):
    smem = pl.BlockSpec(memory_space=pltpu.SMEM)
    vmem = pl.BlockSpec(memory_space=pltpu.VMEM)
    hbm = pl.BlockSpec(memory_space=pltpu.HBM)
    return pl.pallas_call(
        functools.partial(load_kernel, half, place),
        out_shape=(
            pltpu.VMEM((depth, 2 * half), w_gate.dtype),
            jax.ShapeDtypeStruct((8, LANES), jnp.float32),
        ),
        in_specs=[smem] * 3 + [hbm] * 2,
        out_specs=(vmem, vmem),
        scratch_shapes=[pltpu.SemaphoreType.DMA((2,))],
        compiler_params=pltpu.CompilerParams(vmem_limit_bytes=1 << 20),
        cost_estimate=pl.CostEstimate(
            flops=0, bytes_accessed=2 * depth * half * 2, transcendentals=0
        ),
        name="load_weights",
    )(*requests, w_gate, w_up)


def block_kernel(
    half,
    chunk,
    near_ref,
    far_ref,
    gain_ref,
    first_ref,
    gate_hbm,
    up_hbm,
    down_hbm,
    keep_ref,
    send_ref,
    wide_ref,
    normed_ref,
    product_ref,
    hidden_ref,
    rest_ref,
    down_ref,
    both_sems,
    down_sems,
):
    tile = 256
    ahead = 3
    rows, lines, lanes = wide_ref.shape
    depth = lines * lanes
    loaded = first_ref.shape[0]
    own = pl.multiple_of(lax.axis_index("groups") * half, LANES)
    loads = []
    for step, at in enumerate(range(0, depth - loaded, chunk)):
        loads.append(
            [
                pltpu.make_async_copy(
                    weight.at[pl.ds(loaded + at, chunk), pl.ds(own, half)],
                    rest_ref.at[pl.ds(at, chunk), pl.ds(side * half, half)],
                    both_sems.at[step, side],
                )
                for side, weight in enumerate((gate_hbm, up_hbm))
            ]
        )
    pairs = len(loads)
    for step, at in enumerate(range(0, depth, chunk)):
        loads.append(
            [
                pltpu.make_async_copy(
                    down_hbm.at[pl.ds(own, half), pl.ds(at, chunk)],
                    down_ref.at[:, pl.ds(at, chunk)],
                    down_sems.at[step],
                )
            ]
        )

    def start(number):
        if number < len(loads):
            for copy in loads[number]:
                copy.start()

    def wait(number):
        for copy in loads[number]:
            copy.wait()

    for number in range(ahead):
        start(number)

    wide_ref[: rows // 2] = near_ref[...].astype(jnp.float32)
    wide_ref[rows // 2 :] = far_ref[...].astype(jnp.float32)
    squares = wide_ref[:, 0, :] * wide_ref[:, 0, :]
    for line in range(1, lines):
        value = wide_ref[:, line, :]
        squares = squares + value * value
    scale = lax.rsqrt(jnp.sum(squares, axis=-1, keepdims=True) * (1.0 / depth) + 1e-05)
    for line in range(lines):
        columns = pl.ds(line * lanes, lanes)
        normed_ref[:, columns] = (
            wide_ref[:, line, :] * scale * gain_ref[:, columns].astype(jnp.float32)
        ).astype(jnp.bfloat16)

    started = ahead
    for at in range(0, depth, chunk):
        if at >= loaded:
            wait((at - loaded) // chunk)
        for column in range(0, 2 * half, tile):
            columns = pl.ds(column, tile)
            weight = (
                first_ref[at : at + chunk, columns]
                if at < loaded
                else rest_ref[at - loaded : at - loaded + chunk, columns]
            )
            value = jnp.dot(
                normed_ref[:, at : at + chunk], weight, preferred_element_type=jnp.float32
            )
            if at == 0:
                product_ref[:, columns] = value
            else:
                product_ref[:, columns] += value
        start(started)
        started += 1
    gate_out = product_ref[:, :half]
    up_out = product_ref[:, half:]
    hidden_ref[...] = (gate_out / (1.0 + jnp.exp(-gate_out)) * up_out).astype(jnp.bfloat16)
    for step in range(depth // chunk):
        wait(pairs + step)
        for at in range(step * chunk, (step + 1) * chunk, tile):
            result = jnp.dot(
                hidden_ref[...], down_ref[:, pl.ds(at, tile)], preferred_element_type=jnp.float32
            )
            for line in range(tile // lanes):
                wide_ref[:, at // lanes + line, :] = result[:, line * lanes : (line + 1) * lanes]
        start(started)
        started += 1
        done = pl.ds(step * chunk // lanes, chunk // lanes)
        keep_ref[:, done, :] = wide_ref[: rows // 2, done, :]
        send_ref[:, done, :] = wide_ref[rows // 2 :, done, :].astype(jnp.bfloat16)


def block(near, far, gain, first, w_gate, w_up, w_down, half):
    rows, lines, lanes = near.shape
    depth = lines * lanes
    chunk = 1024
    rest = depth - first.shape[0]
    vmem = pl.BlockSpec(memory_space=pltpu.VMEM)
    hbm = pl.BlockSpec(memory_space=pltpu.HBM)
    return pl.pallas_call(
        functools.partial(block_kernel, half, chunk),
        out_shape=(
            jax.ShapeDtypeStruct(near.shape, jnp.float32),
            jax.ShapeDtypeStruct(near.shape, jnp.bfloat16),
        ),
        in_specs=[vmem] * 4 + [hbm] * 3,
        out_specs=(vmem, vmem),
        scratch_shapes=[
            pltpu.VMEM((2 * rows, lines, lanes), jnp.float32),
            pltpu.VMEM((2 * rows, depth), jnp.bfloat16),
            pltpu.VMEM((2 * rows, 2 * half), jnp.float32),
            pltpu.VMEM((2 * rows, half), jnp.bfloat16),
            pltpu.VMEM((rest, 2 * half), jnp.bfloat16),
            pltpu.VMEM((half, depth), jnp.bfloat16),
            pltpu.SemaphoreType.DMA((rest // chunk, 2)),
            pltpu.SemaphoreType.DMA((depth // chunk,)),
        ],
        compiler_params=pltpu.CompilerParams(
            vmem_limit_bytes=(rest * 2 + depth) * half * 2 + (6 << 20)
        ),
        cost_estimate=pl.CostEstimate(
            flops=12 * rows * depth * half,
            bytes_accessed=(rest * 2 + depth) * half * 2,
            transcendentals=0,
        ),
        name="block",
    )(near, far, gain, pltpu.with_memory_space_constraint(first, pltpu.VMEM), w_gate, w_up, w_down)


def deal(pieces, axes):
    return lax.all_to_all(pieces, axes, split_axis=0, concat_axis=0, tiled=True)


def other_core(value):
    return lax.ppermute(value, "core", [(0, 1), (1, 0)])


def shared(tokens, norm_gain, w_gate, w_up, w_down, lengths, hit_lengths, start_positions):
    depth = tokens.shape[1]
    lines = depth // LANES
    half = w_gate.shape[1] // lax.axis_size("groups")
    deep = lax.axis_size("z")
    square = lax.axis_size("groups") * lax.axis_size("x")
    w_gate, w_up, w_down = (
        pltpu.with_memory_space_constraint(weight, pltpu.HBM) for weight in (w_gate, w_up, w_down)
    )

    def place():
        return (lax.axis_index("z") * lax.axis_size("x") + lax.axis_index("x")) * lax.axis_size(
            "core"
        ) + lax.axis_index("core")

    first, keep = load_weights(
        (lengths, hit_lengths, start_positions), w_gate, w_up, half, depth // 2, place
    )
    column = deal(jnp.broadcast_to(tokens.reshape(1, lines, LANES), (deep, lines, LANES)), "z")
    plane = deal(jnp.broadcast_to(column, (square,) + column.shape), ("groups", "x"))
    near = plane.reshape(square * deep, lines, LANES)
    far = other_core(near)
    kept, sent = block(near, far, norm_gain.reshape(1, depth), first, w_gate, w_up, w_down, half)
    plane = (kept + other_core(sent).astype(jnp.float32)).astype(jnp.bfloat16)
    column = jnp.sum(
        deal(plane.reshape(square, deep, lines, LANES), ("groups", "x")).astype(jnp.float32), axis=0
    ).astype(jnp.bfloat16)
    totals = jnp.sum(deal(column, "z").astype(jnp.float32), axis=0)
    return jnp.where(keep[:1] > 0, totals, jnp.zeros_like(totals)).astype(jnp.bfloat16).reshape(1, depth)


def solution(mesh):
    groups, members = mesh.shape["groups"], mesh.shape["tensor"]

    def placed(axes, whole):
        return (
            P(whole, None),
            P(),
            P(None, axes),
            P(None, axes),
            P(axes, None),
            P("groups"),
            P("groups"),
            P("groups"),
        )

    def run(*arrays):
        units = arrays[2].shape[1] // members
        if (
            units % (LANES * groups) == 0
            and arrays[0].shape[0] == groups * members
            and groups == 2
            and members % 8 == 0
        ):
            body, axes, whole = shared, ("z", "x", "core"), ROW_LINES
            over = jax.sharding.Mesh(mesh.devices.reshape(groups, members // 4, 2, 2), ROW_LINES)
        else:
            body, axes, whole, over = local, "tensor", ("groups", "tensor"), mesh
        return jax.shard_map(
            body,
            mesh=over,
            in_specs=placed(axes, whole),
            out_specs=P(whole, None),
            check_vma=False,
        )(*arrays)

    return run
```

```python
import functools

import jax
import jax.numpy as jnp
from jax import lax
from jax.experimental import pallas as pl
from jax.experimental.pallas import tpu as pltpu
from jax.sharding import PartitionSpec as P

LANES = 128
ROW_LINES = ("groups", "z", "x", "core")


def normalize(tokens, norm_gain):
    values = tokens.astype(jnp.float32)
    mean_sq = jnp.mean(values * values, axis=-1, keepdims=True)
    return (values * lax.rsqrt(mean_sq + 1e-05) * norm_gain.astype(jnp.float32)).astype(
        jnp.bfloat16
    )


def live_rows(lengths, hit_lengths, start_positions, token_index):
    ends = jnp.cumsum(lengths)
    begins = ends - lengths
    member = (token_index[:, None] >= begins[None, :]) & (token_index[:, None] < ends[None, :])
    member_int = member.astype(jnp.int32)
    offsets = token_index - jnp.sum(member_int * begins[None, :], axis=1)
    position = jnp.sum(member_int * start_positions[None, :], axis=1) + offsets
    covered = jnp.sum(member_int * hit_lengths[None, :], axis=1)
    return position >= covered


def local(tokens, norm_gain, w_gate, w_up, w_down, lengths, hit_lengths, start_positions):
    row_count = tokens.shape[0]
    normed = normalize(tokens, norm_gain)
    piece_rows = lax.all_gather(normed, "tensor", axis=0, tiled=True)
    gate_out = jnp.dot(piece_rows, w_gate, preferred_element_type=jnp.float32)
    up_out = jnp.dot(piece_rows, w_up, preferred_element_type=jnp.float32)
    hidden = (jax.nn.silu(gate_out) * up_out).astype(jnp.bfloat16)
    partial_value = jnp.dot(hidden, w_down, preferred_element_type=jnp.float32)
    rounded = partial_value.astype(jnp.bfloat16)
    totals = jnp.sum(
        lax.all_to_all(rounded[None], "tensor", split_axis=1, concat_axis=0, tiled=True).astype(
            jnp.float32
        ),
        axis=0,
    )
    token_index = lax.axis_index("tensor") * row_count + jnp.arange(row_count, dtype=jnp.int32)
    live = live_rows(lengths, hit_lengths, start_positions, token_index)
    return jnp.where(live[:, None], totals, jnp.zeros_like(totals)).astype(jnp.bfloat16)


VMEM = pl.BlockSpec(memory_space=pltpu.VMEM)
HBM = pl.BlockSpec(memory_space=pltpu.HBM)
CHUNK = 1024


def live_flag(lengths, hit_lengths, start_positions, token):
    begin = 0
    live = False
    for request in range(lengths.shape[0]):
        end = begin + lengths[request]
        position = start_positions[request] + token - begin
        inside = (token >= begin) & (token < end)
        live = live | (inside & (position >= hit_lengths[request]))
        begin = end
    return live


def norm_kernel(tokens_hbm, gain_hbm, out_ref, tokens_ref, gain_ref, sems):
    copies = [
        pltpu.make_async_copy(tokens_hbm, tokens_ref, sems.at[0]),
        pltpu.make_async_copy(gain_hbm, gain_ref, sems.at[1]),
    ]
    for copy in copies:
        copy.start()
    for copy in copies:
        copy.wait()
    values = tokens_ref[...].astype(jnp.float32)
    mean_sq = jnp.mean(values * values, axis=-1, keepdims=True)
    scaled = values * lax.rsqrt(mean_sq + 1e-05)
    lines = out_ref.shape[1]
    rows = [scaled[:, line * LANES : (line + 1) * LANES] for line in range(lines)]
    stacked = jnp.concatenate(rows, axis=0)
    out_ref[0] = (stacked * gain_ref[...].astype(jnp.float32)).astype(jnp.bfloat16)


def norm(tokens, gain):
    lines = tokens.shape[1] // LANES
    gain = gain.reshape(lines, LANES)
    return pl.pallas_call(
        norm_kernel,
        out_shape=jax.ShapeDtypeStruct((1, lines, LANES), jnp.bfloat16),
        in_specs=[HBM, HBM],
        out_specs=VMEM,
        scratch_shapes=[
            pltpu.VMEM(tokens.shape, tokens.dtype),
            pltpu.VMEM(gain.shape, gain.dtype),
            pltpu.SemaphoreType.DMA((2,)),
        ],
        compiler_params=pltpu.CompilerParams(vmem_limit_bytes=1 << 20),
        name="norm",
    )(*(pltpu.with_memory_space_constraint(array, pltpu.HBM) for array in (tokens, gain)))


def stack_kernel(*refs):
    for at, piece in enumerate(refs[:-2]):
        refs[-1][at : at + 1] = piece[...]


def stack(pieces, mark):
    return pl.pallas_call(
        stack_kernel,
        out_shape=jax.ShapeDtypeStruct((len(pieces),) + pieces[0].shape[1:], pieces[0].dtype),
        in_specs=[VMEM] * len(pieces) + [pl.BlockSpec(memory_space=pl.ANY)],
        out_specs=VMEM,
        compiler_params=pltpu.CompilerParams(vmem_limit_bytes=1 << 20),
        name="stack",
    )(*pieces, mark)


def load_kernel(half, row, gate_hbm, up_hbm, both_vmem, mark_vmem, sems):
    own = pl.multiple_of(lax.axis_index("groups") * half, LANES)
    copies = [
        pltpu.make_async_copy(
            weight.at[pl.ds(row, both_vmem.shape[0]), pl.ds(own, half)],
            both_vmem.at[:, pl.ds(at * half, half)],
            sems.at[at],
        )
        for at, weight in enumerate((gate_hbm, up_hbm))
    ]
    for copy in copies:
        copy.start()
    mark_vmem[...] = jnp.ones(mark_vmem.shape, mark_vmem.dtype)
    for copy in copies:
        copy.wait()


def load_live_kernel(
    half,
    row,
    place,
    lengths,
    hit_lengths,
    start_positions,
    gate_hbm,
    up_hbm,
    both_vmem,
    mark_vmem,
    lengths_smem,
    hit_smem,
    start_smem,
    sems,
):
    own = pl.multiple_of(lax.axis_index("groups") * half, LANES)
    small = [
        pltpu.make_async_copy(source, target, sems.at[2 + at])
        for at, (source, target) in enumerate(
            ((lengths, lengths_smem), (hit_lengths, hit_smem), (start_positions, start_smem))
        )
    ]
    copies = [
        pltpu.make_async_copy(
            weight.at[pl.ds(row, both_vmem.shape[0]), pl.ds(own, half)],
            both_vmem.at[:, pl.ds(at * half, half)],
            sems.at[at],
        )
        for at, weight in enumerate((gate_hbm, up_hbm))
    ]
    for copy in small + copies:
        copy.start()
    for copy in small:
        copy.wait()
    live = live_flag(lengths_smem, hit_smem, start_smem, place())
    mark_vmem[...] = jnp.full(mark_vmem.shape, live.astype(jnp.float32), jnp.float32)
    for copy in copies:
        copy.wait()


def load_weights(w_gate, w_up, half, row, count, requests=(), place=None):
    if requests:
        body = functools.partial(load_live_kernel, half, row, place)
        small = [pltpu.SMEM(array.shape, array.dtype) for array in requests]
    else:
        body, small = functools.partial(load_kernel, half, row), []
    return pl.pallas_call(
        body,
        out_shape=(
            pltpu.VMEM((count, 2 * half), w_gate.dtype),
            jax.ShapeDtypeStruct((8, LANES), jnp.float32),
        ),
        in_specs=[HBM] * (2 + len(requests)),
        out_specs=(VMEM, VMEM),
        scratch_shapes=small + [pltpu.SemaphoreType.DMA((5,))],
        compiler_params=pltpu.CompilerParams(vmem_limit_bytes=1 << 20),
        cost_estimate=pl.CostEstimate(
            flops=0, bytes_accessed=2 * count * half * 2, transcendentals=0
        ),
        name="load_weights",
    )(*requests, w_gate, w_up)


def pack_kernel(*refs):
    pieces, out_ref, wide_ref = refs[:-3], refs[-2], refs[-1]
    at = 0
    for piece in pieces:
        wide_ref[at : at + piece.shape[0]] = piece[...].astype(jnp.float32)
        at += piece.shape[0]
    for line in range(wide_ref.shape[1]):
        out_ref[:, line * LANES : (line + 1) * LANES] = wide_ref[:, line, :].astype(jnp.bfloat16)


def pack(pieces, mark):
    rows = sum(piece.shape[0] for piece in pieces)
    lines = pieces[0].shape[1]
    return pl.pallas_call(
        pack_kernel,
        out_shape=jax.ShapeDtypeStruct((rows, lines * LANES), jnp.bfloat16),
        in_specs=[VMEM] * len(pieces) + [pl.BlockSpec(memory_space=pl.ANY)],
        out_specs=VMEM,
        scratch_shapes=[pltpu.VMEM((rows, lines, LANES), jnp.float32)],
        compiler_params=pltpu.CompilerParams(vmem_limit_bytes=4 << 20),
        name="pack",
    )(*pieces, mark)


def block_kernel(
    half,
    chunk,
    near_ref,
    far_ref,
    first_refs,
    gate_hbm,
    up_hbm,
    down_hbm,
    keep_ref,
    send_ref,
    wide_ref,
    rows_ref,
    product_ref,
    hidden_ref,
    rest_ref,
    down_ref,
    both_sems,
    down_sems,
):
    tile = 256
    ahead = 3
    rows, lines, lanes = wide_ref.shape
    depth = lines * lanes
    held = [(ref, at) for ref in first_refs for at in range(0, ref.shape[0], chunk)]
    loaded = len(held) * chunk
    own = pl.multiple_of(lax.axis_index("groups") * half, LANES)
    loads = []
    for step, at in enumerate(range(0, depth - loaded, chunk)):
        loads.append(
            [
                pltpu.make_async_copy(
                    weight.at[pl.ds(loaded + at, chunk), pl.ds(own, half)],
                    rest_ref.at[pl.ds(at, chunk), pl.ds(side * half, half)],
                    both_sems.at[step, side],
                )
                for side, weight in enumerate((gate_hbm, up_hbm))
            ]
        )
    pairs = len(loads)
    for step, at in enumerate(range(0, depth, chunk)):
        loads.append(
            [
                pltpu.make_async_copy(
                    down_hbm.at[pl.ds(own, half), pl.ds(at, chunk)],
                    down_ref.at[:, pl.ds(at, chunk)],
                    down_sems.at[step],
                )
            ]
        )

    def start(number):
        if number < len(loads):
            for copy in loads[number]:
                copy.start()

    def wait(number):
        for copy in loads[number]:
            copy.wait()

    for number in range(ahead):
        start(number)

    rows_ref[: rows // 2] = near_ref[...]
    rows_ref[rows // 2 :] = far_ref[...]
    started = ahead
    for at in range(0, depth, chunk):
        if at >= loaded:
            wait((at - loaded) // chunk)
        for column in range(0, 2 * half, tile):
            columns = pl.ds(column, tile)
            ref, row = held[at // chunk] if at < loaded else (rest_ref, at - loaded)
            value = jnp.dot(
                rows_ref[:, at : at + chunk],
                ref[row : row + chunk, columns],
                preferred_element_type=jnp.float32,
            )
            if at == 0:
                product_ref[:, columns] = value
            else:
                product_ref[:, columns] += value
        start(started)
        started += 1
    gate_out = product_ref[:, :half]
    up_out = product_ref[:, half:]
    hidden_ref[...] = (gate_out / (1.0 + jnp.exp(-gate_out)) * up_out).astype(jnp.bfloat16)
    for step in range(depth // chunk):
        wait(pairs + step)
        for at in range(step * chunk, (step + 1) * chunk, tile):
            result = jnp.dot(
                hidden_ref[...], down_ref[:, pl.ds(at, tile)], preferred_element_type=jnp.float32
            )
            for line in range(tile // lanes):
                wide_ref[:, at // lanes + line, :] = result[:, line * lanes : (line + 1) * lanes]
        start(started)
        started += 1
        done = pl.ds(step * chunk // lanes, chunk // lanes)
        keep_ref[:, done, :] = wide_ref[: rows // 2, done, :]
        send_ref[:, done, :] = wide_ref[rows // 2 :, done, :].astype(jnp.bfloat16)


def block(near, far, firsts, w_gate, w_up, w_down, half):
    rows, depth = near.shape
    lines = depth // LANES
    rest = depth - sum(first.shape[0] for first in firsts)

    def body(near_ref, far_ref, *refs):
        count = len(firsts)
        block_kernel(half, CHUNK, near_ref, far_ref, refs[:count], *refs[count:])

    return pl.pallas_call(
        body,
        out_shape=(
            jax.ShapeDtypeStruct((rows, lines, LANES), jnp.float32),
            jax.ShapeDtypeStruct((rows, lines, LANES), jnp.bfloat16),
        ),
        in_specs=[VMEM] * (2 + len(firsts)) + [HBM] * 3,
        out_specs=(VMEM, VMEM),
        scratch_shapes=[
            pltpu.VMEM((2 * rows, lines, LANES), jnp.float32),
            pltpu.VMEM((2 * rows, depth), jnp.bfloat16),
            pltpu.VMEM((2 * rows, 2 * half), jnp.float32),
            pltpu.VMEM((2 * rows, half), jnp.bfloat16),
            pltpu.VMEM((rest, 2 * half), jnp.bfloat16),
            pltpu.VMEM((half, depth), jnp.bfloat16),
            pltpu.SemaphoreType.DMA((rest // CHUNK, 2)),
            pltpu.SemaphoreType.DMA((depth // CHUNK,)),
        ],
        compiler_params=pltpu.CompilerParams(
            vmem_limit_bytes=(rest * 2 + depth) * half * 2 + (6 << 20)
        ),
        cost_estimate=pl.CostEstimate(
            flops=12 * rows * depth * half,
            bytes_accessed=(rest * 2 + depth) * half * 2,
            transcendentals=0,
        ),
        name="block",
    )(
        near,
        far,
        *(pltpu.with_memory_space_constraint(first, pltpu.VMEM) for first in firsts),
        w_gate,
        w_up,
        w_down,
    )


def finish_kernel(*refs):
    pieces, live_ref, out_ref = refs[:-2], refs[-2], refs[-1]
    totals = pieces[0][...].astype(jnp.float32)
    for piece in pieces[1:]:
        totals = totals + piece[...].astype(jnp.float32)
    totals = jnp.where(live_ref[:1] > 0, totals[0], jnp.zeros_like(totals[0]))
    for line in range(totals.shape[0]):
        out_ref[:, line * LANES : (line + 1) * LANES] = totals[line : line + 1].astype(jnp.bfloat16)


def finish(pieces, live):
    lines = pieces[0].shape[1]
    return pl.pallas_call(
        finish_kernel,
        out_shape=jax.ShapeDtypeStruct((1, lines * LANES), jnp.bfloat16),
        in_specs=[VMEM] * (len(pieces) + 1),
        out_specs=VMEM,
        compiler_params=pltpu.CompilerParams(vmem_limit_bytes=1 << 20),
        name="finish",
    )(*pieces, live)


def swap(value, axes, offset):
    places = range(lax.axis_size(axes))
    return lax.ppermute(value, axes, [(place, place ^ offset) for place in places])


def shared(tokens, norm_gain, w_gate, w_up, w_down, lengths, hit_lengths, start_positions):
    square = ("groups", "x")
    half = w_gate.shape[1] // lax.axis_size("groups")
    w_gate, w_up, w_down = (
        pltpu.with_memory_space_constraint(array, pltpu.HBM) for array in (w_gate, w_up, w_down)
    )
    requests = tuple(
        pltpu.with_memory_space_constraint(array, pltpu.HBM)
        for array in (lengths, hit_lengths, start_positions)
    )

    def place():
        return (lax.axis_index("z") * lax.axis_size("x") + lax.axis_index("x")) * lax.axis_size(
            "core"
        ) + lax.axis_index("core")

    own = norm(tokens, norm_gain)
    column = [own] + [swap(own, "z", at) for at in range(1, lax.axis_size("z"))]
    first, mark = load_weights(w_gate, w_up, half, 0, CHUNK)
    column = stack(column, mark)
    plane = [column] + [swap(column, square, at) for at in range(1, lax.axis_size(square))]
    second, live = load_weights(w_gate, w_up, half, CHUNK, 2 * CHUNK, requests, place)
    near = pack(plane, live)
    far = swap(near, "core", 1)
    third, mark = load_weights(w_gate, w_up, half, 3 * CHUNK, CHUNK)
    kept, sent = block(near, far, (first, second, third), w_gate, w_up, w_down, half)
    plane = (kept + swap(sent, "core", 1).astype(jnp.float32)).astype(jnp.bfloat16)
    pieces = jnp.split(plane, lax.axis_size(square), axis=0)
    column = pieces[0].astype(jnp.float32)
    for at, piece in enumerate(pieces[1:]):
        column = column + swap(piece, square, at + 1).astype(jnp.float32)
    column = column.astype(jnp.bfloat16)
    pieces = jnp.split(column, lax.axis_size("z"), axis=0)
    return finish(
        pieces[:1] + [swap(piece, "z", at + 1) for at, piece in enumerate(pieces[1:])], live
    )


def solution(mesh):
    groups, members = mesh.shape["groups"], mesh.shape["tensor"]

    def placed(axes, whole):
        return (
            P(whole, None),
            P(),
            P(None, axes),
            P(None, axes),
            P(axes, None),
            P("groups"),
            P("groups"),
            P("groups"),
        )

    def run(*arrays):
        units = arrays[2].shape[1] // members
        if (
            units % (LANES * groups) == 0
            and arrays[0].shape[0] == groups * members
            and groups == 2
            and members >= 8
            and members & (members - 1) == 0
        ):
            body, axes, whole = shared, ("z", "x", "core"), ROW_LINES
            over = jax.sharding.Mesh(mesh.devices.reshape(groups, members // 4, 2, 2), ROW_LINES)
        else:
            body, axes, whole, over = local, "tensor", ("groups", "tensor"), mesh
        return jax.shard_map(
            body,
            mesh=over,
            in_specs=placed(axes, whole),
            out_specs=P(whole, None),
            check_vma=False,
        )(*arrays)

    return run
```

```python
import functools

import jax
import jax.numpy as jnp
from jax import lax
from jax.experimental import pallas as pl
from jax.experimental.pallas import tpu as pltpu
from jax.sharding import PartitionSpec as P

LANES = 128
ROW_LINES = ("groups", "z", "x", "core")


def normalize(tokens, norm_gain):
    values = tokens.astype(jnp.float32)
    mean_sq = jnp.mean(values * values, axis=-1, keepdims=True)
    return (values * lax.rsqrt(mean_sq + 1e-05) * norm_gain.astype(jnp.float32)).astype(
        jnp.bfloat16
    )


def live_rows(lengths, hit_lengths, start_positions, token_index):
    ends = jnp.cumsum(lengths)
    begins = ends - lengths
    member = (token_index[:, None] >= begins[None, :]) & (token_index[:, None] < ends[None, :])
    member_int = member.astype(jnp.int32)
    offsets = token_index - jnp.sum(member_int * begins[None, :], axis=1)
    position = jnp.sum(member_int * start_positions[None, :], axis=1) + offsets
    covered = jnp.sum(member_int * hit_lengths[None, :], axis=1)
    return position >= covered


def local(tokens, norm_gain, w_gate, w_up, w_down, lengths, hit_lengths, start_positions):
    row_count = tokens.shape[0]
    normed = normalize(tokens, norm_gain)
    piece_rows = lax.all_gather(normed, "tensor", axis=0, tiled=True)
    gate_out = jnp.dot(piece_rows, w_gate, preferred_element_type=jnp.float32)
    up_out = jnp.dot(piece_rows, w_up, preferred_element_type=jnp.float32)
    hidden = (jax.nn.silu(gate_out) * up_out).astype(jnp.bfloat16)
    partial_value = jnp.dot(hidden, w_down, preferred_element_type=jnp.float32)
    rounded = partial_value.astype(jnp.bfloat16)
    totals = jnp.sum(
        lax.all_to_all(rounded[None], "tensor", split_axis=1, concat_axis=0, tiled=True).astype(
            jnp.float32
        ),
        axis=0,
    )
    token_index = lax.axis_index("tensor") * row_count + jnp.arange(row_count, dtype=jnp.int32)
    live = live_rows(lengths, hit_lengths, start_positions, token_index)
    return jnp.where(live[:, None], totals, jnp.zeros_like(totals)).astype(jnp.bfloat16)


VMEM = pl.BlockSpec(memory_space=pltpu.VMEM)
HBM = pl.BlockSpec(memory_space=pltpu.HBM)
CHUNK = 1024


def live_flag(lengths, hit_lengths, start_positions, token):
    begin = 0
    live = False
    for request in range(lengths.shape[0]):
        end = begin + lengths[request]
        position = start_positions[request] + token - begin
        inside = (token >= begin) & (token < end)
        live = live | (inside & (position >= hit_lengths[request]))
        begin = end
    return live


def norm_kernel(tokens_hbm, gain_hbm, out_ref, tokens_ref, gain_ref, sems):
    copies = [
        pltpu.make_async_copy(tokens_hbm, tokens_ref, sems.at[0]),
        pltpu.make_async_copy(gain_hbm, gain_ref, sems.at[1]),
    ]
    for copy in copies:
        copy.start()
    for copy in copies:
        copy.wait()
    values = tokens_ref[...].astype(jnp.float32)
    mean_sq = jnp.mean(values * values, axis=-1, keepdims=True)
    scaled = values * lax.rsqrt(mean_sq + 1e-05)
    lines = out_ref.shape[1]
    rows = [scaled[:, line * LANES : (line + 1) * LANES] for line in range(lines)]
    stacked = jnp.concatenate(rows, axis=0)
    out_ref[0] = (stacked * gain_ref[...].astype(jnp.float32)).astype(jnp.bfloat16)


def norm(tokens, gain):
    lines = tokens.shape[1] // LANES
    gain = gain.reshape(lines, LANES)
    return pl.pallas_call(
        norm_kernel,
        out_shape=jax.ShapeDtypeStruct((1, lines, LANES), jnp.bfloat16),
        in_specs=[HBM, HBM],
        out_specs=VMEM,
        scratch_shapes=[
            pltpu.VMEM(tokens.shape, tokens.dtype),
            pltpu.VMEM(gain.shape, gain.dtype),
            pltpu.SemaphoreType.DMA((2,)),
        ],
        compiler_params=pltpu.CompilerParams(vmem_limit_bytes=1 << 20),
        name="norm",
    )(*(pltpu.with_memory_space_constraint(array, pltpu.HBM) for array in (tokens, gain)))


def stack_kernel(*refs):
    for at, piece in enumerate(refs[:-2]):
        refs[-1][at : at + 1] = piece[...]


def stack(pieces, mark):
    return pl.pallas_call(
        stack_kernel,
        out_shape=jax.ShapeDtypeStruct((len(pieces),) + pieces[0].shape[1:], pieces[0].dtype),
        in_specs=[VMEM] * len(pieces) + [pl.BlockSpec(memory_space=pl.ANY)],
        out_specs=VMEM,
        compiler_params=pltpu.CompilerParams(vmem_limit_bytes=1 << 20),
        name="stack",
    )(*pieces, mark)


def load_kernel(half, row, gate_hbm, up_hbm, both_vmem, mark_vmem, sems):
    own = pl.multiple_of(lax.axis_index("groups") * half, LANES)
    copies = [
        pltpu.make_async_copy(
            weight.at[pl.ds(row, both_vmem.shape[0]), pl.ds(own, half)],
            both_vmem.at[:, pl.ds(at * half, half)],
            sems.at[at],
        )
        for at, weight in enumerate((gate_hbm, up_hbm))
    ]
    for copy in copies:
        copy.start()
    mark_vmem[...] = jnp.ones(mark_vmem.shape, mark_vmem.dtype)
    for copy in copies:
        copy.wait()


def load_live_kernel(
    half,
    row,
    place,
    lengths,
    hit_lengths,
    start_positions,
    gate_hbm,
    up_hbm,
    both_vmem,
    mark_vmem,
    lengths_smem,
    hit_smem,
    start_smem,
    sems,
):
    own = pl.multiple_of(lax.axis_index("groups") * half, LANES)
    small = [
        pltpu.make_async_copy(source, target, sems.at[2 + at])
        for at, (source, target) in enumerate(
            ((lengths, lengths_smem), (hit_lengths, hit_smem), (start_positions, start_smem))
        )
    ]
    copies = [
        pltpu.make_async_copy(
            weight.at[pl.ds(row, both_vmem.shape[0]), pl.ds(own, half)],
            both_vmem.at[:, pl.ds(at * half, half)],
            sems.at[at],
        )
        for at, weight in enumerate((gate_hbm, up_hbm))
    ]
    for copy in small + copies:
        copy.start()
    for copy in small:
        copy.wait()
    live = live_flag(lengths_smem, hit_smem, start_smem, place())
    mark_vmem[...] = jnp.full(mark_vmem.shape, live.astype(jnp.float32), jnp.float32)
    for copy in copies:
        copy.wait()


def load_weights(w_gate, w_up, half, row, count, requests=(), place=None):
    if requests:
        body = functools.partial(load_live_kernel, half, row, place)
        small = [pltpu.SMEM(array.shape, array.dtype) for array in requests]
    else:
        body, small = functools.partial(load_kernel, half, row), []
    return pl.pallas_call(
        body,
        out_shape=(
            pltpu.VMEM((count, 2 * half), w_gate.dtype),
            jax.ShapeDtypeStruct((8, LANES), jnp.float32),
        ),
        in_specs=[HBM] * (2 + len(requests)),
        out_specs=(VMEM, VMEM),
        scratch_shapes=small + [pltpu.SemaphoreType.DMA((5,))],
        compiler_params=pltpu.CompilerParams(vmem_limit_bytes=1 << 20),
        cost_estimate=pl.CostEstimate(
            flops=0, bytes_accessed=2 * count * half * 2, transcendentals=0
        ),
        name="load_weights",
    )(*requests, w_gate, w_up)


def pack_kernel(*refs):
    pieces, out_ref, wide_ref = refs[:-3], refs[-2], refs[-1]
    rows = out_ref.shape[0]
    lines = out_ref.shape[1] // LANES
    stride = wide_ref.shape[0] // rows
    row = 0
    for piece in pieces:
        for at in range(piece.shape[0]):
            wide_ref[row * stride : row * stride + lines] = piece[at].astype(jnp.float32)
            row += 1
    for line in range(lines):
        out_ref[:, line * LANES : (line + 1) * LANES] = wide_ref[
            pl.ds(line, rows, stride=stride), :
        ].astype(jnp.bfloat16)


def pack(pieces, mark):
    rows = sum(piece.shape[0] for piece in pieces)
    lines = pieces[0].shape[1]
    return pl.pallas_call(
        pack_kernel,
        out_shape=jax.ShapeDtypeStruct((rows, lines * LANES), jnp.bfloat16),
        in_specs=[VMEM] * len(pieces) + [pl.BlockSpec(memory_space=pl.ANY)],
        out_specs=VMEM,
        scratch_shapes=[pltpu.VMEM((rows * (lines + 1), LANES), jnp.float32)],
        compiler_params=pltpu.CompilerParams(vmem_limit_bytes=4 << 20),
        name="pack",
    )(*pieces, mark)


def block_kernel(
    half,
    chunk,
    near_ref,
    far_ref,
    first_refs,
    gate_hbm,
    up_hbm,
    down_hbm,
    keep_ref,
    send_ref,
    wide_ref,
    rows_ref,
    product_ref,
    hidden_ref,
    rest_ref,
    down_ref,
    both_sems,
    down_sems,
):
    tile = 256
    rows, depth = rows_ref.shape
    lanes = LANES
    lines = depth // lanes
    stride = wide_ref.shape[0] // rows
    held = [(ref, at) for ref in first_refs for at in range(0, ref.shape[0], chunk)]
    loaded = len(held) * chunk
    own = pl.multiple_of(lax.axis_index("groups") * half, LANES)
    loads = []
    for step, at in enumerate(range(0, depth - loaded, chunk)):
        loads.append(
            [
                pltpu.make_async_copy(
                    weight.at[pl.ds(loaded + at, chunk), pl.ds(own, half)],
                    rest_ref.at[pl.ds(at, chunk), pl.ds(side * half, half)],
                    both_sems.at[step, side],
                )
                for side, weight in enumerate((gate_hbm, up_hbm))
            ]
        )
    pairs = len(loads)
    for step, at in enumerate(range(0, depth, chunk)):
        loads.append(
            [
                pltpu.make_async_copy(
                    down_hbm.at[pl.ds(own, half), pl.ds(at, chunk)],
                    down_ref.at[:, pl.ds(at, chunk)],
                    down_sems.at[step],
                )
            ]
        )

    steps = depth // chunk
    early = min(3, pairs)
    due = [[] for _ in range(2 * steps)]
    for number in range(early, pairs):
        due[number - early].append(number)
    for number in range(pairs, len(loads)):
        due[pairs - 1 + (number - pairs) // 2].append(number)

    def start(numbers):
        for number in numbers:
            for copy in loads[number]:
                copy.start()

    def wait(number):
        for copy in loads[number]:
            copy.wait()

    start(range(early))
    rows_ref[: rows // 2] = near_ref[...]
    rows_ref[rows // 2 :] = far_ref[...]
    for at in range(0, depth, chunk):
        if at >= loaded:
            wait((at - loaded) // chunk)
        for column in range(0, 2 * half, tile):
            columns = pl.ds(column, tile)
            ref, row = held[at // chunk] if at < loaded else (rest_ref, at - loaded)
            value = jnp.dot(
                rows_ref[:, at : at + chunk],
                ref[row : row + chunk, columns],
                preferred_element_type=jnp.float32,
            )
            if at == 0:
                product_ref[:, columns] = value
            else:
                product_ref[:, columns] += value
        start(due[at // chunk])
    gate_out = product_ref[:, :half]
    up_out = product_ref[:, half:]
    hidden_ref[...] = (gate_out / (1.0 + jnp.exp(-gate_out)) * up_out).astype(jnp.bfloat16)
    for step in range(steps):
        wait(pairs + step)
        for at in range(step * chunk, (step + 1) * chunk, tile):
            result = jnp.dot(
                hidden_ref[...], down_ref[:, pl.ds(at, tile)], preferred_element_type=jnp.float32
            )
            for line in range(tile // lanes):
                wide_ref[pl.ds(at // lanes + line, rows, stride=stride), :] = result[
                    :, line * lanes : (line + 1) * lanes
                ]
        start(due[steps + step])
        done = step * chunk // lanes
        count = chunk // lanes
        for row in range(rows):
            ready = wide_ref[row * stride + done : row * stride + done + count]
            if row < rows // 2:
                keep_ref[row, done : done + count] = ready
            else:
                send_ref[row - rows // 2, done : done + count] = ready.astype(jnp.bfloat16)


def block(near, far, firsts, w_gate, w_up, w_down, half):
    rows, depth = near.shape
    lines = depth // LANES
    rest = depth - sum(first.shape[0] for first in firsts)

    def body(near_ref, far_ref, *refs):
        count = len(firsts)
        block_kernel(half, CHUNK, near_ref, far_ref, refs[:count], *refs[count:])

    return pl.pallas_call(
        body,
        out_shape=(
            jax.ShapeDtypeStruct((rows, lines, LANES), jnp.float32),
            jax.ShapeDtypeStruct((rows, lines, LANES), jnp.bfloat16),
        ),
        in_specs=[VMEM] * (2 + len(firsts)) + [HBM] * 3,
        out_specs=(VMEM, VMEM),
        scratch_shapes=[
            pltpu.VMEM((2 * rows * (lines + 1), LANES), jnp.float32),
            pltpu.VMEM((2 * rows, depth), jnp.bfloat16),
            pltpu.VMEM((2 * rows, 2 * half), jnp.float32),
            pltpu.VMEM((2 * rows, half), jnp.bfloat16),
            pltpu.VMEM((rest, 2 * half), jnp.bfloat16),
            pltpu.VMEM((half, depth), jnp.bfloat16),
            pltpu.SemaphoreType.DMA((rest // CHUNK, 2)),
            pltpu.SemaphoreType.DMA((depth // CHUNK,)),
        ],
        compiler_params=pltpu.CompilerParams(
            vmem_limit_bytes=(rest * 2 + depth) * half * 2 + (6 << 20)
        ),
        cost_estimate=pl.CostEstimate(
            flops=12 * rows * depth * half,
            bytes_accessed=(rest * 2 + depth) * half * 2,
            transcendentals=0,
        ),
        name="block",
    )(
        near,
        far,
        *(pltpu.with_memory_space_constraint(first, pltpu.VMEM) for first in firsts),
        w_gate,
        w_up,
        w_down,
    )


def finish_kernel(*refs):
    pieces, live_ref, out_ref = refs[:-2], refs[-2], refs[-1]
    totals = pieces[0][...].astype(jnp.float32)
    for piece in pieces[1:]:
        totals = totals + piece[...].astype(jnp.float32)
    totals = jnp.where(live_ref[:1] > 0, totals[0], jnp.zeros_like(totals[0]))
    for line in range(totals.shape[0]):
        out_ref[:, line * LANES : (line + 1) * LANES] = totals[line : line + 1].astype(jnp.bfloat16)


def finish(pieces, live):
    lines = pieces[0].shape[1]
    return pl.pallas_call(
        finish_kernel,
        out_shape=jax.ShapeDtypeStruct((1, lines * LANES), jnp.bfloat16),
        in_specs=[VMEM] * (len(pieces) + 1),
        out_specs=VMEM,
        compiler_params=pltpu.CompilerParams(vmem_limit_bytes=1 << 20),
        name="finish",
    )(*pieces, live)


def swap(value, axes, offset):
    places = range(lax.axis_size(axes))
    return lax.ppermute(value, axes, [(place, place ^ offset) for place in places])


def halving(count):
    order = [0]
    bit = count // 2
    while bit:
        order = order + [at + bit for at in order]
        bit //= 2
    return order


def shared(tokens, norm_gain, w_gate, w_up, w_down, lengths, hit_lengths, start_positions):
    square = ("groups", "x")
    half = w_gate.shape[1] // lax.axis_size("groups")
    w_gate, w_up, w_down = (
        pltpu.with_memory_space_constraint(array, pltpu.HBM) for array in (w_gate, w_up, w_down)
    )
    requests = tuple(
        pltpu.with_memory_space_constraint(array, pltpu.HBM)
        for array in (lengths, hit_lengths, start_positions)
    )

    def place():
        return (lax.axis_index("z") * lax.axis_size("x") + lax.axis_index("x")) * lax.axis_size(
            "core"
        ) + lax.axis_index("core")

    deep = lax.axis_size("z")
    far_first = [3, 1, 2]
    rest = [0] + far_first
    own = norm(tokens, norm_gain)
    column = [own] + [swap(own, "z", at) for at in halving(deep)[1:]]
    first, mark = load_weights(w_gate, w_up, half, 0, 2 * CHUNK)
    column = stack(column, mark)
    plane = [column] + [swap(column, square, at) for at in far_first]
    second, live = load_weights(w_gate, w_up, half, 2 * CHUNK, 2 * CHUNK, requests, place)
    near = pack(plane, live)
    far = swap(near, "core", 1)
    kept, sent = block(near, far, (first, second), w_gate, w_up, w_down, half)
    plane = (kept + swap(sent, "core", 1).astype(jnp.float32)).astype(jnp.bfloat16)
    pieces = jnp.split(plane, len(rest), axis=0)
    arrived = [swap(piece, square, at) for at, piece in zip(far_first, pieces[1:])]
    column = pieces[0].astype(jnp.float32)
    for piece in arrived:
        column = column + piece.astype(jnp.float32)
    column = column.astype(jnp.bfloat16)
    distance = 1
    while distance < deep // 2:
        kept, sent = jnp.split(column, 2, axis=0)
        column = (kept.astype(jnp.float32) + swap(sent, "z", distance).astype(jnp.float32)).astype(
            jnp.bfloat16
        )
        distance *= 2
    kept, sent = jnp.split(column, 2, axis=0)
    return finish([kept, swap(sent, "z", distance)], live)


def solution(mesh):
    groups, members = mesh.shape["groups"], mesh.shape["tensor"]

    def placed(axes, whole):
        return (
            P(whole, None),
            P(),
            P(None, axes),
            P(None, axes),
            P(axes, None),
            P("groups"),
            P("groups"),
            P("groups"),
        )

    def run(*arrays):
        units = arrays[2].shape[1] // members
        if (
            units % (LANES * groups) == 0
            and arrays[0].shape[0] == groups * members
            and groups == 2
            and members >= 8
            and members & (members - 1) == 0
        ):
            body, axes, whole = shared, ("z", "x", "core"), ROW_LINES
            over = jax.sharding.Mesh(mesh.devices.reshape(groups, members // 4, 2, 2), ROW_LINES)
        else:
            body, axes, whole, over = local, "tensor", ("groups", "tensor"), mesh
        return jax.shard_map(
            body,
            mesh=over,
            in_specs=placed(axes, whole),
            out_specs=P(whole, None),
            check_vma=False,
        )(*arrays)

    return run
```

```python
import functools

import jax
import jax.numpy as jnp
from jax import lax
from jax.experimental import pallas as pl
from jax.experimental.pallas import tpu as pltpu
from jax.sharding import PartitionSpec as P

LANES = 128
ROW_LINES = ("groups", "z", "x", "core")


def normalize(tokens, norm_gain):
    values = tokens.astype(jnp.float32)
    mean_sq = jnp.mean(values * values, axis=-1, keepdims=True)
    return (values * lax.rsqrt(mean_sq + 1e-05) * norm_gain.astype(jnp.float32)).astype(
        jnp.bfloat16
    )


def live_rows(lengths, hit_lengths, start_positions, token_index):
    ends = jnp.cumsum(lengths)
    begins = ends - lengths
    member = (token_index[:, None] >= begins[None, :]) & (token_index[:, None] < ends[None, :])
    member_int = member.astype(jnp.int32)
    offsets = token_index - jnp.sum(member_int * begins[None, :], axis=1)
    position = jnp.sum(member_int * start_positions[None, :], axis=1) + offsets
    covered = jnp.sum(member_int * hit_lengths[None, :], axis=1)
    return position >= covered


def local(tokens, norm_gain, w_gate, w_up, w_down, lengths, hit_lengths, start_positions):
    row_count = tokens.shape[0]
    normed = normalize(tokens, norm_gain)
    piece_rows = lax.all_gather(normed, "tensor", axis=0, tiled=True)
    gate_out = jnp.dot(piece_rows, w_gate, preferred_element_type=jnp.float32)
    up_out = jnp.dot(piece_rows, w_up, preferred_element_type=jnp.float32)
    hidden = (jax.nn.silu(gate_out) * up_out).astype(jnp.bfloat16)
    partial_value = jnp.dot(hidden, w_down, preferred_element_type=jnp.float32)
    rounded = partial_value.astype(jnp.bfloat16)
    totals = jnp.sum(
        lax.all_to_all(rounded[None], "tensor", split_axis=1, concat_axis=0, tiled=True).astype(
            jnp.float32
        ),
        axis=0,
    )
    token_index = lax.axis_index("tensor") * row_count + jnp.arange(row_count, dtype=jnp.int32)
    live = live_rows(lengths, hit_lengths, start_positions, token_index)
    return jnp.where(live[:, None], totals, jnp.zeros_like(totals)).astype(jnp.bfloat16)


VMEM = pl.BlockSpec(memory_space=pltpu.VMEM)
HBM = pl.BlockSpec(memory_space=pltpu.HBM)
CHUNK = 1024


def live_flag(lengths, hit_lengths, start_positions, token):
    begin = 0
    live = False
    for request in range(lengths.shape[0]):
        end = begin + lengths[request]
        position = start_positions[request] + token - begin
        inside = (token >= begin) & (token < end)
        live = live | (inside & (position >= hit_lengths[request]))
        begin = end
    return live


def stack_kernel(*refs):
    pieces, out_ref, wide_ref = refs[:-3], refs[-2], refs[-1]
    lines = out_ref.shape[1]
    for at, piece in enumerate(pieces):
        values = piece[...].astype(jnp.float32)
        for line in range(lines):
            wide_ref[at, line : line + 1] = values[:, line * LANES : (line + 1) * LANES]
    out_ref[...] = wide_ref[...].astype(out_ref.dtype)


def stack(pieces, gain):
    shape = (len(pieces), pieces[0].shape[1] // LANES, LANES)
    return pl.pallas_call(
        stack_kernel,
        out_shape=jax.ShapeDtypeStruct(shape, pieces[0].dtype),
        in_specs=[VMEM] * len(pieces) + [pl.BlockSpec(memory_space=pl.ANY)],
        out_specs=VMEM,
        scratch_shapes=[pltpu.VMEM(shape, jnp.float32)],
        compiler_params=pltpu.CompilerParams(vmem_limit_bytes=2 << 20),
        name="stack",
    )(*pieces, gain)


def load_gain_kernel(half, gate_hbm, up_hbm, gain_hbm, both_vmem, gain_vmem, sems):
    own = pl.multiple_of(lax.axis_index("groups") * half, LANES)
    copies = [pltpu.make_async_copy(gain_hbm, gain_vmem, sems.at[2])] + [
        pltpu.make_async_copy(
            weight.at[pl.ds(0, both_vmem.shape[0]), pl.ds(own, half)],
            both_vmem.at[:, pl.ds(at * half, half)],
            sems.at[at],
        )
        for at, weight in enumerate((gate_hbm, up_hbm))
    ]
    for copy in copies:
        copy.start()
    for copy in copies:
        copy.wait()


def load_first(w_gate, w_up, gain, half, count):
    return pl.pallas_call(
        functools.partial(load_gain_kernel, half),
        out_shape=(
            pltpu.VMEM((count, 2 * half), w_gate.dtype),
            pltpu.VMEM(gain.shape, gain.dtype),
        ),
        in_specs=[HBM] * 3,
        out_specs=(VMEM, VMEM),
        scratch_shapes=[pltpu.SemaphoreType.DMA((3,))],
        compiler_params=pltpu.CompilerParams(vmem_limit_bytes=1 << 20),
        cost_estimate=pl.CostEstimate(
            flops=0, bytes_accessed=2 * count * half * 2, transcendentals=0
        ),
        name="load_first",
    )(w_gate, w_up, pltpu.with_memory_space_constraint(gain, pltpu.HBM))


def load_second_kernel(
    half,
    row,
    place,
    lengths,
    hit_lengths,
    start_positions,
    gate_hbm,
    up_hbm,
    both_vmem,
    mark_vmem,
    lengths_smem,
    hit_smem,
    start_smem,
    sems,
):
    own = pl.multiple_of(lax.axis_index("groups") * half, LANES)
    small = [
        pltpu.make_async_copy(source, target, sems.at[2 + at])
        for at, (source, target) in enumerate(
            ((lengths, lengths_smem), (hit_lengths, hit_smem), (start_positions, start_smem))
        )
    ]
    copies = [
        pltpu.make_async_copy(
            weight.at[pl.ds(row, both_vmem.shape[0]), pl.ds(own, half)],
            both_vmem.at[:, pl.ds(at * half, half)],
            sems.at[at],
        )
        for at, weight in enumerate((gate_hbm, up_hbm))
    ]
    for copy in small + copies:
        copy.start()
    for copy in small:
        copy.wait()
    live = live_flag(lengths_smem, hit_smem, start_smem, place())
    mark_vmem[...] = jnp.full(mark_vmem.shape, live.astype(jnp.float32), jnp.float32)
    for copy in copies:
        copy.wait()


def load_second(w_gate, w_up, half, row, count, requests, place):
    return pl.pallas_call(
        functools.partial(load_second_kernel, half, row, place),
        out_shape=(
            pltpu.VMEM((count, 2 * half), w_gate.dtype),
            jax.ShapeDtypeStruct((8, LANES), jnp.float32),
        ),
        in_specs=[HBM] * (2 + len(requests)),
        out_specs=(VMEM, VMEM),
        scratch_shapes=[pltpu.SMEM(array.shape, array.dtype) for array in requests]
        + [pltpu.SemaphoreType.DMA((5,))],
        compiler_params=pltpu.CompilerParams(vmem_limit_bytes=1 << 20),
        cost_estimate=pl.CostEstimate(
            flops=0, bytes_accessed=2 * count * half * 2, transcendentals=0
        ),
        name="load_second",
    )(*requests, w_gate, w_up)


def pack_kernel(*refs):
    pieces, gain_ref, out_ref, wide_ref = refs[:-4], refs[-4], refs[-2], refs[-1]
    rows = out_ref.shape[0]
    lines = out_ref.shape[1] // LANES
    stride = wide_ref.shape[0] // rows
    gain = gain_ref[...].astype(jnp.float32)
    row = 0
    for piece in pieces:
        values = piece[...].astype(jnp.float32)
        mean_sq = jnp.sum(values * values, axis=(1, 2), keepdims=True) * (1.0 / (lines * LANES))
        scaled = values * lax.rsqrt(mean_sq + 1e-05) * gain[None]
        for at in range(piece.shape[0]):
            wide_ref[row * stride : row * stride + lines] = scaled[at]
            row += 1
    for line in range(lines):
        out_ref[:, line * LANES : (line + 1) * LANES] = wide_ref[
            pl.ds(line, rows, stride=stride), :
        ].astype(jnp.bfloat16)


def pack(pieces, gain, mark):
    rows = sum(piece.shape[0] for piece in pieces)
    lines = pieces[0].shape[1]
    return pl.pallas_call(
        pack_kernel,
        out_shape=jax.ShapeDtypeStruct((rows, lines * LANES), jnp.bfloat16),
        in_specs=[VMEM] * (len(pieces) + 1) + [pl.BlockSpec(memory_space=pl.ANY)],
        out_specs=VMEM,
        scratch_shapes=[pltpu.VMEM((rows * (lines + 1), LANES), jnp.float32)],
        compiler_params=pltpu.CompilerParams(vmem_limit_bytes=4 << 20),
        name="pack",
    )(*pieces, pltpu.with_memory_space_constraint(gain, pltpu.VMEM), mark)


def block_kernel(
    half,
    chunk,
    near_ref,
    far_ref,
    first_refs,
    gate_hbm,
    up_hbm,
    down_hbm,
    keep_ref,
    send_ref,
    wide_ref,
    rows_ref,
    product_ref,
    hidden_ref,
    rest_ref,
    down_ref,
    both_sems,
    down_sems,
):
    tile = 256
    rows, depth = rows_ref.shape
    lanes = LANES
    lines = depth // lanes
    stride = wide_ref.shape[0] // rows
    loaded = sum(ref.shape[0] for ref in first_refs)
    own = pl.multiple_of(lax.axis_index("groups") * half, LANES)
    loads = []
    for step, at in enumerate(range(0, depth - loaded, chunk)):
        loads.append(
            [
                pltpu.make_async_copy(
                    weight.at[pl.ds(loaded + at, chunk), pl.ds(own, half)],
                    rest_ref.at[pl.ds(at, chunk), pl.ds(side * half, half)],
                    both_sems.at[step, side],
                )
                for side, weight in enumerate((gate_hbm, up_hbm))
            ]
        )
    pairs = len(loads)
    for step, at in enumerate(range(0, depth, chunk)):
        loads.append(
            [
                pltpu.make_async_copy(
                    down_hbm.at[pl.ds(own, half), pl.ds(at, chunk)],
                    down_ref.at[:, pl.ds(at, chunk)],
                    down_sems.at[step],
                )
            ]
        )

    def start(numbers):
        for number in numbers:
            for copy in loads[number]:
                copy.start()

    def wait(number):
        for copy in loads[number]:
            copy.wait()

    waiting = list(range(len(loads)))

    def start_next(count):
        start(waiting[:count])
        del waiting[:count]

    start_next(1)
    rows_ref[: rows // 2] = near_ref[...]
    rows_ref[rows // 2 :] = far_ref[...]

    def multiply(at, count, ref, row, paced):
        for number, column in enumerate(range(0, 2 * half, tile)):
            columns = pl.ds(column, tile)
            value = jnp.dot(
                rows_ref[:, at : at + count],
                ref[row : row + count, columns],
                preferred_element_type=jnp.float32,
            )
            if at == 0:
                product_ref[:, columns] = value
            else:
                product_ref[:, columns] += value
            if number in paced:
                start_next(1)

    at = 0
    for ref in first_refs:
        multiply(at, ref.shape[0], ref, 0, (1, 6) if at == 0 else (3, 5, 6))
        at += ref.shape[0]
    for step in range(pairs):
        wait(step)
        multiply(at, chunk, rest_ref, step * chunk, (3, 6))
        at += chunk
    gate_out = product_ref[:, :half]
    up_out = product_ref[:, half:]
    hidden_ref[...] = (gate_out / (1.0 + jnp.exp(-gate_out)) * up_out).astype(jnp.bfloat16)
    start_next(len(waiting))
    for step in range(depth // chunk):
        wait(pairs + step)
        for at in range(step * chunk, (step + 1) * chunk, tile):
            result = jnp.dot(
                hidden_ref[...], down_ref[:, pl.ds(at, tile)], preferred_element_type=jnp.float32
            )
            for line in range(tile // lanes):
                wide_ref[pl.ds(at // lanes + line, rows, stride=stride), :] = result[
                    :, line * lanes : (line + 1) * lanes
                ]
        done = step * chunk // lanes
        count = chunk // lanes
        for row in range(rows):
            ready = wide_ref[row * stride + done : row * stride + done + count]
            if row < rows // 2:
                keep_ref[row, done : done + count] = ready
            else:
                send_ref[row - rows // 2, done : done + count] = ready.astype(jnp.bfloat16)


def block(near, far, firsts, w_gate, w_up, w_down, half):
    rows, depth = near.shape
    lines = depth // LANES
    rest = depth - sum(first.shape[0] for first in firsts)

    def body(near_ref, far_ref, *refs):
        count = len(firsts)
        block_kernel(half, CHUNK, near_ref, far_ref, refs[:count], *refs[count:])

    return pl.pallas_call(
        body,
        out_shape=(
            jax.ShapeDtypeStruct((rows, lines, LANES), jnp.float32),
            jax.ShapeDtypeStruct((rows, lines, LANES), jnp.bfloat16),
        ),
        in_specs=[VMEM] * (2 + len(firsts)) + [HBM] * 3,
        out_specs=(VMEM, VMEM),
        scratch_shapes=[
            pltpu.VMEM((2 * rows * (lines + 1), LANES), jnp.float32),
            pltpu.VMEM((2 * rows, depth), jnp.bfloat16),
            pltpu.VMEM((2 * rows, 2 * half), jnp.float32),
            pltpu.VMEM((2 * rows, half), jnp.bfloat16),
            pltpu.VMEM((rest, 2 * half), jnp.bfloat16),
            pltpu.VMEM((half, depth), jnp.bfloat16),
            pltpu.SemaphoreType.DMA((rest // CHUNK, 2)),
            pltpu.SemaphoreType.DMA((depth // CHUNK,)),
        ],
        compiler_params=pltpu.CompilerParams(
            vmem_limit_bytes=(rest * 2 + depth) * half * 2 + (6 << 20)
        ),
        cost_estimate=pl.CostEstimate(
            flops=12 * rows * depth * half,
            bytes_accessed=(rest * 2 + depth) * half * 2,
            transcendentals=0,
        ),
        name="block",
    )(
        near,
        far,
        *(pltpu.with_memory_space_constraint(first, pltpu.VMEM) for first in firsts),
        w_gate,
        w_up,
        w_down,
    )


def finish_kernel(*refs):
    pieces, live_ref, out_ref = refs[:-2], refs[-2], refs[-1]
    totals = pieces[0][...].astype(jnp.float32)
    for piece in pieces[1:]:
        totals = totals + piece[...].astype(jnp.float32)
    totals = jnp.where(live_ref[:1] > 0, totals[0], jnp.zeros_like(totals[0]))
    for line in range(totals.shape[0]):
        out_ref[:, line * LANES : (line + 1) * LANES] = totals[line : line + 1].astype(jnp.bfloat16)


def finish(pieces, live):
    lines = pieces[0].shape[1]
    return pl.pallas_call(
        finish_kernel,
        out_shape=jax.ShapeDtypeStruct((1, lines * LANES), jnp.bfloat16),
        in_specs=[VMEM] * (len(pieces) + 1),
        out_specs=VMEM,
        compiler_params=pltpu.CompilerParams(vmem_limit_bytes=1 << 20),
        name="finish",
    )(*pieces, live)


def swap(value, axes, offset):
    places = range(lax.axis_size(axes))
    return lax.ppermute(value, axes, [(place, place ^ offset) for place in places])


def shared(tokens, norm_gain, w_gate, w_up, w_down, lengths, hit_lengths, start_positions):
    square = ("groups", "x")
    half = w_gate.shape[1] // lax.axis_size("groups")
    w_gate, w_up, w_down = (
        pltpu.with_memory_space_constraint(array, pltpu.HBM) for array in (w_gate, w_up, w_down)
    )
    requests = tuple(
        pltpu.with_memory_space_constraint(array, pltpu.HBM)
        for array in (lengths, hit_lengths, start_positions)
    )

    def place():
        return (lax.axis_index("z") * lax.axis_size("x") + lax.axis_index("x")) * lax.axis_size(
            "core"
        ) + lax.axis_index("core")

    deep = lax.axis_size("z")
    far_first = [3, 1, 2]
    rest = [0] + far_first
    column = [tokens] + [swap(tokens, "z", at) for at in range(1, deep)]
    first, gain = load_first(w_gate, w_up, norm_gain.reshape(-1, LANES), half, 2 * CHUNK)
    column = stack(column, gain)
    plane = [column] + [swap(column, square, at) for at in far_first]
    second, live = load_second(w_gate, w_up, half, 2 * CHUNK, 2 * CHUNK, requests, place)
    near = pack(plane, gain, live)
    far = swap(near, "core", 1)
    kept, sent = block(near, far, (first, second), w_gate, w_up, w_down, half)
    plane = (kept + swap(sent, "core", 1).astype(jnp.float32)).astype(jnp.bfloat16)
    pieces = jnp.split(plane, len(rest), axis=0)
    arrived = [swap(piece, square, at) for at, piece in zip(far_first, pieces[1:])]
    column = pieces[0].astype(jnp.float32)
    for piece in arrived:
        column = column + piece.astype(jnp.float32)
    column = column.astype(jnp.bfloat16)
    pieces = jnp.split(column, deep, axis=0)
    return finish(
        pieces[:1] + [swap(piece, "z", at + 1) for at, piece in enumerate(pieces[1:])], live
    )


def solution(mesh):
    groups, members = mesh.shape["groups"], mesh.shape["tensor"]

    def placed(axes, whole):
        return (
            P(whole, None),
            P(),
            P(None, axes),
            P(None, axes),
            P(axes, None),
            P("groups"),
            P("groups"),
            P("groups"),
        )

    def run(*arrays):
        units = arrays[2].shape[1] // members
        if (
            units % (LANES * groups) == 0
            and arrays[0].shape[0] == groups * members
            and groups == 2
            and members >= 8
            and members & (members - 1) == 0
        ):
            body, axes, whole = shared, ("z", "x", "core"), ROW_LINES
            over = jax.sharding.Mesh(mesh.devices.reshape(groups, members // 4, 2, 2), ROW_LINES)
        else:
            body, axes, whole, over = local, "tensor", ("groups", "tensor"), mesh
        return jax.shard_map(
            body,
            mesh=over,
            in_specs=placed(axes, whole),
            out_specs=P(whole, None),
            check_vma=False,
        )(*arrays)

    return run
```

```python
import functools

import jax
import jax.numpy as jnp
from jax import lax
from jax.experimental import pallas as pl
from jax.experimental.pallas import tpu as pltpu
from jax.sharding import PartitionSpec as P

LANES = 128
ROW_LINES = ("groups", "z", "x", "core")


def normalize(tokens, norm_gain):
    values = tokens.astype(jnp.float32)
    mean_sq = jnp.mean(values * values, axis=-1, keepdims=True)
    return (values * lax.rsqrt(mean_sq + 1e-05) * norm_gain.astype(jnp.float32)).astype(
        jnp.bfloat16
    )


def live_rows(lengths, hit_lengths, start_positions, token_index):
    ends = jnp.cumsum(lengths)
    begins = ends - lengths
    member = (token_index[:, None] >= begins[None, :]) & (token_index[:, None] < ends[None, :])
    member_int = member.astype(jnp.int32)
    offsets = token_index - jnp.sum(member_int * begins[None, :], axis=1)
    position = jnp.sum(member_int * start_positions[None, :], axis=1) + offsets
    covered = jnp.sum(member_int * hit_lengths[None, :], axis=1)
    return position >= covered


def local(tokens, norm_gain, w_gate, w_up, w_down, lengths, hit_lengths, start_positions):
    row_count = tokens.shape[0]
    normed = normalize(tokens, norm_gain)
    piece_rows = lax.all_gather(normed, "tensor", axis=0, tiled=True)
    gate_out = jnp.dot(piece_rows, w_gate, preferred_element_type=jnp.float32)
    up_out = jnp.dot(piece_rows, w_up, preferred_element_type=jnp.float32)
    hidden = (jax.nn.silu(gate_out) * up_out).astype(jnp.bfloat16)
    partial_value = jnp.dot(hidden, w_down, preferred_element_type=jnp.float32)
    rounded = partial_value.astype(jnp.bfloat16)
    totals = jnp.sum(
        lax.all_to_all(rounded[None], "tensor", split_axis=1, concat_axis=0, tiled=True).astype(
            jnp.float32
        ),
        axis=0,
    )
    token_index = lax.axis_index("tensor") * row_count + jnp.arange(row_count, dtype=jnp.int32)
    live = live_rows(lengths, hit_lengths, start_positions, token_index)
    return jnp.where(live[:, None], totals, jnp.zeros_like(totals)).astype(jnp.bfloat16)


VMEM = pl.BlockSpec(memory_space=pltpu.VMEM)
HBM = pl.BlockSpec(memory_space=pltpu.HBM)
CHUNK = 1024


def live_flag(lengths, hit_lengths, start_positions, token):
    begin = 0
    live = False
    for request in range(lengths.shape[0]):
        end = begin + lengths[request]
        position = start_positions[request] + token - begin
        inside = (token >= begin) & (token < end)
        live = live | (inside & (position >= hit_lengths[request]))
        begin = end
    return live


def stack_kernel(*refs):
    pieces, out_ref, wide_ref = refs[:-3], refs[-2], refs[-1]
    lines = out_ref.shape[1]
    for at, piece in enumerate(pieces):
        values = piece[...].astype(jnp.float32)
        for line in range(lines):
            wide_ref[at, line : line + 1] = values[:, line * LANES : (line + 1) * LANES]
    out_ref[...] = wide_ref[...].astype(out_ref.dtype)


def stack(pieces, gain):
    shape = (len(pieces), pieces[0].shape[1] // LANES, LANES)
    return pl.pallas_call(
        stack_kernel,
        out_shape=jax.ShapeDtypeStruct(shape, pieces[0].dtype),
        in_specs=[VMEM] * len(pieces) + [pl.BlockSpec(memory_space=pl.ANY)],
        out_specs=VMEM,
        scratch_shapes=[pltpu.VMEM(shape, jnp.float32)],
        compiler_params=pltpu.CompilerParams(vmem_limit_bytes=2 << 20),
        name="stack",
    )(*pieces, gain)


def load_gain_kernel(half, gate_hbm, up_hbm, gain_hbm, both_vmem, gain_vmem, sems):
    own = pl.multiple_of(lax.axis_index("groups") * half, LANES)
    copies = [pltpu.make_async_copy(gain_hbm, gain_vmem, sems.at[2])] + [
        pltpu.make_async_copy(
            weight.at[pl.ds(0, both_vmem.shape[0]), pl.ds(own, half)],
            both_vmem.at[:, pl.ds(at * half, half)],
            sems.at[at],
        )
        for at, weight in enumerate((gate_hbm, up_hbm))
    ]
    for copy in copies:
        copy.start()
    for copy in copies:
        copy.wait()


def load_first(w_gate, w_up, gain, half, count):
    return pl.pallas_call(
        functools.partial(load_gain_kernel, half),
        out_shape=(
            pltpu.VMEM((count, 2 * half), w_gate.dtype),
            pltpu.VMEM(gain.shape, gain.dtype),
        ),
        in_specs=[HBM] * 3,
        out_specs=(VMEM, VMEM),
        scratch_shapes=[pltpu.SemaphoreType.DMA((3,))],
        compiler_params=pltpu.CompilerParams(vmem_limit_bytes=1 << 20),
        cost_estimate=pl.CostEstimate(
            flops=0, bytes_accessed=2 * count * half * 2, transcendentals=0
        ),
        name="load_first",
    )(w_gate, w_up, pltpu.with_memory_space_constraint(gain, pltpu.HBM))


def load_second_kernel(
    half,
    row,
    place,
    lengths,
    hit_lengths,
    start_positions,
    gate_hbm,
    up_hbm,
    both_vmem,
    mark_vmem,
    lengths_smem,
    hit_smem,
    start_smem,
    sems,
):
    own = pl.multiple_of(lax.axis_index("groups") * half, LANES)
    small = [
        pltpu.make_async_copy(source, target, sems.at[2 + at])
        for at, (source, target) in enumerate(
            ((lengths, lengths_smem), (hit_lengths, hit_smem), (start_positions, start_smem))
        )
    ]
    copies = [
        pltpu.make_async_copy(
            weight.at[pl.ds(row, both_vmem.shape[0]), pl.ds(own, half)],
            both_vmem.at[:, pl.ds(at * half, half)],
            sems.at[at],
        )
        for at, weight in enumerate((gate_hbm, up_hbm))
    ]
    for copy in small + copies:
        copy.start()
    for copy in small:
        copy.wait()
    live = live_flag(lengths_smem, hit_smem, start_smem, place())
    mark_vmem[...] = jnp.full(mark_vmem.shape, live.astype(jnp.float32), jnp.float32)
    for copy in copies:
        copy.wait()


def load_second(w_gate, w_up, half, row, count, requests, place):
    return pl.pallas_call(
        functools.partial(load_second_kernel, half, row, place),
        out_shape=(
            pltpu.VMEM((count, 2 * half), w_gate.dtype),
            jax.ShapeDtypeStruct((8, LANES), jnp.float32),
        ),
        in_specs=[HBM] * (2 + len(requests)),
        out_specs=(VMEM, VMEM),
        scratch_shapes=[pltpu.SMEM(array.shape, array.dtype) for array in requests]
        + [pltpu.SemaphoreType.DMA((5,))],
        compiler_params=pltpu.CompilerParams(vmem_limit_bytes=1 << 20),
        cost_estimate=pl.CostEstimate(
            flops=0, bytes_accessed=2 * count * half * 2, transcendentals=0
        ),
        name="load_second",
    )(*requests, w_gate, w_up)


def pack_kernel(*refs):
    pieces, gain_ref, out_ref, wide_ref = refs[:-4], refs[-4], refs[-2], refs[-1]
    rows = out_ref.shape[0]
    lines = out_ref.shape[1] // LANES
    stride = wide_ref.shape[0] // rows
    gain = gain_ref[...].astype(jnp.float32)
    row = 0
    for piece in pieces:
        values = piece[...].astype(jnp.float32)
        mean_sq = jnp.sum(values * values, axis=(1, 2), keepdims=True) * (1.0 / (lines * LANES))
        scaled = values * lax.rsqrt(mean_sq + 1e-05) * gain[None]
        for at in range(piece.shape[0]):
            wide_ref[row * stride : row * stride + lines] = scaled[at]
            row += 1
    for line in range(lines):
        out_ref[:, line * LANES : (line + 1) * LANES] = wide_ref[
            pl.ds(line, rows, stride=stride), :
        ].astype(jnp.bfloat16)


def pack(pieces, gain, mark):
    rows = sum(piece.shape[0] for piece in pieces)
    lines = pieces[0].shape[1]
    return pl.pallas_call(
        pack_kernel,
        out_shape=jax.ShapeDtypeStruct((rows, lines * LANES), jnp.bfloat16),
        in_specs=[VMEM] * (len(pieces) + 1) + [pl.BlockSpec(memory_space=pl.ANY)],
        out_specs=VMEM,
        scratch_shapes=[pltpu.VMEM((rows * (lines + 1), LANES), jnp.float32)],
        compiler_params=pltpu.CompilerParams(vmem_limit_bytes=4 << 20),
        name="pack",
    )(*pieces, pltpu.with_memory_space_constraint(gain, pltpu.VMEM), mark)


def block_kernel(
    half,
    chunk,
    near_ref,
    far_ref,
    first_refs,
    gate_hbm,
    up_hbm,
    down_hbm,
    keep_ref,
    send_ref,
    wide_ref,
    rows_ref,
    product_ref,
    hidden_ref,
    rest_ref,
    down_ref,
    both_sems,
    down_sems,
):
    tile = 256
    rows, depth = rows_ref.shape
    lanes = LANES
    lines = depth // lanes
    stride = wide_ref.shape[0] // rows
    loaded = sum(ref.shape[0] for ref in first_refs)
    own = pl.multiple_of(lax.axis_index("groups") * half, LANES)
    loads = []
    for step, at in enumerate(range(0, depth - loaded, chunk)):
        loads.append(
            [
                pltpu.make_async_copy(
                    weight.at[pl.ds(loaded + at, chunk), pl.ds(own, half)],
                    rest_ref.at[pl.ds(at, chunk), pl.ds(side * half, half)],
                    both_sems.at[step, side],
                )
                for side, weight in enumerate((gate_hbm, up_hbm))
            ]
        )
    pairs = len(loads)
    for step, at in enumerate(range(0, depth, chunk)):
        loads.append(
            [
                pltpu.make_async_copy(
                    down_hbm.at[pl.ds(own, half), pl.ds(at, chunk)],
                    down_ref.at[:, pl.ds(at, chunk)],
                    down_sems.at[step],
                )
            ]
        )

    def start(numbers):
        for number in numbers:
            for copy in loads[number]:
                copy.start()

    def wait(number):
        for copy in loads[number]:
            copy.wait()

    waiting = list(range(len(loads)))

    def start_next(count):
        start(waiting[:count])
        del waiting[:count]

    start_next(1)
    rows_ref[: rows // 2] = near_ref[...]
    rows_ref[rows // 2 :] = far_ref[...]

    def multiply(at, count, ref, row, paced):
        for number, column in enumerate(range(0, 2 * half, tile)):
            columns = pl.ds(column, tile)
            value = jnp.dot(
                rows_ref[:, at : at + count],
                ref[row : row + count, columns],
                preferred_element_type=jnp.float32,
            )
            if at == 0:
                product_ref[:, columns] = value
            else:
                product_ref[:, columns] += value
            if number in paced:
                start_next(1)

    at = 0
    for ref in first_refs:
        multiply(at, ref.shape[0], ref, 0, (1, 6) if at == 0 else (3, 5, 6))
        at += ref.shape[0]
    for step in range(pairs):
        wait(step)
        multiply(at, chunk, rest_ref, step * chunk, (3, 6))
        at += chunk
    gate_out = product_ref[:, :half]
    up_out = product_ref[:, half:]
    hidden_ref[...] = (gate_out / (1.0 + jnp.exp(-gate_out)) * up_out).astype(jnp.bfloat16)
    start_next(len(waiting))
    for step in range(depth // chunk):
        wait(pairs + step)
        for at in range(step * chunk, (step + 1) * chunk, tile):
            result = jnp.dot(
                hidden_ref[...], down_ref[:, pl.ds(at, tile)], preferred_element_type=jnp.float32
            )
            for line in range(tile // lanes):
                wide_ref[pl.ds(at // lanes + line, rows, stride=stride), :] = result[
                    :, line * lanes : (line + 1) * lanes
                ]
        done = step * chunk // lanes
        count = chunk // lanes
        for row in range(rows):
            ready = wide_ref[row * stride + done : row * stride + done + count]
            if row < rows // 2:
                keep_ref[row, done : done + count] = ready
            else:
                send_ref[row - rows // 2, done : done + count] = ready.astype(jnp.bfloat16)


def block(near, far, firsts, w_gate, w_up, w_down, half):
    rows, depth = near.shape
    lines = depth // LANES
    rest = depth - sum(first.shape[0] for first in firsts)

    def body(near_ref, far_ref, *refs):
        count = len(firsts)
        block_kernel(half, CHUNK, near_ref, far_ref, refs[:count], *refs[count:])

    return pl.pallas_call(
        body,
        out_shape=(
            jax.ShapeDtypeStruct((rows, lines, LANES), jnp.float32),
            jax.ShapeDtypeStruct((rows, lines, LANES), jnp.bfloat16),
        ),
        in_specs=[VMEM] * (2 + len(firsts)) + [HBM] * 3,
        out_specs=(VMEM, VMEM),
        scratch_shapes=[
            pltpu.VMEM((2 * rows * (lines + 1), LANES), jnp.float32),
            pltpu.VMEM((2 * rows, depth), jnp.bfloat16),
            pltpu.VMEM((2 * rows, 2 * half), jnp.float32),
            pltpu.VMEM((2 * rows, half), jnp.bfloat16),
            pltpu.VMEM((rest, 2 * half), jnp.bfloat16),
            pltpu.VMEM((half, depth), jnp.bfloat16),
            pltpu.SemaphoreType.DMA((rest // CHUNK, 2)),
            pltpu.SemaphoreType.DMA((depth // CHUNK,)),
        ],
        compiler_params=pltpu.CompilerParams(
            vmem_limit_bytes=(rest * 2 + depth) * half * 2 + (6 << 20)
        ),
        cost_estimate=pl.CostEstimate(
            flops=12 * rows * depth * half,
            bytes_accessed=(rest * 2 + depth) * half * 2,
            transcendentals=0,
        ),
        name="block",
    )(
        near,
        far,
        *(pltpu.with_memory_space_constraint(first, pltpu.VMEM) for first in firsts),
        w_gate,
        w_up,
        w_down,
    )


def finish_kernel(*refs):
    pieces, live_ref, out_ref = refs[:-2], refs[-2], refs[-1]
    totals = pieces[0][...].astype(jnp.float32)
    for piece in pieces[1:]:
        totals = totals + piece[...].astype(jnp.float32)
    totals = jnp.where(live_ref[:1] > 0, totals[0], jnp.zeros_like(totals[0]))
    for line in range(totals.shape[0]):
        out_ref[:, line * LANES : (line + 1) * LANES] = totals[line : line + 1].astype(jnp.bfloat16)


def finish(pieces, live):
    lines = pieces[0].shape[1]
    return pl.pallas_call(
        finish_kernel,
        out_shape=jax.ShapeDtypeStruct((1, lines * LANES), jnp.bfloat16),
        in_specs=[VMEM] * (len(pieces) + 1),
        out_specs=VMEM,
        compiler_params=pltpu.CompilerParams(vmem_limit_bytes=1 << 20),
        name="finish",
    )(*pieces, live)


def swap(value, axes, offset):
    places = range(lax.axis_size(axes))
    return lax.ppermute(value, axes, [(place, place ^ offset) for place in places])


def sum_direct(column, deep):
    pieces = jnp.split(column.astype(jnp.bfloat16), deep, axis=0)
    return pieces[:1] + [swap(piece, "z", at + 1) for at, piece in enumerate(pieces[1:])]


def sum_line(column):
    inward = lax.ppermute(column[1:].astype(jnp.bfloat16), "z", [(0, 1), (3, 2)]).astype(
        jnp.float32
    )
    own = column[:1] + inward[:1]
    crossing = jnp.concatenate([column[3:] + inward[1:2], column[2:3] + inward[2:]], axis=0)
    crossed = lax.ppermute(crossing.astype(jnp.bfloat16), "z", [(1, 2), (2, 1)])
    outer = column[1:2] + crossed[1:].astype(jnp.float32)
    outward = lax.ppermute(outer.astype(jnp.bfloat16), "z", [(1, 0), (2, 3)])
    return [own, crossed[:1], outward]


def shared(tokens, norm_gain, w_gate, w_up, w_down, lengths, hit_lengths, start_positions):
    square = ("groups", "x")
    half = w_gate.shape[1] // lax.axis_size("groups")
    w_gate, w_up, w_down = (
        pltpu.with_memory_space_constraint(array, pltpu.HBM) for array in (w_gate, w_up, w_down)
    )
    requests = tuple(
        pltpu.with_memory_space_constraint(array, pltpu.HBM)
        for array in (lengths, hit_lengths, start_positions)
    )

    def place():
        return (lax.axis_index("z") * lax.axis_size("x") + lax.axis_index("x")) * lax.axis_size(
            "core"
        ) + lax.axis_index("core")

    deep = lax.axis_size("z")
    far_first = [3, 1, 2]
    rest = [0] + far_first
    column = [tokens] + [swap(tokens, "z", at) for at in range(1, deep)]
    first, gain = load_first(w_gate, w_up, norm_gain.reshape(-1, LANES), half, 2 * CHUNK)
    column = stack(column, gain)
    plane = [column] + [swap(column, square, at) for at in far_first]
    second, live = load_second(w_gate, w_up, half, 2 * CHUNK, 3 * CHUNK, requests, place)
    near = pack(plane, gain, live)
    far = swap(near, "core", 1)
    kept, sent = block(near, far, (first, second), w_gate, w_up, w_down, half)
    plane = (kept + swap(sent, "core", 1).astype(jnp.float32)).astype(jnp.bfloat16)
    pieces = jnp.split(plane, len(rest), axis=0)
    arrived = [swap(piece, square, at) for at, piece in zip(far_first, pieces[1:])]
    column = pieces[0].astype(jnp.float32)
    for piece in arrived:
        column = column + piece.astype(jnp.float32)
    return finish(sum_line(column) if deep == 4 else sum_direct(column, deep), live)


def solution(mesh):
    groups, members = mesh.shape["groups"], mesh.shape["tensor"]

    def placed(axes, whole):
        return (
            P(whole, None),
            P(),
            P(None, axes),
            P(None, axes),
            P(axes, None),
            P("groups"),
            P("groups"),
            P("groups"),
        )

    def run(*arrays):
        units = arrays[2].shape[1] // members
        if (
            units % (LANES * groups) == 0
            and arrays[0].shape[0] == groups * members
            and groups == 2
            and members >= 8
            and members & (members - 1) == 0
        ):
            body, axes, whole = shared, ("z", "x", "core"), ROW_LINES
            over = jax.sharding.Mesh(mesh.devices.reshape(groups, members // 4, 2, 2), ROW_LINES)
        else:
            body, axes, whole, over = local, "tensor", ("groups", "tensor"), mesh
        return jax.shard_map(
            body,
            mesh=over,
            in_specs=placed(axes, whole),
            out_specs=P(whole, None),
            check_vma=False,
        )(*arrays)

    return run
```

```python
import functools

import jax
import jax.numpy as jnp
from jax import lax
from jax.experimental import pallas as pl
from jax.experimental.pallas import tpu as pltpu
from jax.sharding import PartitionSpec as P

LANES = 128
ROW_LINES = ("groups", "z", "x", "core")


def normalize(tokens, norm_gain):
    values = tokens.astype(jnp.float32)
    mean_sq = jnp.mean(values * values, axis=-1, keepdims=True)
    return (values * lax.rsqrt(mean_sq + 1e-05) * norm_gain.astype(jnp.float32)).astype(
        jnp.bfloat16
    )


def live_rows(lengths, hit_lengths, start_positions, token_index):
    ends = jnp.cumsum(lengths)
    begins = ends - lengths
    member = (token_index[:, None] >= begins[None, :]) & (token_index[:, None] < ends[None, :])
    member_int = member.astype(jnp.int32)
    offsets = token_index - jnp.sum(member_int * begins[None, :], axis=1)
    position = jnp.sum(member_int * start_positions[None, :], axis=1) + offsets
    covered = jnp.sum(member_int * hit_lengths[None, :], axis=1)
    return position >= covered


def local(tokens, norm_gain, w_gate, w_up, w_down, lengths, hit_lengths, start_positions):
    row_count = tokens.shape[0]
    normed = normalize(tokens, norm_gain)
    piece_rows = lax.all_gather(normed, "tensor", axis=0, tiled=True)
    gate_out = jnp.dot(piece_rows, w_gate, preferred_element_type=jnp.float32)
    up_out = jnp.dot(piece_rows, w_up, preferred_element_type=jnp.float32)
    hidden = (jax.nn.silu(gate_out) * up_out).astype(jnp.bfloat16)
    partial_value = jnp.dot(hidden, w_down, preferred_element_type=jnp.float32)
    rounded = partial_value.astype(jnp.bfloat16)
    totals = jnp.sum(
        lax.all_to_all(rounded[None], "tensor", split_axis=1, concat_axis=0, tiled=True).astype(
            jnp.float32
        ),
        axis=0,
    )
    token_index = lax.axis_index("tensor") * row_count + jnp.arange(row_count, dtype=jnp.int32)
    live = live_rows(lengths, hit_lengths, start_positions, token_index)
    return jnp.where(live[:, None], totals, jnp.zeros_like(totals)).astype(jnp.bfloat16)


VMEM = pl.BlockSpec(memory_space=pltpu.VMEM)
HBM = pl.BlockSpec(memory_space=pltpu.HBM)
CHUNK = 1024


def live_flag(lengths, hit_lengths, start_positions, token):
    begin = 0
    live = False
    for request in range(lengths.shape[0]):
        end = begin + lengths[request]
        position = start_positions[request] + token - begin
        inside = (token >= begin) & (token < end)
        live = live | (inside & (position >= hit_lengths[request]))
        begin = end
    return live


def stack_kernel(rows, *refs):
    pieces, out_ref, wide_ref = refs[:-3], refs[-2], refs[-1]
    lines = out_ref.shape[1]
    for at, piece in zip(rows, pieces):
        values = piece[...].astype(jnp.float32)
        for line in range(lines):
            wide_ref[at, line : line + 1] = values[:, line * LANES : (line + 1) * LANES]
    out_ref[...] = wide_ref[...].astype(out_ref.dtype)


def stack(rows, pieces, gain):
    shape = (len(pieces), pieces[0].shape[1] // LANES, LANES)
    return pl.pallas_call(
        functools.partial(stack_kernel, rows),
        out_shape=jax.ShapeDtypeStruct(shape, pieces[0].dtype),
        in_specs=[VMEM] * len(pieces) + [pl.BlockSpec(memory_space=pl.ANY)],
        out_specs=VMEM,
        scratch_shapes=[pltpu.VMEM(shape, jnp.float32)],
        compiler_params=pltpu.CompilerParams(vmem_limit_bytes=2 << 20),
        name="stack",
    )(*pieces, gain)


def load_gain_kernel(half, gate_hbm, up_hbm, gain_hbm, both_vmem, gain_vmem, sems):
    own = pl.multiple_of(lax.axis_index("groups") * half, LANES)
    copies = [pltpu.make_async_copy(gain_hbm, gain_vmem, sems.at[2])] + [
        pltpu.make_async_copy(
            weight.at[pl.ds(0, both_vmem.shape[0]), pl.ds(own, half)],
            both_vmem.at[:, pl.ds(at * half, half)],
            sems.at[at],
        )
        for at, weight in enumerate((gate_hbm, up_hbm))
    ]
    for copy in copies:
        copy.start()
    for copy in copies:
        copy.wait()


def load_first(w_gate, w_up, gain, half, count):
    return pl.pallas_call(
        functools.partial(load_gain_kernel, half),
        out_shape=(
            pltpu.VMEM((count, 2 * half), w_gate.dtype),
            pltpu.VMEM(gain.shape, gain.dtype),
        ),
        in_specs=[HBM] * 3,
        out_specs=(VMEM, VMEM),
        scratch_shapes=[pltpu.SemaphoreType.DMA((3,))],
        compiler_params=pltpu.CompilerParams(vmem_limit_bytes=1 << 20),
        cost_estimate=pl.CostEstimate(
            flops=0, bytes_accessed=2 * count * half * 2, transcendentals=0
        ),
        name="load_first",
    )(w_gate, w_up, pltpu.with_memory_space_constraint(gain, pltpu.HBM))


def load_second_kernel(
    half,
    row,
    place,
    lengths,
    hit_lengths,
    start_positions,
    gate_hbm,
    up_hbm,
    both_vmem,
    mark_vmem,
    lengths_smem,
    hit_smem,
    start_smem,
    sems,
):
    own = pl.multiple_of(lax.axis_index("groups") * half, LANES)
    small = [
        pltpu.make_async_copy(source, target, sems.at[2 + at])
        for at, (source, target) in enumerate(
            ((lengths, lengths_smem), (hit_lengths, hit_smem), (start_positions, start_smem))
        )
    ]
    copies = [
        pltpu.make_async_copy(
            weight.at[pl.ds(row, both_vmem.shape[0]), pl.ds(own, half)],
            both_vmem.at[:, pl.ds(at * half, half)],
            sems.at[at],
        )
        for at, weight in enumerate((gate_hbm, up_hbm))
    ]
    for copy in small + copies:
        copy.start()
    for copy in small:
        copy.wait()
    live = live_flag(lengths_smem, hit_smem, start_smem, place())
    mark_vmem[...] = jnp.full(mark_vmem.shape, live.astype(jnp.float32), jnp.float32)
    for copy in copies:
        copy.wait()


def load_second(w_gate, w_up, half, row, count, requests, place):
    return pl.pallas_call(
        functools.partial(load_second_kernel, half, row, place),
        out_shape=(
            pltpu.VMEM((count, 2 * half), w_gate.dtype),
            jax.ShapeDtypeStruct((8, LANES), jnp.float32),
        ),
        in_specs=[HBM] * (2 + len(requests)),
        out_specs=(VMEM, VMEM),
        scratch_shapes=[pltpu.SMEM(array.shape, array.dtype) for array in requests]
        + [pltpu.SemaphoreType.DMA((5,))],
        compiler_params=pltpu.CompilerParams(vmem_limit_bytes=1 << 20),
        cost_estimate=pl.CostEstimate(
            flops=0, bytes_accessed=2 * count * half * 2, transcendentals=0
        ),
        name="load_second",
    )(*requests, w_gate, w_up)


def pack_kernel(*refs):
    pieces, gain_ref, out_ref, wide_ref = refs[:-4], refs[-4], refs[-2], refs[-1]
    rows = out_ref.shape[0]
    lines = out_ref.shape[1] // LANES
    stride = wide_ref.shape[0] // rows
    gain = gain_ref[...].astype(jnp.float32)
    row = 0
    for piece in pieces:
        values = piece[...].astype(jnp.float32)
        mean_sq = jnp.sum(values * values, axis=(1, 2), keepdims=True) * (1.0 / (lines * LANES))
        scaled = values * lax.rsqrt(mean_sq + 1e-05) * gain[None]
        for at in range(piece.shape[0]):
            wide_ref[row * stride : row * stride + lines] = scaled[at]
            row += 1
    for line in range(lines):
        out_ref[:, line * LANES : (line + 1) * LANES] = wide_ref[
            pl.ds(line, rows, stride=stride), :
        ].astype(jnp.bfloat16)


def pack(pieces, gain, mark):
    rows = sum(piece.shape[0] for piece in pieces)
    lines = pieces[0].shape[1]
    return pl.pallas_call(
        pack_kernel,
        out_shape=jax.ShapeDtypeStruct((rows, lines * LANES), jnp.bfloat16),
        in_specs=[VMEM] * (len(pieces) + 1) + [pl.BlockSpec(memory_space=pl.ANY)],
        out_specs=VMEM,
        scratch_shapes=[pltpu.VMEM((rows * (lines + 1), LANES), jnp.float32)],
        compiler_params=pltpu.CompilerParams(vmem_limit_bytes=4 << 20),
        name="pack",
    )(*pieces, pltpu.with_memory_space_constraint(gain, pltpu.VMEM), mark)


def block_kernel(
    half,
    chunk,
    near_ref,
    far_ref,
    first_refs,
    gate_hbm,
    up_hbm,
    down_hbm,
    keep_ref,
    send_ref,
    wide_ref,
    rows_ref,
    product_ref,
    hidden_ref,
    rest_ref,
    down_ref,
    both_sems,
    down_sems,
):
    tile = 256
    rows, depth = rows_ref.shape
    lanes = LANES
    lines = depth // lanes
    stride = wide_ref.shape[0] // rows
    loaded = sum(ref.shape[0] for ref in first_refs)
    own = pl.multiple_of(lax.axis_index("groups") * half, LANES)
    loads = []
    deal = rest_ref.shape[0] // both_sems.shape[0]
    for step, at in enumerate(range(0, depth - loaded, deal)):
        loads.append(
            [
                pltpu.make_async_copy(
                    weight.at[pl.ds(loaded + at, deal), pl.ds(own, half)],
                    rest_ref.at[pl.ds(at, deal), pl.ds(side * half, half)],
                    both_sems.at[step, side],
                )
                for side, weight in enumerate((gate_hbm, up_hbm))
            ]
        )
    pairs = len(loads)
    for step, at in enumerate(range(0, depth, chunk)):
        loads.append(
            [
                pltpu.make_async_copy(
                    down_hbm.at[pl.ds(own, half), pl.ds(at, chunk)],
                    down_ref.at[:, pl.ds(at, chunk)],
                    down_sems.at[step],
                )
            ]
        )

    def start(first, last):
        for number in range(first, min(last, len(loads))):
            for copy in loads[number]:
                copy.start()

    def wait(number):
        for copy in loads[number]:
            copy.wait()

    def multiply(at, count, ref, row):
        for column in range(0, 2 * half, tile):
            columns = pl.ds(column, tile)
            value = jnp.dot(
                rows_ref[:, at : at + count],
                ref[row : row + count, columns],
                preferred_element_type=jnp.float32,
            )
            if at == 0:
                product_ref[:, columns] = value
            else:
                product_ref[:, columns] += value

    start(0, pairs)
    rows_ref[: rows // 2] = near_ref[...]
    rows_ref[rows // 2 :] = far_ref[...]
    at = 0
    for ref in first_refs:
        multiply(at, ref.shape[0], ref, 0)
        at += ref.shape[0]
    start(pairs, pairs + 2)
    for step in range(pairs):
        wait(step)
        multiply(at, deal, rest_ref, step * deal)
        start(pairs + 2 + step, len(loads) if step == pairs - 1 else pairs + 3 + step)
        at += deal
    gate_out = product_ref[:, :half]
    up_out = product_ref[:, half:]
    hidden_ref[...] = (gate_out / (1.0 + jnp.exp(-gate_out)) * up_out).astype(jnp.bfloat16)
    for step in range(depth // chunk):
        wait(pairs + step)
        for at in range(step * chunk, (step + 1) * chunk, tile):
            result = jnp.dot(
                hidden_ref[...], down_ref[:, pl.ds(at, tile)], preferred_element_type=jnp.float32
            )
            for line in range(tile // lanes):
                wide_ref[pl.ds(at // lanes + line, rows, stride=stride), :] = result[
                    :, line * lanes : (line + 1) * lanes
                ]
        done = step * chunk // lanes
        count = chunk // lanes
        for row in range(rows):
            ready = wide_ref[row * stride + done : row * stride + done + count]
            if row < rows // 2:
                keep_ref[row, done : done + count] = ready
            else:
                send_ref[row - rows // 2, done : done + count] = ready.astype(jnp.bfloat16)


def block(near, far, firsts, w_gate, w_up, w_down, half):
    rows, depth = near.shape
    lines = depth // LANES
    rest = depth - sum(first.shape[0] for first in firsts)

    def body(near_ref, far_ref, *refs):
        count = len(firsts)
        block_kernel(half, 2 * CHUNK, near_ref, far_ref, refs[:count], *refs[count:])

    return pl.pallas_call(
        body,
        out_shape=(
            jax.ShapeDtypeStruct((rows, lines, LANES), jnp.float32),
            jax.ShapeDtypeStruct((rows, lines, LANES), jnp.bfloat16),
        ),
        in_specs=[VMEM] * (2 + len(firsts)) + [HBM] * 3,
        out_specs=(VMEM, VMEM),
        scratch_shapes=[
            pltpu.VMEM((2 * rows * (lines + 1), LANES), jnp.float32),
            pltpu.VMEM((2 * rows, depth), jnp.bfloat16),
            pltpu.VMEM((2 * rows, 2 * half), jnp.float32),
            pltpu.VMEM((2 * rows, half), jnp.bfloat16),
            pltpu.VMEM((rest, 2 * half), jnp.bfloat16),
            pltpu.VMEM((half, depth), jnp.bfloat16),
            pltpu.SemaphoreType.DMA((2, 2)),
            pltpu.SemaphoreType.DMA((depth // (2 * CHUNK),)),
        ],
        compiler_params=pltpu.CompilerParams(
            vmem_limit_bytes=(rest * 2 + depth) * half * 2 + (6 << 20)
        ),
        cost_estimate=pl.CostEstimate(
            flops=12 * rows * depth * half,
            bytes_accessed=(rest * 2 + depth) * half * 2,
            transcendentals=0,
        ),
        name="block",
    )(
        near,
        far,
        *(pltpu.with_memory_space_constraint(first, pltpu.VMEM) for first in firsts),
        w_gate,
        w_up,
        w_down,
    )


def finish_kernel(*refs):
    pieces, live_ref, out_ref = refs[:-2], refs[-2], refs[-1]
    totals = pieces[0][...].astype(jnp.float32)
    for piece in pieces[1:]:
        totals = totals + piece[...].astype(jnp.float32)
    totals = jnp.where(live_ref[:1] > 0, totals[0], jnp.zeros_like(totals[0]))
    for line in range(totals.shape[0]):
        out_ref[:, line * LANES : (line + 1) * LANES] = totals[line : line + 1].astype(jnp.bfloat16)


def finish(pieces, live):
    lines = pieces[0].shape[1]
    return pl.pallas_call(
        finish_kernel,
        out_shape=jax.ShapeDtypeStruct((1, lines * LANES), jnp.bfloat16),
        in_specs=[VMEM] * (len(pieces) + 1),
        out_specs=VMEM,
        compiler_params=pltpu.CompilerParams(vmem_limit_bytes=1 << 20),
        name="finish",
    )(*pieces, live)


def swap(value, axes, offset):
    places = range(lax.axis_size(axes))
    return lax.ppermute(value, axes, [(place, place ^ offset) for place in places])


def shared(tokens, norm_gain, w_gate, w_up, w_down, lengths, hit_lengths, start_positions):
    square = ("groups", "x")
    half = w_gate.shape[1] // lax.axis_size("groups")
    w_gate, w_up, w_down = (
        pltpu.with_memory_space_constraint(array, pltpu.HBM) for array in (w_gate, w_up, w_down)
    )
    requests = tuple(
        pltpu.with_memory_space_constraint(array, pltpu.HBM)
        for array in (lengths, hit_lengths, start_positions)
    )

    def place():
        return (lax.axis_index("z") * lax.axis_size("x") + lax.axis_index("x")) * lax.axis_size(
            "core"
        ) + lax.axis_index("core")

    deep = lax.axis_size("z")
    others = range(1, lax.axis_size(square))
    rows = [0] + list(range(2, deep)) + [1]
    column = [swap(tokens, "z", at) if at else tokens for at in rows]
    first, gain = load_first(w_gate, w_up, norm_gain.reshape(-1, LANES), half, 2 * CHUNK)
    column = stack(rows, column, gain)
    plane = [column] + [swap(column, square, at) for at in others]
    second, live = load_second(w_gate, w_up, half, 2 * CHUNK, 3 * CHUNK, requests, place)
    near = pack(plane, gain, live)
    far = swap(near, "core", 1)
    kept, sent = block(near, far, (first, second), w_gate, w_up, w_down, half)
    plane = (kept + swap(sent, "core", 1).astype(jnp.float32)).astype(jnp.bfloat16)
    pieces = jnp.split(plane, lax.axis_size(square), axis=0)
    column = pieces[0].astype(jnp.float32)
    for piece in [swap(pieces[at], square, at) for at in reversed(others)]:
        column = column + piece.astype(jnp.float32)
    pieces = jnp.split(column.astype(jnp.bfloat16), deep, axis=0)
    return finish(
        pieces[:1] + [swap(piece, "z", at + 1) for at, piece in enumerate(pieces[1:])], live
    )


def solution(mesh):
    groups, members = mesh.shape["groups"], mesh.shape["tensor"]

    def placed(axes, whole):
        return (
            P(whole, None),
            P(),
            P(None, axes),
            P(None, axes),
            P(axes, None),
            P("groups"),
            P("groups"),
            P("groups"),
        )

    def run(*arrays):
        units = arrays[2].shape[1] // members
        if (
            units % (LANES * groups) == 0
            and arrays[0].shape[0] == groups * members
            and groups == 2
            and members >= 8
            and members & (members - 1) == 0
        ):
            body, axes, whole = shared, ("z", "x", "core"), ROW_LINES
            over = jax.sharding.Mesh(mesh.devices.reshape(groups, members // 4, 2, 2), ROW_LINES)
        else:
            body, axes, whole, over = local, "tensor", ("groups", "tensor"), mesh
        return jax.shard_map(
            body,
            mesh=over,
            in_specs=placed(axes, whole),
            out_specs=P(whole, None),
            check_vma=False,
        )(*arrays)

    return run
```

```python
import functools

import jax
import jax.numpy as jnp
from jax import lax
from jax.experimental import pallas as pl
from jax.experimental.pallas import tpu as pltpu
from jax.sharding import PartitionSpec as P

LANES = 128
ROW_LINES = ("groups", "z", "x", "core")


def normalize(tokens, norm_gain):
    values = tokens.astype(jnp.float32)
    mean_sq = jnp.mean(values * values, axis=-1, keepdims=True)
    return (values * lax.rsqrt(mean_sq + 1e-05) * norm_gain.astype(jnp.float32)).astype(
        jnp.bfloat16
    )


def live_rows(lengths, hit_lengths, start_positions, token_index):
    ends = jnp.cumsum(lengths)
    begins = ends - lengths
    member = (token_index[:, None] >= begins[None, :]) & (token_index[:, None] < ends[None, :])
    member_int = member.astype(jnp.int32)
    offsets = token_index - jnp.sum(member_int * begins[None, :], axis=1)
    position = jnp.sum(member_int * start_positions[None, :], axis=1) + offsets
    covered = jnp.sum(member_int * hit_lengths[None, :], axis=1)
    return position >= covered


def local(tokens, norm_gain, w_gate, w_up, w_down, lengths, hit_lengths, start_positions):
    row_count = tokens.shape[0]
    normed = normalize(tokens, norm_gain)
    piece_rows = lax.all_gather(normed, "tensor", axis=0, tiled=True)
    gate_out = jnp.dot(piece_rows, w_gate, preferred_element_type=jnp.float32)
    up_out = jnp.dot(piece_rows, w_up, preferred_element_type=jnp.float32)
    hidden = (jax.nn.silu(gate_out) * up_out).astype(jnp.bfloat16)
    partial_value = jnp.dot(hidden, w_down, preferred_element_type=jnp.float32)
    rounded = partial_value.astype(jnp.bfloat16)
    totals = jnp.sum(
        lax.all_to_all(rounded[None], "tensor", split_axis=1, concat_axis=0, tiled=True).astype(
            jnp.float32
        ),
        axis=0,
    )
    token_index = lax.axis_index("tensor") * row_count + jnp.arange(row_count, dtype=jnp.int32)
    live = live_rows(lengths, hit_lengths, start_positions, token_index)
    return jnp.where(live[:, None], totals, jnp.zeros_like(totals)).astype(jnp.bfloat16)


VMEM = pl.BlockSpec(memory_space=pltpu.VMEM)
HBM = pl.BlockSpec(memory_space=pltpu.HBM)
CHUNK = 1024


def live_flag(lengths, hit_lengths, start_positions, token):
    begin = 0
    live = False
    for request in range(lengths.shape[0]):
        end = begin + lengths[request]
        position = start_positions[request] + token - begin
        inside = (token >= begin) & (token < end)
        live = live | (inside & (position >= hit_lengths[request]))
        begin = end
    return live


def stack_kernel(rows, *refs):
    pieces, out_ref, wide_ref = refs[:-3], refs[-2], refs[-1]
    lines = out_ref.shape[1]
    for at, piece in zip(rows, pieces):
        values = piece[...].astype(jnp.float32)
        for line in range(lines):
            wide_ref[at, line : line + 1] = values[:, line * LANES : (line + 1) * LANES]
    out_ref[...] = wide_ref[...].astype(out_ref.dtype)


def stack(rows, pieces, gain):
    shape = (len(pieces), pieces[0].shape[1] // LANES, LANES)
    return pl.pallas_call(
        functools.partial(stack_kernel, rows),
        out_shape=jax.ShapeDtypeStruct(shape, pieces[0].dtype),
        in_specs=[VMEM] * len(pieces) + [pl.BlockSpec(memory_space=pl.ANY)],
        out_specs=VMEM,
        scratch_shapes=[pltpu.VMEM(shape, jnp.float32)],
        compiler_params=pltpu.CompilerParams(vmem_limit_bytes=2 << 20),
        name="stack",
    )(*pieces, gain)


def load_gain_kernel(half, gate_hbm, up_hbm, gain_hbm, both_vmem, gain_vmem, sems):
    own = pl.multiple_of(lax.axis_index("groups") * half, LANES)
    copies = [pltpu.make_async_copy(gain_hbm, gain_vmem, sems.at[2])] + [
        pltpu.make_async_copy(
            weight.at[pl.ds(0, both_vmem.shape[0]), pl.ds(own, half)],
            both_vmem.at[:, pl.ds(at * half, half)],
            sems.at[at],
        )
        for at, weight in enumerate((gate_hbm, up_hbm))
    ]
    for copy in copies:
        copy.start()
    for copy in copies:
        copy.wait()


def load_first(w_gate, w_up, gain, half, count):
    return pl.pallas_call(
        functools.partial(load_gain_kernel, half),
        out_shape=(
            pltpu.VMEM((count, 2 * half), w_gate.dtype),
            pltpu.VMEM(gain.shape, gain.dtype),
        ),
        in_specs=[HBM] * 3,
        out_specs=(VMEM, VMEM),
        scratch_shapes=[pltpu.SemaphoreType.DMA((3,))],
        compiler_params=pltpu.CompilerParams(vmem_limit_bytes=1 << 20),
        cost_estimate=pl.CostEstimate(
            flops=0, bytes_accessed=2 * count * half * 2, transcendentals=0
        ),
        name="load_first",
    )(w_gate, w_up, pltpu.with_memory_space_constraint(gain, pltpu.HBM))


def load_second_kernel(
    half,
    row,
    place,
    lengths,
    hit_lengths,
    start_positions,
    gate_hbm,
    up_hbm,
    both_vmem,
    mark_vmem,
    lengths_smem,
    hit_smem,
    start_smem,
    sems,
):
    own = pl.multiple_of(lax.axis_index("groups") * half, LANES)
    small = [
        pltpu.make_async_copy(source, target, sems.at[2 + at])
        for at, (source, target) in enumerate(
            ((lengths, lengths_smem), (hit_lengths, hit_smem), (start_positions, start_smem))
        )
    ]
    copies = [
        pltpu.make_async_copy(
            weight.at[pl.ds(row, both_vmem.shape[0]), pl.ds(own, half)],
            both_vmem.at[:, pl.ds(at * half, half)],
            sems.at[at],
        )
        for at, weight in enumerate((gate_hbm, up_hbm))
    ]
    for copy in small + copies:
        copy.start()
    for copy in small:
        copy.wait()
    live = live_flag(lengths_smem, hit_smem, start_smem, place())
    mark_vmem[...] = jnp.full(mark_vmem.shape, live.astype(jnp.float32), jnp.float32)
    for copy in copies:
        copy.wait()


def load_second(w_gate, w_up, half, row, count, requests, place):
    return pl.pallas_call(
        functools.partial(load_second_kernel, half, row, place),
        out_shape=(
            pltpu.VMEM((count, 2 * half), w_gate.dtype),
            jax.ShapeDtypeStruct((8, LANES), jnp.float32),
        ),
        in_specs=[HBM] * (2 + len(requests)),
        out_specs=(VMEM, VMEM),
        scratch_shapes=[pltpu.SMEM(array.shape, array.dtype) for array in requests]
        + [pltpu.SemaphoreType.DMA((5,))],
        compiler_params=pltpu.CompilerParams(vmem_limit_bytes=1 << 20),
        cost_estimate=pl.CostEstimate(
            flops=0, bytes_accessed=2 * count * half * 2, transcendentals=0
        ),
        name="load_second",
    )(*requests, w_gate, w_up)


def pack_kernel(*refs):
    pieces, gain_ref, out_ref, wide_ref = refs[:-4], refs[-4], refs[-2], refs[-1]
    rows = out_ref.shape[0]
    lines = out_ref.shape[1] // LANES
    stride = wide_ref.shape[0] // rows
    gain = gain_ref[...].astype(jnp.float32)
    row = 0
    for piece in pieces:
        values = piece[...].astype(jnp.float32)
        mean_sq = jnp.sum(values * values, axis=(1, 2), keepdims=True) * (1.0 / (lines * LANES))
        scaled = values * lax.rsqrt(mean_sq + 1e-05) * gain[None]
        for at in range(piece.shape[0]):
            wide_ref[row * stride : row * stride + lines] = scaled[at]
            row += 1
    for line in range(lines):
        out_ref[:, line * LANES : (line + 1) * LANES] = wide_ref[
            pl.ds(line, rows, stride=stride), :
        ].astype(jnp.bfloat16)


def pack(pieces, gain, mark):
    rows = sum(piece.shape[0] for piece in pieces)
    lines = pieces[0].shape[1]
    return pl.pallas_call(
        pack_kernel,
        out_shape=jax.ShapeDtypeStruct((rows, lines * LANES), jnp.bfloat16),
        in_specs=[VMEM] * (len(pieces) + 1) + [pl.BlockSpec(memory_space=pl.ANY)],
        out_specs=VMEM,
        scratch_shapes=[pltpu.VMEM((rows * (lines + 1), LANES), jnp.float32)],
        compiler_params=pltpu.CompilerParams(vmem_limit_bytes=4 << 20),
        name="pack",
    )(*pieces, pltpu.with_memory_space_constraint(gain, pltpu.VMEM), mark)


def block_kernel(
    half,
    chunk,
    deals,
    near_ref,
    far_ref,
    first_refs,
    gate_hbm,
    up_hbm,
    down_hbm,
    keep_ref,
    send_ref,
    wide_ref,
    rows_ref,
    product_ref,
    hidden_ref,
    rest_ref,
    down_ref,
    both_sems,
    down_sems,
):
    tile = 512
    rows, depth = rows_ref.shape
    lanes = LANES
    lines = depth // lanes
    stride = wide_ref.shape[0] // rows
    loaded = sum(ref.shape[0] for ref in first_refs)
    own = pl.multiple_of(lax.axis_index("groups") * half, LANES)
    loads = []
    at = 0
    for step, deal in enumerate(deals):
        loads.append(
            [
                pltpu.make_async_copy(
                    weight.at[pl.ds(loaded + at, deal), pl.ds(own, half)],
                    rest_ref.at[pl.ds(at, deal), pl.ds(side * half, half)],
                    both_sems.at[step, side],
                )
                for side, weight in enumerate((gate_hbm, up_hbm))
            ]
        )
        at += deal
    pairs = len(loads)
    for step, at in enumerate(range(0, depth, chunk)):
        loads.append(
            [
                pltpu.make_async_copy(
                    down_hbm.at[pl.ds(own, half), pl.ds(at, chunk)],
                    down_ref.at[:, pl.ds(at, chunk)],
                    down_sems.at[step],
                )
            ]
        )

    waiting = list(loads)

    def start():
        if waiting:
            for copy in waiting.pop(0):
                copy.start()

    def wait(number):
        for copy in loads[number]:
            copy.wait()

    def multiply(at, count, ref, row, halfway):
        for column in range(0, 2 * half, tile):
            columns = pl.ds(column, min(tile, 2 * half - column))
            value = jnp.dot(
                rows_ref[:, at : at + count],
                ref[row : row + count, columns],
                preferred_element_type=jnp.float32,
            )
            if at == 0:
                product_ref[:, columns] = value
            else:
                product_ref[:, columns] += value
            if halfway and column == tile:
                start()

    start()
    rows_ref[: rows // 2] = near_ref[...]
    rows_ref[rows // 2 :] = far_ref[...]
    at = 0
    for ref in first_refs:
        multiply(at, ref.shape[0], ref, 0, False)
        if at == 0:
            start()
        at += ref.shape[0]
    row = 0
    for step, deal in enumerate(deals):
        wait(step)
        multiply(at, deal, rest_ref, row, True)
        start()
        at += deal
        row += deal
    while waiting:
        start()
    gate_out = product_ref[:, :half]
    up_out = product_ref[:, half:]
    hidden_ref[...] = (gate_out / (1.0 + jnp.exp(-gate_out)) * up_out).astype(jnp.bfloat16)
    for step in range(depth // chunk):
        wait(pairs + step)
        for at in range(step * chunk, (step + 1) * chunk, tile):
            result = jnp.dot(
                hidden_ref[...], down_ref[:, pl.ds(at, tile)], preferred_element_type=jnp.float32
            )
            for line in range(tile // lanes):
                wide_ref[pl.ds(at // lanes + line, rows, stride=stride), :] = result[
                    :, line * lanes : (line + 1) * lanes
                ]
        done = step * chunk // lanes
        count = chunk // lanes
        for row in range(rows):
            ready = wide_ref[row * stride + done : row * stride + done + count]
            if row < rows // 2:
                keep_ref[row, done : done + count] = ready
            else:
                send_ref[row - rows // 2, done : done + count] = ready.astype(jnp.bfloat16)


def block(near, far, firsts, w_gate, w_up, w_down, half):
    rows, depth = near.shape
    lines = depth // LANES
    rest = depth - sum(first.shape[0] for first in firsts)
    deals = (rest * 3 // 7, rest - rest * 3 // 7)

    def body(near_ref, far_ref, *refs):
        count = len(firsts)
        block_kernel(half, 2 * CHUNK, deals, near_ref, far_ref, refs[:count], *refs[count:])

    return pl.pallas_call(
        body,
        out_shape=(
            jax.ShapeDtypeStruct((rows, lines, LANES), jnp.float32),
            jax.ShapeDtypeStruct((rows, lines, LANES), jnp.bfloat16),
        ),
        in_specs=[VMEM] * (2 + len(firsts)) + [HBM] * 3,
        out_specs=(VMEM, VMEM),
        scratch_shapes=[
            pltpu.VMEM((2 * rows * (lines + 1), LANES), jnp.float32),
            pltpu.VMEM((2 * rows, depth), jnp.bfloat16),
            pltpu.VMEM((2 * rows, 2 * half), jnp.float32),
            pltpu.VMEM((2 * rows, half), jnp.bfloat16),
            pltpu.VMEM((rest, 2 * half), jnp.bfloat16),
            pltpu.VMEM((half, depth), jnp.bfloat16),
            pltpu.SemaphoreType.DMA((2, 2)),
            pltpu.SemaphoreType.DMA((depth // (2 * CHUNK),)),
        ],
        compiler_params=pltpu.CompilerParams(
            vmem_limit_bytes=(rest * 2 + depth) * half * 2 + (6 << 20)
        ),
        cost_estimate=pl.CostEstimate(
            flops=12 * rows * depth * half,
            bytes_accessed=(rest * 2 + depth) * half * 2,
            transcendentals=0,
        ),
        name="block",
    )(
        near,
        far,
        *(pltpu.with_memory_space_constraint(first, pltpu.VMEM) for first in firsts),
        w_gate,
        w_up,
        w_down,
    )


def finish_kernel(*refs):
    pieces, live_ref, out_ref = refs[:-2], refs[-2], refs[-1]
    totals = pieces[0][...].astype(jnp.float32)
    for piece in pieces[1:]:
        totals = totals + piece[...].astype(jnp.float32)
    totals = jnp.where(live_ref[:1] > 0, totals[0], jnp.zeros_like(totals[0]))
    for line in range(totals.shape[0]):
        out_ref[:, line * LANES : (line + 1) * LANES] = totals[line : line + 1].astype(jnp.bfloat16)


def finish(pieces, live):
    lines = pieces[0].shape[1]
    return pl.pallas_call(
        finish_kernel,
        out_shape=jax.ShapeDtypeStruct((1, lines * LANES), jnp.bfloat16),
        in_specs=[VMEM] * (len(pieces) + 1),
        out_specs=VMEM,
        compiler_params=pltpu.CompilerParams(vmem_limit_bytes=1 << 20),
        name="finish",
    )(*pieces, live)


def swap(value, axes, offset):
    places = range(lax.axis_size(axes))
    return lax.ppermute(value, axes, [(place, place ^ offset) for place in places])


def shared(tokens, norm_gain, w_gate, w_up, w_down, lengths, hit_lengths, start_positions):
    square = ("groups", "x")
    half = w_gate.shape[1] // lax.axis_size("groups")
    w_gate, w_up, w_down = (
        pltpu.with_memory_space_constraint(array, pltpu.HBM) for array in (w_gate, w_up, w_down)
    )
    requests = tuple(
        pltpu.with_memory_space_constraint(array, pltpu.HBM)
        for array in (lengths, hit_lengths, start_positions)
    )

    def place():
        return (lax.axis_index("z") * lax.axis_size("x") + lax.axis_index("x")) * lax.axis_size(
            "core"
        ) + lax.axis_index("core")

    deep = lax.axis_size("z")
    others = range(1, lax.axis_size(square))
    rows = [0] + list(range(2, deep)) + [1]
    column = [swap(tokens, "z", at) if at else tokens for at in rows]
    first, gain = load_first(w_gate, w_up, norm_gain.reshape(-1, LANES), half, 2 * CHUNK)
    column = stack(rows, column, gain)
    plane = [column] + [swap(column, square, at) for at in others]
    second, live = load_second(w_gate, w_up, half, 2 * CHUNK, 5 * CHUNK // 2, requests, place)
    near = pack(plane, gain, live)
    far = swap(near, "core", 1)
    kept, sent = block(near, far, (first, second), w_gate, w_up, w_down, half)
    plane = (kept + swap(sent, "core", 1).astype(jnp.float32)).astype(jnp.bfloat16)
    pieces = jnp.split(plane, lax.axis_size(square), axis=0)
    column = pieces[0].astype(jnp.float32)
    for piece in [swap(pieces[at], square, at) for at in reversed(others)]:
        column = column + piece.astype(jnp.float32)
    pieces = jnp.split(column.astype(jnp.bfloat16), deep, axis=0)
    return finish(
        pieces[:1] + [swap(piece, "z", at + 1) for at, piece in enumerate(pieces[1:])], live
    )


def solution(mesh):
    groups, members = mesh.shape["groups"], mesh.shape["tensor"]

    def placed(axes, whole):
        return (
            P(whole, None),
            P(),
            P(None, axes),
            P(None, axes),
            P(axes, None),
            P("groups"),
            P("groups"),
            P("groups"),
        )

    def run(*arrays):
        units = arrays[2].shape[1] // members
        if (
            units % (LANES * groups) == 0
            and arrays[0].shape[0] == groups * members
            and groups == 2
            and members >= 8
            and members & (members - 1) == 0
        ):
            body, axes, whole = shared, ("z", "x", "core"), ROW_LINES
            over = jax.sharding.Mesh(mesh.devices.reshape(groups, members // 4, 2, 2), ROW_LINES)
        else:
            body, axes, whole, over = local, "tensor", ("groups", "tensor"), mesh
        return jax.shard_map(
            body,
            mesh=over,
            in_specs=placed(axes, whole),
            out_specs=P(whole, None),
            check_vma=False,
        )(*arrays)

    return run
```

```python
import functools

import jax
import jax.numpy as jnp
from jax import lax
from jax.experimental import pallas as pl
from jax.experimental.pallas import tpu as pltpu
from jax.sharding import PartitionSpec as P

LANES = 128
ROW_LINES = ("groups", "z", "x", "core")
LAYER = ("groups", "x", "z")


def normalize(tokens, norm_gain):
    values = tokens.astype(jnp.float32)
    mean_sq = jnp.mean(values * values, axis=-1, keepdims=True)
    return (values * lax.rsqrt(mean_sq + 1e-05) * norm_gain.astype(jnp.float32)).astype(
        jnp.bfloat16
    )


def live_rows(lengths, hit_lengths, start_positions, token_index):
    ends = jnp.cumsum(lengths)
    begins = ends - lengths
    member = (token_index[:, None] >= begins[None, :]) & (token_index[:, None] < ends[None, :])
    member_int = member.astype(jnp.int32)
    offsets = token_index - jnp.sum(member_int * begins[None, :], axis=1)
    position = jnp.sum(member_int * start_positions[None, :], axis=1) + offsets
    covered = jnp.sum(member_int * hit_lengths[None, :], axis=1)
    return position >= covered


def local(tokens, norm_gain, w_gate, w_up, w_down, lengths, hit_lengths, start_positions):
    row_count = tokens.shape[0]
    normed = normalize(tokens, norm_gain)
    piece_rows = lax.all_gather(normed, "tensor", axis=0, tiled=True)
    gate_out = jnp.dot(piece_rows, w_gate, preferred_element_type=jnp.float32)
    up_out = jnp.dot(piece_rows, w_up, preferred_element_type=jnp.float32)
    hidden = (jax.nn.silu(gate_out) * up_out).astype(jnp.bfloat16)
    partial_value = jnp.dot(hidden, w_down, preferred_element_type=jnp.float32)
    rounded = partial_value.astype(jnp.bfloat16)
    totals = jnp.sum(
        lax.all_to_all(rounded[None], "tensor", split_axis=1, concat_axis=0, tiled=True).astype(
            jnp.float32
        ),
        axis=0,
    )
    token_index = lax.axis_index("tensor") * row_count + jnp.arange(row_count, dtype=jnp.int32)
    live = live_rows(lengths, hit_lengths, start_positions, token_index)
    return jnp.where(live[:, None], totals, jnp.zeros_like(totals)).astype(jnp.bfloat16)


VMEM = pl.BlockSpec(memory_space=pltpu.VMEM)
HBM = pl.BlockSpec(memory_space=pltpu.HBM)
CHUNK = 1024


def live_flag(lengths, hit_lengths, start_positions, token):
    begin = 0
    live = False
    for request in range(lengths.shape[0]):
        end = begin + lengths[request]
        position = start_positions[request] + token - begin
        inside = (token >= begin) & (token < end)
        live = live | (inside & (position >= hit_lengths[request]))
        begin = end
    return live


def stack_kernel(rows, *refs):
    pieces, out_ref, wide_ref = refs[:-3], refs[-2], refs[-1]
    lines = out_ref.shape[1]
    for at, piece in zip(rows, pieces):
        values = piece[...].astype(jnp.float32)
        for line in range(lines):
            wide_ref[at, line : line + 1] = values[:, line * LANES : (line + 1) * LANES]
    out_ref[...] = wide_ref[...].astype(out_ref.dtype)


def stack(rows, pieces, gain):
    shape = (len(pieces), pieces[0].shape[1] // LANES, LANES)
    return pl.pallas_call(
        functools.partial(stack_kernel, rows),
        out_shape=jax.ShapeDtypeStruct(shape, pieces[0].dtype),
        in_specs=[VMEM] * len(pieces) + [pl.BlockSpec(memory_space=pl.ANY)],
        out_specs=VMEM,
        scratch_shapes=[pltpu.VMEM(shape, jnp.float32)],
        compiler_params=pltpu.CompilerParams(vmem_limit_bytes=2 << 20),
        name="stack",
    )(*pieces, gain)


def load_gain_kernel(half, gate_hbm, up_hbm, gain_hbm, both_vmem, gain_vmem, sems):
    own = pl.multiple_of(lax.axis_index("groups") * half, LANES)
    copies = [pltpu.make_async_copy(gain_hbm, gain_vmem, sems.at[2])] + [
        pltpu.make_async_copy(
            weight.at[pl.ds(0, both_vmem.shape[0]), pl.ds(own, half)],
            both_vmem.at[:, pl.ds(at * half, half)],
            sems.at[at],
        )
        for at, weight in enumerate((gate_hbm, up_hbm))
    ]
    for copy in copies:
        copy.start()
    for copy in copies:
        copy.wait()


def load_first(w_gate, w_up, gain, half, count):
    return pl.pallas_call(
        functools.partial(load_gain_kernel, half),
        out_shape=(
            pltpu.VMEM((count, 2 * half), w_gate.dtype),
            pltpu.VMEM(gain.shape, gain.dtype),
        ),
        in_specs=[HBM] * 3,
        out_specs=(VMEM, VMEM),
        scratch_shapes=[pltpu.SemaphoreType.DMA((3,))],
        compiler_params=pltpu.CompilerParams(vmem_limit_bytes=1 << 20),
        cost_estimate=pl.CostEstimate(
            flops=0, bytes_accessed=2 * count * half * 2, transcendentals=0
        ),
        name="load_first",
    )(w_gate, w_up, pltpu.with_memory_space_constraint(gain, pltpu.HBM))


def load_second_kernel(
    half,
    row,
    place,
    lengths,
    hit_lengths,
    start_positions,
    gate_hbm,
    up_hbm,
    both_vmem,
    mark_vmem,
    lengths_smem,
    hit_smem,
    start_smem,
    sems,
):
    own = pl.multiple_of(lax.axis_index("groups") * half, LANES)
    small = [
        pltpu.make_async_copy(source, target, sems.at[2 + at])
        for at, (source, target) in enumerate(
            ((lengths, lengths_smem), (hit_lengths, hit_smem), (start_positions, start_smem))
        )
    ]
    copies = [
        pltpu.make_async_copy(
            weight.at[pl.ds(row, both_vmem.shape[0]), pl.ds(own, half)],
            both_vmem.at[:, pl.ds(at * half, half)],
            sems.at[at],
        )
        for at, weight in enumerate((gate_hbm, up_hbm))
    ]
    for copy in small + copies:
        copy.start()
    for copy in small:
        copy.wait()
    live = live_flag(lengths_smem, hit_smem, start_smem, place())
    mark_vmem[...] = jnp.full(mark_vmem.shape, live.astype(jnp.float32), jnp.float32)
    for copy in copies:
        copy.wait()


def load_second(w_gate, w_up, half, row, count, requests, place):
    return pl.pallas_call(
        functools.partial(load_second_kernel, half, row, place),
        out_shape=(
            pltpu.VMEM((count, 2 * half), w_gate.dtype),
            jax.ShapeDtypeStruct((8, LANES), jnp.float32),
        ),
        in_specs=[HBM] * (2 + len(requests)),
        out_specs=(VMEM, VMEM),
        scratch_shapes=[pltpu.SMEM(array.shape, array.dtype) for array in requests]
        + [pltpu.SemaphoreType.DMA((5,))],
        compiler_params=pltpu.CompilerParams(vmem_limit_bytes=1 << 20),
        cost_estimate=pl.CostEstimate(
            flops=0, bytes_accessed=2 * count * half * 2, transcendentals=0
        ),
        name="load_second",
    )(*requests, w_gate, w_up)


def pack_kernel(*refs):
    pieces, gain_ref, out_ref, wide_ref = refs[:-4], refs[-4], refs[-2], refs[-1]
    rows = out_ref.shape[0]
    lines = out_ref.shape[1] // LANES
    stride = wide_ref.shape[0] // rows
    gain = gain_ref[...].astype(jnp.float32)
    row = 0
    for piece in pieces:
        values = piece[...].astype(jnp.float32)
        mean_sq = jnp.sum(values * values, axis=(1, 2), keepdims=True) * (1.0 / (lines * LANES))
        scaled = values * lax.rsqrt(mean_sq + 1e-05) * gain[None]
        for at in range(piece.shape[0]):
            wide_ref[row * stride : row * stride + lines] = scaled[at]
            row += 1
    for line in range(lines):
        out_ref[:, line * LANES : (line + 1) * LANES] = wide_ref[
            pl.ds(line, rows, stride=stride), :
        ].astype(jnp.bfloat16)


def pack(pieces, gain, mark):
    rows = sum(piece.shape[0] for piece in pieces)
    lines = pieces[0].shape[1]
    return pl.pallas_call(
        pack_kernel,
        out_shape=jax.ShapeDtypeStruct((rows, lines * LANES), jnp.bfloat16),
        in_specs=[VMEM] * (len(pieces) + 1) + [pl.BlockSpec(memory_space=pl.ANY)],
        out_specs=VMEM,
        scratch_shapes=[pltpu.VMEM((rows * (lines + 1), LANES), jnp.float32)],
        compiler_params=pltpu.CompilerParams(vmem_limit_bytes=4 << 20),
        name="pack",
    )(*pieces, pltpu.with_memory_space_constraint(gain, pltpu.VMEM), mark)


def block_kernel(
    half,
    chunk,
    deals,
    near_ref,
    far_ref,
    first_refs,
    gate_hbm,
    up_hbm,
    down_hbm,
    keep_ref,
    send_ref,
    wide_ref,
    rows_ref,
    product_ref,
    hidden_ref,
    rest_ref,
    down_ref,
    both_sems,
    down_sems,
):
    tile = 512
    rows, depth = rows_ref.shape
    lanes = LANES
    lines = depth // lanes
    stride = wide_ref.shape[0] // rows
    loaded = sum(ref.shape[0] for ref in first_refs)
    own = pl.multiple_of(lax.axis_index("groups") * half, LANES)
    loads = []
    at = 0
    for step, deal in enumerate(deals):
        loads.append(
            [
                pltpu.make_async_copy(
                    weight.at[pl.ds(loaded + at, deal), pl.ds(own, half)],
                    rest_ref.at[pl.ds(at, deal), pl.ds(side * half, half)],
                    both_sems.at[step, side],
                )
                for side, weight in enumerate((gate_hbm, up_hbm))
            ]
        )
        at += deal
    pairs = len(loads)
    for step, at in enumerate(range(0, depth, chunk)):
        loads.append(
            [
                pltpu.make_async_copy(
                    down_hbm.at[pl.ds(own, half), pl.ds(at, chunk)],
                    down_ref.at[:, pl.ds(at, chunk)],
                    down_sems.at[step],
                )
            ]
        )

    waiting = list(loads)

    def start():
        if waiting:
            for copy in waiting.pop(0):
                copy.start()

    def wait(number):
        for copy in loads[number]:
            copy.wait()

    def multiply(at, count, ref, row, halfway):
        for column in range(0, 2 * half, tile):
            columns = pl.ds(column, min(tile, 2 * half - column))
            value = jnp.dot(
                rows_ref[:, at : at + count],
                ref[row : row + count, columns],
                preferred_element_type=jnp.float32,
            )
            if at == 0:
                product_ref[:, columns] = value
            else:
                product_ref[:, columns] += value
            if halfway and column == tile:
                start()

    start()
    rows_ref[: rows // 2] = near_ref[...]
    rows_ref[rows // 2 :] = far_ref[...]
    at = 0
    for ref in first_refs:
        multiply(at, ref.shape[0], ref, 0, False)
        if at == 0:
            start()
        at += ref.shape[0]
    row = 0
    for step, deal in enumerate(deals):
        wait(step)
        multiply(at, deal, rest_ref, row, True)
        start()
        at += deal
        row += deal
    while waiting:
        start()
    gate_out = product_ref[:, :half]
    up_out = product_ref[:, half:]
    hidden_ref[...] = (gate_out / (1.0 + jnp.exp(-gate_out)) * up_out).astype(jnp.bfloat16)
    place = lax.axis_index(LAYER)
    for step in range(depth // chunk):
        wait(pairs + step)
        for at in range(step * chunk, (step + 1) * chunk, tile):
            result = jnp.dot(
                hidden_ref[...], down_ref[:, pl.ds(at, tile)], preferred_element_type=jnp.float32
            )
            for line in range(tile // lanes):
                wide_ref[pl.ds(at // lanes + line, rows, stride=stride), :] = result[
                    :, line * lanes : (line + 1) * lanes
                ]
        done = step * chunk // lanes
        count = chunk // lanes
        for row in range(rows // 2):
            owner = lax.bitwise_xor(place, row)
            keep_ref[owner, done : done + count] = wide_ref[
                row * stride + done : row * stride + done + count
            ]
            at = (row + rows // 2) * stride + done
            send_ref[owner, done : done + count] = wide_ref[at : at + count].astype(jnp.bfloat16)


def block(near, far, firsts, w_gate, w_up, w_down, half):
    rows, depth = near.shape
    lines = depth // LANES
    rest = depth - sum(first.shape[0] for first in firsts)
    deals = (rest * 3 // 7, rest - rest * 3 // 7)

    def body(near_ref, far_ref, *refs):
        count = len(firsts)
        block_kernel(half, 2 * CHUNK, deals, near_ref, far_ref, refs[:count], *refs[count:])

    return pl.pallas_call(
        body,
        out_shape=(
            jax.ShapeDtypeStruct((rows, lines, LANES), jnp.float32),
            jax.ShapeDtypeStruct((rows, lines, LANES), jnp.bfloat16),
        ),
        in_specs=[VMEM] * (2 + len(firsts)) + [HBM] * 3,
        out_specs=(VMEM, VMEM),
        scratch_shapes=[
            pltpu.VMEM((2 * rows * (lines + 1), LANES), jnp.float32),
            pltpu.VMEM((2 * rows, depth), jnp.bfloat16),
            pltpu.VMEM((2 * rows, 2 * half), jnp.float32),
            pltpu.VMEM((2 * rows, half), jnp.bfloat16),
            pltpu.VMEM((rest, 2 * half), jnp.bfloat16),
            pltpu.VMEM((half, depth), jnp.bfloat16),
            pltpu.SemaphoreType.DMA((2, 2)),
            pltpu.SemaphoreType.DMA((depth // (2 * CHUNK),)),
        ],
        compiler_params=pltpu.CompilerParams(
            vmem_limit_bytes=(rest * 2 + depth) * half * 2 + (6 << 20)
        ),
        cost_estimate=pl.CostEstimate(
            flops=12 * rows * depth * half,
            bytes_accessed=(rest * 2 + depth) * half * 2,
            transcendentals=0,
        ),
        name="block",
    )(
        near,
        far,
        *(pltpu.with_memory_space_constraint(first, pltpu.VMEM) for first in firsts),
        w_gate,
        w_up,
        w_down,
    )


def finish_kernel(pieces_ref, live_ref, out_ref):
    totals = jnp.sum(pieces_ref[...].astype(jnp.float32), axis=0)
    totals = jnp.where(live_ref[:1] > 0, totals, jnp.zeros_like(totals))
    for line in range(totals.shape[0]):
        out_ref[:, line * LANES : (line + 1) * LANES] = totals[line : line + 1].astype(jnp.bfloat16)


def finish(pieces, live):
    return pl.pallas_call(
        finish_kernel,
        out_shape=jax.ShapeDtypeStruct((1, pieces.shape[1] * LANES), jnp.bfloat16),
        in_specs=[VMEM] * 2,
        out_specs=VMEM,
        compiler_params=pltpu.CompilerParams(vmem_limit_bytes=4 << 20),
        name="finish",
    )(pieces, live)


def swap(value, axes, offset):
    places = range(lax.axis_size(axes))
    return lax.ppermute(value, axes, [(place, place ^ offset) for place in places])


def shared(tokens, norm_gain, w_gate, w_up, w_down, lengths, hit_lengths, start_positions):
    square = ("groups", "x")
    half = w_gate.shape[1] // lax.axis_size("groups")
    w_gate, w_up, w_down = (
        pltpu.with_memory_space_constraint(array, pltpu.HBM) for array in (w_gate, w_up, w_down)
    )
    requests = tuple(
        pltpu.with_memory_space_constraint(array, pltpu.HBM)
        for array in (lengths, hit_lengths, start_positions)
    )

    def place():
        return (lax.axis_index("z") * lax.axis_size("x") + lax.axis_index("x")) * lax.axis_size(
            "core"
        ) + lax.axis_index("core")

    deep = lax.axis_size("z")
    others = range(1, lax.axis_size(square))
    rows = [0] + list(range(2, deep)) + [1]
    column = [swap(tokens, "z", at) if at else tokens for at in rows]
    first, gain = load_first(w_gate, w_up, norm_gain.reshape(-1, LANES), half, 2 * CHUNK)
    column = stack(rows, column, gain)
    plane = [column] + [swap(column, square, at) for at in others]
    second, live = load_second(w_gate, w_up, half, 2 * CHUNK, 5 * CHUNK // 2, requests, place)
    near = pack(plane, gain, live)
    far = swap(near, "core", 1)
    kept, sent = block(near, far, (first, second), w_gate, w_up, w_down, half)
    plane = (kept + swap(sent, "core", 1).astype(jnp.float32)).astype(jnp.bfloat16)
    return finish(lax.all_to_all(plane, LAYER, split_axis=0, concat_axis=0, tiled=True), live)


def solution(mesh):
    groups, members = mesh.shape["groups"], mesh.shape["tensor"]

    def placed(axes, whole):
        return (
            P(whole, None),
            P(),
            P(None, axes),
            P(None, axes),
            P(axes, None),
            P("groups"),
            P("groups"),
            P("groups"),
        )

    def run(*arrays):
        units = arrays[2].shape[1] // members
        if (
            units % (LANES * groups) == 0
            and arrays[0].shape[0] == groups * members
            and groups == 2
            and members >= 8
            and members & (members - 1) == 0
        ):
            body, axes, whole = shared, ("z", "x", "core"), ROW_LINES
            over = jax.sharding.Mesh(mesh.devices.reshape(groups, members // 4, 2, 2), ROW_LINES)
        else:
            body, axes, whole, over = local, "tensor", ("groups", "tensor"), mesh
        return jax.shard_map(
            body,
            mesh=over,
            in_specs=placed(axes, whole),
            out_specs=P(whole, None),
            check_vma=False,
        )(*arrays)

    return run
```

```python
import functools

import jax
import jax.numpy as jnp
from jax import lax
from jax.experimental import pallas as pl
from jax.experimental.pallas import tpu as pltpu
from jax.sharding import PartitionSpec as P

LANES = 128
ROW_LINES = ("groups", "z", "x", "core")


def normalize(tokens, norm_gain):
    values = tokens.astype(jnp.float32)
    mean_sq = jnp.mean(values * values, axis=-1, keepdims=True)
    return (values * lax.rsqrt(mean_sq + 1e-05) * norm_gain.astype(jnp.float32)).astype(
        jnp.bfloat16
    )


def live_rows(lengths, hit_lengths, start_positions, token_index):
    ends = jnp.cumsum(lengths)
    begins = ends - lengths
    member = (token_index[:, None] >= begins[None, :]) & (token_index[:, None] < ends[None, :])
    member_int = member.astype(jnp.int32)
    offsets = token_index - jnp.sum(member_int * begins[None, :], axis=1)
    position = jnp.sum(member_int * start_positions[None, :], axis=1) + offsets
    covered = jnp.sum(member_int * hit_lengths[None, :], axis=1)
    return position >= covered


def local(tokens, norm_gain, w_gate, w_up, w_down, lengths, hit_lengths, start_positions):
    row_count = tokens.shape[0]
    normed = normalize(tokens, norm_gain)
    piece_rows = lax.all_gather(normed, "tensor", axis=0, tiled=True)
    gate_out = jnp.dot(piece_rows, w_gate, preferred_element_type=jnp.float32)
    up_out = jnp.dot(piece_rows, w_up, preferred_element_type=jnp.float32)
    hidden = (jax.nn.silu(gate_out) * up_out).astype(jnp.bfloat16)
    partial_value = jnp.dot(hidden, w_down, preferred_element_type=jnp.float32)
    rounded = partial_value.astype(jnp.bfloat16)
    totals = jnp.sum(
        lax.all_to_all(rounded[None], "tensor", split_axis=1, concat_axis=0, tiled=True).astype(
            jnp.float32
        ),
        axis=0,
    )
    token_index = lax.axis_index("tensor") * row_count + jnp.arange(row_count, dtype=jnp.int32)
    live = live_rows(lengths, hit_lengths, start_positions, token_index)
    return jnp.where(live[:, None], totals, jnp.zeros_like(totals)).astype(jnp.bfloat16)


VMEM = pl.BlockSpec(memory_space=pltpu.VMEM)
HBM = pl.BlockSpec(memory_space=pltpu.HBM)
CHUNK = 1024


def live_flag(lengths, hit_lengths, start_positions, token):
    begin = 0
    live = False
    for request in range(lengths.shape[0]):
        end = begin + lengths[request]
        position = start_positions[request] + token - begin
        inside = (token >= begin) & (token < end)
        live = live | (inside & (position >= hit_lengths[request]))
        begin = end
    return live


def stack_kernel(rows, *refs):
    pieces, out_ref, wide_ref = refs[:-3], refs[-2], refs[-1]
    lines = out_ref.shape[1]
    for at, piece in zip(rows, pieces):
        values = piece[...].astype(jnp.float32)
        for line in range(lines):
            wide_ref[at, line : line + 1] = values[:, line * LANES : (line + 1) * LANES]
    out_ref[...] = wide_ref[...].astype(out_ref.dtype)


def stack(rows, pieces, gain):
    shape = (len(pieces), pieces[0].shape[1] // LANES, LANES)
    return pl.pallas_call(
        functools.partial(stack_kernel, rows),
        out_shape=jax.ShapeDtypeStruct(shape, pieces[0].dtype),
        in_specs=[VMEM] * len(pieces) + [pl.BlockSpec(memory_space=pl.ANY)],
        out_specs=VMEM,
        scratch_shapes=[pltpu.VMEM(shape, jnp.float32)],
        compiler_params=pltpu.CompilerParams(vmem_limit_bytes=2 << 20),
        name="stack",
    )(*pieces, gain)


def load_gain_kernel(half, gate_hbm, up_hbm, gain_hbm, both_vmem, gain_vmem, sems):
    own = pl.multiple_of(lax.axis_index("groups") * half, LANES)
    copies = [pltpu.make_async_copy(gain_hbm, gain_vmem, sems.at[2])] + [
        pltpu.make_async_copy(
            weight.at[pl.ds(0, both_vmem.shape[0]), pl.ds(own, half)],
            both_vmem.at[:, pl.ds(at * half, half)],
            sems.at[at],
        )
        for at, weight in enumerate((gate_hbm, up_hbm))
    ]
    for copy in copies:
        copy.start()
    for copy in copies:
        copy.wait()


def load_first(w_gate, w_up, gain, half, count):
    return pl.pallas_call(
        functools.partial(load_gain_kernel, half),
        out_shape=(
            pltpu.VMEM((count, 2 * half), w_gate.dtype),
            pltpu.VMEM(gain.shape, gain.dtype),
        ),
        in_specs=[HBM] * 3,
        out_specs=(VMEM, VMEM),
        scratch_shapes=[pltpu.SemaphoreType.DMA((3,))],
        compiler_params=pltpu.CompilerParams(vmem_limit_bytes=1 << 20),
        cost_estimate=pl.CostEstimate(
            flops=0, bytes_accessed=2 * count * half * 2, transcendentals=0
        ),
        name="load_first",
    )(w_gate, w_up, pltpu.with_memory_space_constraint(gain, pltpu.HBM))


def load_second_kernel(
    half,
    row,
    place,
    lengths,
    hit_lengths,
    start_positions,
    gate_hbm,
    up_hbm,
    both_vmem,
    mark_vmem,
    lengths_smem,
    hit_smem,
    start_smem,
    sems,
):
    own = pl.multiple_of(lax.axis_index("groups") * half, LANES)
    small = [
        pltpu.make_async_copy(source, target, sems.at[2 + at])
        for at, (source, target) in enumerate(
            ((lengths, lengths_smem), (hit_lengths, hit_smem), (start_positions, start_smem))
        )
    ]
    copies = [
        pltpu.make_async_copy(
            weight.at[pl.ds(row, both_vmem.shape[0]), pl.ds(own, half)],
            both_vmem.at[:, pl.ds(at * half, half)],
            sems.at[at],
        )
        for at, weight in enumerate((gate_hbm, up_hbm))
    ]
    for copy in small + copies:
        copy.start()
    for copy in small:
        copy.wait()
    live = live_flag(lengths_smem, hit_smem, start_smem, place())
    mark_vmem[...] = jnp.full(mark_vmem.shape, live.astype(jnp.float32), jnp.float32)
    for copy in copies:
        copy.wait()


def load_second(w_gate, w_up, half, row, count, requests, place):
    return pl.pallas_call(
        functools.partial(load_second_kernel, half, row, place),
        out_shape=(
            pltpu.VMEM((count, 2 * half), w_gate.dtype),
            jax.ShapeDtypeStruct((8, LANES), jnp.float32),
        ),
        in_specs=[HBM] * (2 + len(requests)),
        out_specs=(VMEM, VMEM),
        scratch_shapes=[pltpu.SMEM(array.shape, array.dtype) for array in requests]
        + [pltpu.SemaphoreType.DMA((5,))],
        compiler_params=pltpu.CompilerParams(vmem_limit_bytes=1 << 20),
        cost_estimate=pl.CostEstimate(
            flops=0, bytes_accessed=2 * count * half * 2, transcendentals=0
        ),
        name="load_second",
    )(*requests, w_gate, w_up)


def load_third_kernel(half, row, gate_hbm, up_hbm, near_ref, both_vmem, sems):
    own = pl.multiple_of(lax.axis_index("groups") * half, LANES)
    copies = [
        pltpu.make_async_copy(
            weight.at[pl.ds(row, both_vmem.shape[0]), pl.ds(own, half)],
            both_vmem.at[:, pl.ds(at * half, half)],
            sems.at[at],
        )
        for at, weight in enumerate((gate_hbm, up_hbm))
    ]
    for copy in copies:
        copy.start()
    for copy in copies:
        copy.wait()


def load_third(w_gate, w_up, near, half, row, count):
    return pl.pallas_call(
        functools.partial(load_third_kernel, half, row),
        out_shape=pltpu.VMEM((count, 2 * half), w_gate.dtype),
        in_specs=[HBM] * 2 + [pl.BlockSpec(memory_space=pl.ANY)],
        out_specs=VMEM,
        scratch_shapes=[pltpu.SemaphoreType.DMA((2,))],
        compiler_params=pltpu.CompilerParams(vmem_limit_bytes=1 << 20),
        cost_estimate=pl.CostEstimate(
            flops=0, bytes_accessed=2 * count * half * 2, transcendentals=0
        ),
        name="load_third",
    )(w_gate, w_up, near)


def pack_kernel(*refs):
    pieces, gain_ref, out_ref, wide_ref = refs[:-4], refs[-4], refs[-2], refs[-1]
    rows = out_ref.shape[0]
    lines = out_ref.shape[1] // LANES
    stride = wide_ref.shape[0] // rows
    gain = gain_ref[...].astype(jnp.float32)
    row = 0
    for piece in pieces:
        values = piece[...].astype(jnp.float32)
        mean_sq = jnp.sum(values * values, axis=(1, 2), keepdims=True) * (1.0 / (lines * LANES))
        scaled = values * lax.rsqrt(mean_sq + 1e-05) * gain[None]
        for at in range(piece.shape[0]):
            wide_ref[row * stride : row * stride + lines] = scaled[at]
            row += 1
    for line in range(lines):
        out_ref[:, line * LANES : (line + 1) * LANES] = wide_ref[
            pl.ds(line, rows, stride=stride), :
        ].astype(jnp.bfloat16)


def pack(pieces, gain, mark):
    rows = sum(piece.shape[0] for piece in pieces)
    lines = pieces[0].shape[1]
    return pl.pallas_call(
        pack_kernel,
        out_shape=jax.ShapeDtypeStruct((rows, lines * LANES), jnp.bfloat16),
        in_specs=[VMEM] * (len(pieces) + 1) + [pl.BlockSpec(memory_space=pl.ANY)],
        out_specs=VMEM,
        scratch_shapes=[pltpu.VMEM((rows * (lines + 1), LANES), jnp.float32)],
        compiler_params=pltpu.CompilerParams(vmem_limit_bytes=4 << 20),
        name="pack",
    )(*pieces, pltpu.with_memory_space_constraint(gain, pltpu.VMEM), mark)


def block_kernel(
    half,
    chunk,
    deals,
    near_ref,
    far_ref,
    first_refs,
    gate_hbm,
    up_hbm,
    down_hbm,
    keep_ref,
    send_ref,
    wide_ref,
    rows_ref,
    product_ref,
    hidden_ref,
    rest_ref,
    down_ref,
    both_sems,
    down_sems,
):
    tile = 512
    rows, depth = rows_ref.shape
    lanes = LANES
    lines = depth // lanes
    stride = wide_ref.shape[0] // rows
    loaded = sum(ref.shape[0] for ref in first_refs)
    own = pl.multiple_of(lax.axis_index("groups") * half, LANES)
    loads = []
    at = 0
    for step, deal in enumerate(deals):
        loads.append(
            [
                pltpu.make_async_copy(
                    weight.at[pl.ds(loaded + at, deal), pl.ds(own, half)],
                    rest_ref.at[pl.ds(at, deal), pl.ds(side * half, half)],
                    both_sems.at[step, side],
                )
                for side, weight in enumerate((gate_hbm, up_hbm))
            ]
        )
        at += deal
    pairs = len(loads)
    for step, at in enumerate(range(0, depth, chunk)):
        loads.append(
            [
                pltpu.make_async_copy(
                    down_hbm.at[pl.ds(own, half), pl.ds(at, chunk)],
                    down_ref.at[:, pl.ds(at, chunk)],
                    down_sems.at[step],
                )
            ]
        )

    waiting = list(loads)

    def start():
        if waiting:
            for copy in waiting.pop(0):
                copy.start()

    def wait(number):
        for copy in loads[number]:
            copy.wait()

    def multiply(at, count, ref, row, halfway):
        for column in range(0, 2 * half, tile):
            columns = pl.ds(column, min(tile, 2 * half - column))
            value = jnp.dot(
                rows_ref[:, at : at + count],
                ref[row : row + count, columns],
                preferred_element_type=jnp.float32,
            )
            if at == 0:
                product_ref[:, columns] = value
            else:
                product_ref[:, columns] += value
            if halfway and column == tile:
                start()

    start()
    rows_ref[: rows // 2] = near_ref[...]
    rows_ref[rows // 2 :] = far_ref[...]
    at = 0
    for ref in first_refs:
        multiply(at, ref.shape[0], ref, 0, False)
        if at == 0:
            start()
        at += ref.shape[0]
    row = 0
    for step, deal in enumerate(deals):
        wait(step)
        multiply(at, deal, rest_ref, row, True)
        start()
        at += deal
        row += deal
    while waiting:
        start()
    gate_out = product_ref[:, :half]
    up_out = product_ref[:, half:]
    hidden_ref[...] = (gate_out / (1.0 + jnp.exp(-gate_out)) * up_out).astype(jnp.bfloat16)
    zero = jnp.minimum(lax.axis_index("core"), 0)
    for step in range(depth // chunk):
        wait(pairs + step)
        for at in range(step * chunk, (step + 1) * chunk, tile):
            result = jnp.dot(
                hidden_ref[...], down_ref[:, pl.ds(at, tile)], preferred_element_type=jnp.float32
            )
            for line in range(tile // lanes):
                wide_ref[pl.ds(at // lanes + line, rows, stride=stride), :] = result[
                    :, line * lanes : (line + 1) * lanes
                ]
        done = step * chunk // lanes
        count = chunk // lanes
        for row in range(rows // 2):
            keep_ref[row + zero, done : done + count] = wide_ref[
                row * stride + done : row * stride + done + count
            ]
            at = (row + rows // 2) * stride + done
            send_ref[row + zero, done : done + count] = wide_ref[at : at + count].astype(
                jnp.bfloat16
            )


def block(near, far, firsts, w_gate, w_up, w_down, half):
    rows, depth = near.shape
    lines = depth // LANES
    rest = depth - sum(first.shape[0] for first in firsts)
    early = rest * 3 // 7 // 256 * 256
    deals = (early, rest - early)

    def body(near_ref, far_ref, *refs):
        count = len(firsts)
        block_kernel(half, 2 * CHUNK, deals, near_ref, far_ref, refs[:count], *refs[count:])

    return pl.pallas_call(
        body,
        out_shape=(
            jax.ShapeDtypeStruct((rows, lines, LANES), jnp.float32),
            jax.ShapeDtypeStruct((rows, lines, LANES), jnp.bfloat16),
        ),
        in_specs=[VMEM] * (2 + len(firsts)) + [HBM] * 3,
        out_specs=(VMEM, VMEM),
        scratch_shapes=[
            pltpu.VMEM((2 * rows * (lines + 1), LANES), jnp.float32),
            pltpu.VMEM((2 * rows, depth), jnp.bfloat16),
            pltpu.VMEM((2 * rows, 2 * half), jnp.float32),
            pltpu.VMEM((2 * rows, half), jnp.bfloat16),
            pltpu.VMEM((rest, 2 * half), jnp.bfloat16),
            pltpu.VMEM((half, depth), jnp.bfloat16),
            pltpu.SemaphoreType.DMA((2, 2)),
            pltpu.SemaphoreType.DMA((depth // (2 * CHUNK),)),
        ],
        compiler_params=pltpu.CompilerParams(
            vmem_limit_bytes=(rest * 2 + depth) * half * 2 + (6 << 20)
        ),
        cost_estimate=pl.CostEstimate(
            flops=12 * rows * depth * half,
            bytes_accessed=(rest * 2 + depth) * half * 2,
            transcendentals=0,
        ),
        name="block",
    )(
        near,
        far,
        *(pltpu.with_memory_space_constraint(first, pltpu.VMEM) for first in firsts),
        w_gate,
        w_up,
        w_down,
    )


def finish_kernel(*refs):
    pieces, live_ref, out_ref = refs[:-2], refs[-2], refs[-1]
    totals = pieces[0][...].astype(jnp.float32)
    for piece in pieces[1:]:
        totals = totals + piece[...].astype(jnp.float32)
    totals = jnp.where(live_ref[:1] > 0, totals[0], jnp.zeros_like(totals[0]))
    for line in range(totals.shape[0]):
        out_ref[:, line * LANES : (line + 1) * LANES] = totals[line : line + 1].astype(jnp.bfloat16)


def finish(pieces, live):
    lines = pieces[0].shape[1]
    return pl.pallas_call(
        finish_kernel,
        out_shape=jax.ShapeDtypeStruct((1, lines * LANES), jnp.bfloat16),
        in_specs=[VMEM] * (len(pieces) + 1),
        out_specs=VMEM,
        compiler_params=pltpu.CompilerParams(vmem_limit_bytes=1 << 20),
        name="finish",
    )(*pieces, live)


def swap(value, axes, offset):
    places = range(lax.axis_size(axes))
    return lax.ppermute(value, axes, [(place, place ^ offset) for place in places])


def shared(tokens, norm_gain, w_gate, w_up, w_down, lengths, hit_lengths, start_positions):
    square = ("groups", "x")
    half = w_gate.shape[1] // lax.axis_size("groups")
    w_gate, w_up, w_down = (
        pltpu.with_memory_space_constraint(array, pltpu.HBM) for array in (w_gate, w_up, w_down)
    )
    requests = tuple(
        pltpu.with_memory_space_constraint(array, pltpu.HBM)
        for array in (lengths, hit_lengths, start_positions)
    )

    def place():
        return (lax.axis_index("z") * lax.axis_size("x") + lax.axis_index("x")) * lax.axis_size(
            "core"
        ) + lax.axis_index("core")

    deep = lax.axis_size("z")
    others = range(1, lax.axis_size(square))
    rows = [0] + list(range(2, deep)) + [1]
    column = [swap(tokens, "z", at) if at else tokens for at in rows]
    first, gain = load_first(w_gate, w_up, norm_gain.reshape(-1, LANES), half, 2 * CHUNK)
    column = stack(rows, column, gain)
    plane = [column] + [swap(column, square, at) for at in others]
    second, live = load_second(w_gate, w_up, half, 2 * CHUNK, 5 * CHUNK // 2, requests, place)
    near = pack(plane, gain, live)
    far = swap(near, "core", 1)
    third = load_third(w_gate, w_up, near, half, 9 * CHUNK // 2, CHUNK // 2)
    kept, sent = block(near, far, (first, second, third), w_gate, w_up, w_down, half)
    plane = (kept + swap(sent, "core", 1).astype(jnp.float32)).astype(jnp.bfloat16)
    pieces = jnp.split(plane, lax.axis_size(square), axis=0)
    column = pieces[0].astype(jnp.float32)
    for piece in [swap(pieces[at], square, at) for at in reversed(others)]:
        column = column + piece.astype(jnp.float32)
    pieces = jnp.split(column.astype(jnp.bfloat16), deep, axis=0)
    return finish(
        pieces[:1] + [swap(piece, "z", at + 1) for at, piece in enumerate(pieces[1:])], live
    )


def solution(mesh):
    groups, members = mesh.shape["groups"], mesh.shape["tensor"]

    def placed(axes, whole):
        return (
            P(whole, None),
            P(),
            P(None, axes),
            P(None, axes),
            P(axes, None),
            P("groups"),
            P("groups"),
            P("groups"),
        )

    def run(*arrays):
        units = arrays[2].shape[1] // members
        if (
            units % (LANES * groups) == 0
            and arrays[0].shape[0] == groups * members
            and groups == 2
            and members >= 8
            and members & (members - 1) == 0
        ):
            body, axes, whole = shared, ("z", "x", "core"), ROW_LINES
            over = jax.sharding.Mesh(mesh.devices.reshape(groups, members // 4, 2, 2), ROW_LINES)
        else:
            body, axes, whole, over = local, "tensor", ("groups", "tensor"), mesh
        return jax.shard_map(
            body,
            mesh=over,
            in_specs=placed(axes, whole),
            out_specs=P(whole, None),
            check_vma=False,
        )(*arrays)

    return run
```

```python
import functools

import jax
import jax.numpy as jnp
from jax import lax
from jax.experimental import pallas as pl
from jax.experimental.pallas import tpu as pltpu
from jax.sharding import PartitionSpec as P

LANES = 128
ROW_LINES = ("groups", "z", "x", "core")


def normalize(tokens, norm_gain):
    values = tokens.astype(jnp.float32)
    mean_sq = jnp.mean(values * values, axis=-1, keepdims=True)
    return (values * lax.rsqrt(mean_sq + 1e-05) * norm_gain.astype(jnp.float32)).astype(
        jnp.bfloat16
    )


def live_rows(lengths, hit_lengths, start_positions, token_index):
    ends = jnp.cumsum(lengths)
    begins = ends - lengths
    member = (token_index[:, None] >= begins[None, :]) & (token_index[:, None] < ends[None, :])
    member_int = member.astype(jnp.int32)
    offsets = token_index - jnp.sum(member_int * begins[None, :], axis=1)
    position = jnp.sum(member_int * start_positions[None, :], axis=1) + offsets
    covered = jnp.sum(member_int * hit_lengths[None, :], axis=1)
    return position >= covered


def local(tokens, norm_gain, w_gate, w_up, w_down, lengths, hit_lengths, start_positions):
    row_count = tokens.shape[0]
    normed = normalize(tokens, norm_gain)
    piece_rows = lax.all_gather(normed, "tensor", axis=0, tiled=True)
    gate_out = jnp.dot(piece_rows, w_gate, preferred_element_type=jnp.float32)
    up_out = jnp.dot(piece_rows, w_up, preferred_element_type=jnp.float32)
    hidden = (jax.nn.silu(gate_out) * up_out).astype(jnp.bfloat16)
    partial_value = jnp.dot(hidden, w_down, preferred_element_type=jnp.float32)
    rounded = partial_value.astype(jnp.bfloat16)
    totals = jnp.sum(
        lax.all_to_all(rounded[None], "tensor", split_axis=1, concat_axis=0, tiled=True).astype(
            jnp.float32
        ),
        axis=0,
    )
    token_index = lax.axis_index("tensor") * row_count + jnp.arange(row_count, dtype=jnp.int32)
    live = live_rows(lengths, hit_lengths, start_positions, token_index)
    return jnp.where(live[:, None], totals, jnp.zeros_like(totals)).astype(jnp.bfloat16)


VMEM = pl.BlockSpec(memory_space=pltpu.VMEM)
HBM = pl.BlockSpec(memory_space=pltpu.HBM)
CHUNK = 1024


def live_flag(lengths, hit_lengths, start_positions, token):
    begin = 0
    live = False
    for request in range(lengths.shape[0]):
        end = begin + lengths[request]
        position = start_positions[request] + token - begin
        inside = (token >= begin) & (token < end)
        live = live | (inside & (position >= hit_lengths[request]))
        begin = end
    return live


def stack_kernel(rows, *refs):
    pieces, out_ref, wide_ref = refs[:-3], refs[-2], refs[-1]
    lines = out_ref.shape[1]
    for at, piece in zip(rows, pieces):
        values = piece[...].astype(jnp.float32)
        for line in range(lines):
            wide_ref[at, line : line + 1] = values[:, line * LANES : (line + 1) * LANES]
    out_ref[...] = wide_ref[...].astype(out_ref.dtype)


def stack(rows, pieces, gain):
    shape = (len(pieces), pieces[0].shape[1] // LANES, LANES)
    return pl.pallas_call(
        functools.partial(stack_kernel, rows),
        out_shape=jax.ShapeDtypeStruct(shape, pieces[0].dtype),
        in_specs=[VMEM] * len(pieces) + [pl.BlockSpec(memory_space=pl.ANY)],
        out_specs=VMEM,
        scratch_shapes=[pltpu.VMEM(shape, jnp.float32)],
        compiler_params=pltpu.CompilerParams(vmem_limit_bytes=2 << 20),
        name="stack",
    )(*pieces, gain)


def load_gain_kernel(half, gate_hbm, up_hbm, gain_hbm, both_vmem, gain_vmem, sems):
    own = pl.multiple_of(lax.axis_index("groups") * half, LANES)
    copies = [pltpu.make_async_copy(gain_hbm, gain_vmem, sems.at[2])] + [
        pltpu.make_async_copy(
            weight.at[pl.ds(0, both_vmem.shape[0]), pl.ds(own, half)],
            both_vmem.at[:, pl.ds(at * half, half)],
            sems.at[at],
        )
        for at, weight in enumerate((gate_hbm, up_hbm))
    ]
    for copy in copies:
        copy.start()
    for copy in copies:
        copy.wait()


def load_first(w_gate, w_up, gain, half, count):
    return pl.pallas_call(
        functools.partial(load_gain_kernel, half),
        out_shape=(
            pltpu.VMEM((count, 2 * half), w_gate.dtype),
            pltpu.VMEM(gain.shape, gain.dtype),
        ),
        in_specs=[HBM] * 3,
        out_specs=(VMEM, VMEM),
        scratch_shapes=[pltpu.SemaphoreType.DMA((3,))],
        compiler_params=pltpu.CompilerParams(vmem_limit_bytes=1 << 20),
        cost_estimate=pl.CostEstimate(
            flops=0, bytes_accessed=2 * count * half * 2, transcendentals=0
        ),
        name="load_first",
    )(w_gate, w_up, pltpu.with_memory_space_constraint(gain, pltpu.HBM))


def load_second_kernel(
    half,
    row,
    place,
    lengths,
    hit_lengths,
    start_positions,
    gate_hbm,
    up_hbm,
    both_vmem,
    mark_vmem,
    lengths_smem,
    hit_smem,
    start_smem,
    sems,
):
    own = pl.multiple_of(lax.axis_index("groups") * half, LANES)
    small = [
        pltpu.make_async_copy(source, target, sems.at[2 + at])
        for at, (source, target) in enumerate(
            ((lengths, lengths_smem), (hit_lengths, hit_smem), (start_positions, start_smem))
        )
    ]
    copies = [
        pltpu.make_async_copy(
            weight.at[pl.ds(row, both_vmem.shape[0]), pl.ds(own, half)],
            both_vmem.at[:, pl.ds(at * half, half)],
            sems.at[at],
        )
        for at, weight in enumerate((gate_hbm, up_hbm))
    ]
    for copy in small + copies:
        copy.start()
    for copy in small:
        copy.wait()
    live = live_flag(lengths_smem, hit_smem, start_smem, place())
    mark_vmem[...] = jnp.full(mark_vmem.shape, live.astype(jnp.float32), jnp.float32)
    for copy in copies:
        copy.wait()


def load_second(w_gate, w_up, half, row, count, requests, place):
    return pl.pallas_call(
        functools.partial(load_second_kernel, half, row, place),
        out_shape=(
            pltpu.VMEM((count, 2 * half), w_gate.dtype),
            jax.ShapeDtypeStruct((8, LANES), jnp.float32),
        ),
        in_specs=[HBM] * (2 + len(requests)),
        out_specs=(VMEM, VMEM),
        scratch_shapes=[pltpu.SMEM(array.shape, array.dtype) for array in requests]
        + [pltpu.SemaphoreType.DMA((5,))],
        compiler_params=pltpu.CompilerParams(vmem_limit_bytes=1 << 20),
        cost_estimate=pl.CostEstimate(
            flops=0, bytes_accessed=2 * count * half * 2, transcendentals=0
        ),
        name="load_second",
    )(*requests, w_gate, w_up)


def load_third_kernel(half, row, gate_hbm, up_hbm, near_ref, both_vmem, sems):
    own = pl.multiple_of(lax.axis_index("groups") * half, LANES)
    copies = [
        pltpu.make_async_copy(
            weight.at[pl.ds(row, both_vmem.shape[0]), pl.ds(own, half)],
            both_vmem.at[:, pl.ds(at * half, half)],
            sems.at[at],
        )
        for at, weight in enumerate((gate_hbm, up_hbm))
    ]
    for copy in copies:
        copy.start()
    for copy in copies:
        copy.wait()


def load_third(w_gate, w_up, near, half, row, count):
    return pl.pallas_call(
        functools.partial(load_third_kernel, half, row),
        out_shape=pltpu.VMEM((count, 2 * half), w_gate.dtype),
        in_specs=[HBM] * 2 + [pl.BlockSpec(memory_space=pl.ANY)],
        out_specs=VMEM,
        scratch_shapes=[pltpu.SemaphoreType.DMA((2,))],
        compiler_params=pltpu.CompilerParams(vmem_limit_bytes=1 << 20),
        cost_estimate=pl.CostEstimate(
            flops=0, bytes_accessed=2 * count * half * 2, transcendentals=0
        ),
        name="load_third",
    )(w_gate, w_up, near)


def pack_kernel(*refs):
    pieces, gain_ref, out_ref, wide_ref = refs[:-4], refs[-4], refs[-2], refs[-1]
    rows = out_ref.shape[0]
    lines = out_ref.shape[1] // LANES
    stride = wide_ref.shape[0] // rows
    gain = gain_ref[...].astype(jnp.float32)
    row = 0
    for piece in pieces:
        values = piece[...].astype(jnp.float32)
        mean_sq = jnp.sum(values * values, axis=(1, 2), keepdims=True) * (1.0 / (lines * LANES))
        scaled = values * lax.rsqrt(mean_sq + 1e-05) * gain[None]
        for at in range(piece.shape[0]):
            wide_ref[row * stride : row * stride + lines] = scaled[at]
            row += 1
    for line in range(lines):
        out_ref[:, line * LANES : (line + 1) * LANES] = wide_ref[
            pl.ds(line, rows, stride=stride), :
        ].astype(jnp.bfloat16)


def pack(pieces, gain, mark):
    rows = sum(piece.shape[0] for piece in pieces)
    lines = pieces[0].shape[1]
    return pl.pallas_call(
        pack_kernel,
        out_shape=jax.ShapeDtypeStruct((rows, lines * LANES), jnp.bfloat16),
        in_specs=[VMEM] * (len(pieces) + 1) + [pl.BlockSpec(memory_space=pl.ANY)],
        out_specs=VMEM,
        scratch_shapes=[pltpu.VMEM((rows * (lines + 1), LANES), jnp.float32)],
        compiler_params=pltpu.CompilerParams(vmem_limit_bytes=4 << 20),
        name="pack",
    )(*pieces, pltpu.with_memory_space_constraint(gain, pltpu.VMEM), mark)


def block_kernel(
    half,
    chunk,
    deals,
    near_ref,
    far_ref,
    first_refs,
    gate_hbm,
    up_hbm,
    down_hbm,
    keep_ref,
    send_ref,
    wide_ref,
    rows_ref,
    product_ref,
    hidden_ref,
    rest_ref,
    down_ref,
    both_sems,
    down_sems,
):
    tile = 512
    rows, depth = rows_ref.shape
    lanes = LANES
    lines = depth // lanes
    stride = wide_ref.shape[0] // rows
    loaded = sum(ref.shape[0] for ref in first_refs)
    own = pl.multiple_of(lax.axis_index("groups") * half, LANES)
    loads = []
    at = 0
    for step, deal in enumerate(deals):
        loads.append(
            [
                pltpu.make_async_copy(
                    weight.at[pl.ds(loaded + at, deal), pl.ds(own, half)],
                    rest_ref.at[pl.ds(at, deal), pl.ds(side * half, half)],
                    both_sems.at[step, side],
                )
                for side, weight in enumerate((gate_hbm, up_hbm))
            ]
        )
        at += deal
    pairs = len(loads)
    for step, at in enumerate(range(0, depth, chunk)):
        loads.append(
            [
                pltpu.make_async_copy(
                    down_hbm.at[pl.ds(own, half), pl.ds(at, chunk)],
                    down_ref.at[pl.ds(0, half), pl.ds(at, chunk)],
                    down_sems.at[step],
                )
            ]
        )

    waiting = list(loads)

    def start():
        if waiting:
            for copy in waiting.pop(0):
                copy.start()

    def wait(number):
        for copy in loads[number]:
            copy.wait()

    def multiply(at, count, ref, row, halfway):
        for column in range(0, 2 * half, tile):
            columns = pl.ds(column, min(tile, 2 * half - column))
            value = jnp.dot(
                rows_ref[:, at : at + count],
                ref[row : row + count, columns],
                preferred_element_type=jnp.float32,
            )
            if at == 0:
                product_ref[:, columns] = value
            else:
                product_ref[:, columns] += value
            if halfway and column == tile:
                start()

    start()
    padded = down_ref.shape[0]
    if padded > half:
        down_ref[half:] = jnp.zeros((padded - half, depth), down_ref.dtype)
        hidden_ref[:, half:] = jnp.zeros((rows, padded - half), hidden_ref.dtype)
    rows_ref[: rows // 2] = near_ref[...]
    rows_ref[rows // 2 :] = far_ref[...]
    at = 0
    for ref in first_refs:
        multiply(at, ref.shape[0], ref, 0, False)
        start()
        at += ref.shape[0]
    row = 0
    for step, deal in enumerate(deals):
        wait(step)
        multiply(at, deal, rest_ref, row, step > 0)
        start()
        at += deal
        row += deal
    while waiting:
        start()
    gate_out = product_ref[:, :half]
    up_out = product_ref[:, half:]
    hidden_ref[:, :half] = (gate_out / (1.0 + jnp.exp(-gate_out)) * up_out).astype(jnp.bfloat16)
    zero = jnp.minimum(lax.axis_index("core"), 0)
    for step in range(depth // chunk):
        wait(pairs + step)
        for at in range(step * chunk, (step + 1) * chunk, tile):
            result = jnp.dot(
                hidden_ref[...], down_ref[:, pl.ds(at, tile)], preferred_element_type=jnp.float32
            )
            for line in range(tile // lanes):
                wide_ref[pl.ds(at // lanes + line, rows, stride=stride), :] = result[
                    :, line * lanes : (line + 1) * lanes
                ]
        done = step * chunk // lanes
        count = chunk // lanes
        for row in range(rows // 2):
            keep_ref[row + zero, done : done + count] = wide_ref[
                row * stride + done : row * stride + done + count
            ]
            at = (row + rows // 2) * stride + done
            send_ref[row + zero, done : done + count] = wide_ref[at : at + count].astype(
                jnp.bfloat16
            )


def block(near, far, firsts, w_gate, w_up, w_down, half):
    rows, depth = near.shape
    lines = depth // LANES
    rest = depth - sum(first.shape[0] for first in firsts)
    deals = (CHUNK, rest - CHUNK)
    padded = -(-half // 256) * 256

    def body(near_ref, far_ref, *refs):
        count = len(firsts)
        block_kernel(half, 2 * CHUNK, deals, near_ref, far_ref, refs[:count], *refs[count:])

    return pl.pallas_call(
        body,
        out_shape=(
            jax.ShapeDtypeStruct((rows, lines, LANES), jnp.float32),
            jax.ShapeDtypeStruct((rows, lines, LANES), jnp.bfloat16),
        ),
        in_specs=[VMEM] * (2 + len(firsts)) + [HBM] * 3,
        out_specs=(VMEM, VMEM),
        scratch_shapes=[
            pltpu.VMEM((2 * rows * (lines + 1), LANES), jnp.float32),
            pltpu.VMEM((2 * rows, depth), jnp.bfloat16),
            pltpu.VMEM((2 * rows, 2 * half), jnp.float32),
            pltpu.VMEM((2 * rows, padded), jnp.bfloat16),
            pltpu.VMEM((rest, 2 * half), jnp.bfloat16),
            pltpu.VMEM((padded, depth), jnp.bfloat16),
            pltpu.SemaphoreType.DMA((2, 2)),
            pltpu.SemaphoreType.DMA((depth // (2 * CHUNK),)),
        ],
        compiler_params=pltpu.CompilerParams(
            vmem_limit_bytes=(rest * 2 * half + depth * padded) * 2 + (6 << 20)
        ),
        cost_estimate=pl.CostEstimate(
            flops=12 * rows * depth * half,
            bytes_accessed=(rest * 2 + depth) * half * 2,
            transcendentals=0,
        ),
        name="block",
    )(
        near,
        far,
        *(pltpu.with_memory_space_constraint(first, pltpu.VMEM) for first in firsts),
        w_gate,
        w_up,
        w_down,
    )


def finish_kernel(*refs):
    pieces, live_ref, out_ref = refs[:-2], refs[-2], refs[-1]
    totals = pieces[0][...].astype(jnp.float32)
    for piece in pieces[1:]:
        totals = totals + piece[...].astype(jnp.float32)
    totals = jnp.where(live_ref[:1] > 0, totals[0], jnp.zeros_like(totals[0]))
    for line in range(totals.shape[0]):
        out_ref[:, line * LANES : (line + 1) * LANES] = totals[line : line + 1].astype(jnp.bfloat16)


def finish(pieces, live):
    lines = pieces[0].shape[1]
    return pl.pallas_call(
        finish_kernel,
        out_shape=jax.ShapeDtypeStruct((1, lines * LANES), jnp.bfloat16),
        in_specs=[VMEM] * (len(pieces) + 1),
        out_specs=VMEM,
        compiler_params=pltpu.CompilerParams(vmem_limit_bytes=1 << 20),
        name="finish",
    )(*pieces, live)


def swap(value, axes, offset):
    places = range(lax.axis_size(axes))
    return lax.ppermute(value, axes, [(place, place ^ offset) for place in places])


def shared(tokens, norm_gain, w_gate, w_up, w_down, lengths, hit_lengths, start_positions):
    square = ("groups", "x")
    half = w_gate.shape[1] // lax.axis_size("groups")
    w_gate, w_up, w_down = (
        pltpu.with_memory_space_constraint(array, pltpu.HBM) for array in (w_gate, w_up, w_down)
    )
    requests = tuple(
        pltpu.with_memory_space_constraint(array, pltpu.HBM)
        for array in (lengths, hit_lengths, start_positions)
    )

    def place():
        return (lax.axis_index("z") * lax.axis_size("x") + lax.axis_index("x")) * lax.axis_size(
            "core"
        ) + lax.axis_index("core")

    deep = lax.axis_size("z")
    others = range(1, lax.axis_size(square))
    rows = [0] + list(range(2, deep)) + [1]
    column = [swap(tokens, "z", at) if at else tokens for at in rows]
    first, gain = load_first(w_gate, w_up, norm_gain.reshape(-1, LANES), half, 2 * CHUNK)
    column = stack(rows, column, gain)
    plane = [column] + [swap(column, square, at) for at in others]
    second, live = load_second(w_gate, w_up, half, 2 * CHUNK, 5 * CHUNK // 2, requests, place)
    near = pack(plane, gain, live)
    far = swap(near, "core", 1)
    third = load_third(w_gate, w_up, near, half, 9 * CHUNK // 2, CHUNK // 2)
    kept, sent = block(near, far, (first, second, third), w_gate, w_up, w_down, half)
    plane = (kept + swap(sent, "core", 1).astype(jnp.float32)).astype(jnp.bfloat16)
    pieces = jnp.split(plane, lax.axis_size(square), axis=0)
    column = pieces[0].astype(jnp.float32)
    for piece in [swap(pieces[at], square, at) for at in reversed(others)]:
        column = column + piece.astype(jnp.float32)
    pieces = jnp.split(column.astype(jnp.bfloat16), deep, axis=0)
    return finish(
        pieces[:1] + [swap(piece, "z", at + 1) for at, piece in enumerate(pieces[1:])], live
    )


def solution(mesh):
    groups, members = mesh.shape["groups"], mesh.shape["tensor"]

    def placed(axes, whole):
        return (
            P(whole, None),
            P(),
            P(None, axes),
            P(None, axes),
            P(axes, None),
            P("groups"),
            P("groups"),
            P("groups"),
        )

    def run(*arrays):
        units = arrays[2].shape[1] // members
        if (
            units % (LANES * groups) == 0
            and arrays[0].shape[0] == groups * members
            and groups == 2
            and members >= 8
            and members & (members - 1) == 0
        ):
            body, axes, whole = shared, ("z", "x", "core"), ROW_LINES
            over = jax.sharding.Mesh(mesh.devices.reshape(groups, members // 4, 2, 2), ROW_LINES)
        else:
            body, axes, whole, over = local, "tensor", ("groups", "tensor"), mesh
        return jax.shard_map(
            body,
            mesh=over,
            in_specs=placed(axes, whole),
            out_specs=P(whole, None),
            check_vma=False,
        )(*arrays)

    return run
```

```python
import functools

import jax
import jax.numpy as jnp
from jax import lax
from jax.experimental import pallas as pl
from jax.experimental.pallas import tpu as pltpu
from jax.sharding import PartitionSpec as P

LANES = 128
ROW_LINES = ("groups", "z", "x", "core")


def normalize(tokens, norm_gain):
    values = tokens.astype(jnp.float32)
    mean_sq = jnp.mean(values * values, axis=-1, keepdims=True)
    return (values * lax.rsqrt(mean_sq + 1e-05) * norm_gain.astype(jnp.float32)).astype(
        jnp.bfloat16
    )


def live_rows(lengths, hit_lengths, start_positions, token_index):
    ends = jnp.cumsum(lengths)
    begins = ends - lengths
    member = (token_index[:, None] >= begins[None, :]) & (token_index[:, None] < ends[None, :])
    member_int = member.astype(jnp.int32)
    offsets = token_index - jnp.sum(member_int * begins[None, :], axis=1)
    position = jnp.sum(member_int * start_positions[None, :], axis=1) + offsets
    covered = jnp.sum(member_int * hit_lengths[None, :], axis=1)
    return position >= covered


def local(tokens, norm_gain, w_gate, w_up, w_down, lengths, hit_lengths, start_positions):
    row_count = tokens.shape[0]
    normed = normalize(tokens, norm_gain)
    piece_rows = lax.all_gather(normed, "tensor", axis=0, tiled=True)
    gate_out = jnp.dot(piece_rows, w_gate, preferred_element_type=jnp.float32)
    up_out = jnp.dot(piece_rows, w_up, preferred_element_type=jnp.float32)
    hidden = (jax.nn.silu(gate_out) * up_out).astype(jnp.bfloat16)
    partial_value = jnp.dot(hidden, w_down, preferred_element_type=jnp.float32)
    rounded = partial_value.astype(jnp.bfloat16)
    totals = jnp.sum(
        lax.all_to_all(rounded[None], "tensor", split_axis=1, concat_axis=0, tiled=True).astype(
            jnp.float32
        ),
        axis=0,
    )
    token_index = lax.axis_index("tensor") * row_count + jnp.arange(row_count, dtype=jnp.int32)
    live = live_rows(lengths, hit_lengths, start_positions, token_index)
    return jnp.where(live[:, None], totals, jnp.zeros_like(totals)).astype(jnp.bfloat16)


VMEM = pl.BlockSpec(memory_space=pltpu.VMEM)
HBM = pl.BlockSpec(memory_space=pltpu.HBM)
CHUNK = 1024


def live_flag(lengths, hit_lengths, start_positions, token):
    begin = 0
    live = False
    for request in range(lengths.shape[0]):
        end = begin + lengths[request]
        position = start_positions[request] + token - begin
        inside = (token >= begin) & (token < end)
        live = live | (inside & (position >= hit_lengths[request]))
        begin = end
    return live


def stack_kernel(rows, *refs):
    pieces, out_ref, wide_ref = refs[:-3], refs[-2], refs[-1]
    lines = out_ref.shape[1]
    for at, piece in zip(rows, pieces):
        values = piece[...].astype(jnp.float32)
        for line in range(lines):
            wide_ref[at, line : line + 1] = values[:, line * LANES : (line + 1) * LANES]
    out_ref[...] = wide_ref[...].astype(out_ref.dtype)


def stack(rows, pieces, gain):
    shape = (len(pieces), pieces[0].shape[1] // LANES, LANES)
    return pl.pallas_call(
        functools.partial(stack_kernel, rows),
        out_shape=jax.ShapeDtypeStruct(shape, pieces[0].dtype),
        in_specs=[VMEM] * len(pieces) + [pl.BlockSpec(memory_space=pl.ANY)],
        out_specs=VMEM,
        scratch_shapes=[pltpu.VMEM(shape, jnp.float32)],
        compiler_params=pltpu.CompilerParams(vmem_limit_bytes=2 << 20),
        name="stack",
    )(*pieces, gain)


def load_gain_kernel(half, gate_hbm, up_hbm, gain_hbm, both_vmem, gain_vmem, sems):
    own = pl.multiple_of(lax.axis_index("groups") * half, LANES)
    copies = [pltpu.make_async_copy(gain_hbm, gain_vmem, sems.at[2])] + [
        pltpu.make_async_copy(
            weight.at[pl.ds(0, both_vmem.shape[0]), pl.ds(own, half)],
            both_vmem.at[:, pl.ds(at * half, half)],
            sems.at[at],
        )
        for at, weight in enumerate((gate_hbm, up_hbm))
    ]
    for copy in copies:
        copy.start()
    for copy in copies:
        copy.wait()


def load_first(w_gate, w_up, gain, half, count):
    return pl.pallas_call(
        functools.partial(load_gain_kernel, half),
        out_shape=(
            pltpu.VMEM((count, 2 * half), w_gate.dtype),
            pltpu.VMEM(gain.shape, gain.dtype),
        ),
        in_specs=[HBM] * 3,
        out_specs=(VMEM, VMEM),
        scratch_shapes=[pltpu.SemaphoreType.DMA((3,))],
        compiler_params=pltpu.CompilerParams(vmem_limit_bytes=1 << 20),
        cost_estimate=pl.CostEstimate(
            flops=0, bytes_accessed=2 * count * half * 2, transcendentals=0
        ),
        name="load_first",
    )(w_gate, w_up, pltpu.with_memory_space_constraint(gain, pltpu.HBM))


def load_second_kernel(
    half,
    row,
    place,
    lengths,
    hit_lengths,
    start_positions,
    gate_hbm,
    up_hbm,
    both_vmem,
    mark_vmem,
    lengths_smem,
    hit_smem,
    start_smem,
    sems,
):
    own = pl.multiple_of(lax.axis_index("groups") * half, LANES)
    small = [
        pltpu.make_async_copy(source, target, sems.at[2 + at])
        for at, (source, target) in enumerate(
            ((lengths, lengths_smem), (hit_lengths, hit_smem), (start_positions, start_smem))
        )
    ]
    copies = [
        pltpu.make_async_copy(
            weight.at[pl.ds(row, both_vmem.shape[0]), pl.ds(own, half)],
            both_vmem.at[:, pl.ds(at * half, half)],
            sems.at[at],
        )
        for at, weight in enumerate((gate_hbm, up_hbm))
    ]
    for copy in small + copies:
        copy.start()
    for copy in small:
        copy.wait()
    live = live_flag(lengths_smem, hit_smem, start_smem, place())
    mark_vmem[...] = jnp.full(mark_vmem.shape, live.astype(jnp.float32), jnp.float32)
    for copy in copies:
        copy.wait()


def load_second(w_gate, w_up, half, row, count, requests, place):
    return pl.pallas_call(
        functools.partial(load_second_kernel, half, row, place),
        out_shape=(
            pltpu.VMEM((count, 2 * half), w_gate.dtype),
            jax.ShapeDtypeStruct((8, LANES), jnp.float32),
        ),
        in_specs=[HBM] * (2 + len(requests)),
        out_specs=(VMEM, VMEM),
        scratch_shapes=[pltpu.SMEM(array.shape, array.dtype) for array in requests]
        + [pltpu.SemaphoreType.DMA((5,))],
        compiler_params=pltpu.CompilerParams(vmem_limit_bytes=1 << 20),
        cost_estimate=pl.CostEstimate(
            flops=0, bytes_accessed=2 * count * half * 2, transcendentals=0
        ),
        name="load_second",
    )(*requests, w_gate, w_up)


def pack_kernel(*refs):
    pieces, gain_ref, out_ref, wide_ref = refs[:-4], refs[-4], refs[-2], refs[-1]
    rows = out_ref.shape[0]
    lines = out_ref.shape[1] // LANES
    stride = wide_ref.shape[0] // rows
    gain = gain_ref[...].astype(jnp.float32)
    row = 0
    for piece in pieces:
        values = piece[...].astype(jnp.float32)
        mean_sq = jnp.sum(values * values, axis=(1, 2), keepdims=True) * (1.0 / (lines * LANES))
        scaled = values * lax.rsqrt(mean_sq + 1e-05) * gain[None]
        for at in range(piece.shape[0]):
            wide_ref[row * stride : row * stride + lines] = scaled[at]
            row += 1
    for line in range(lines):
        out_ref[:, line * LANES : (line + 1) * LANES] = wide_ref[
            pl.ds(line, rows, stride=stride), :
        ].astype(jnp.bfloat16)


def pack(pieces, gain, mark):
    rows = sum(piece.shape[0] for piece in pieces)
    lines = pieces[0].shape[1]
    return pl.pallas_call(
        pack_kernel,
        out_shape=jax.ShapeDtypeStruct((rows, lines * LANES), jnp.bfloat16),
        in_specs=[VMEM] * (len(pieces) + 1) + [pl.BlockSpec(memory_space=pl.ANY)],
        out_specs=VMEM,
        scratch_shapes=[pltpu.VMEM((rows * (lines + 1), LANES), jnp.float32)],
        compiler_params=pltpu.CompilerParams(vmem_limit_bytes=4 << 20),
        name="pack",
    )(*pieces, pltpu.with_memory_space_constraint(gain, pltpu.VMEM), mark)


def block_kernel(
    half,
    chunk,
    deals,
    near_ref,
    far_ref,
    first_refs,
    gate_hbm,
    up_hbm,
    down_hbm,
    keep_ref,
    send_ref,
    wide_ref,
    rows_ref,
    product_ref,
    hidden_ref,
    rest_ref,
    down_ref,
    both_sems,
    down_sems,
):
    tile = 512
    rows, depth = rows_ref.shape
    lanes = LANES
    lines = depth // lanes
    stride = wide_ref.shape[0] // rows
    loaded = sum(ref.shape[0] for ref in first_refs)
    own = pl.multiple_of(lax.axis_index("groups") * half, LANES)
    loads = []
    at = 0
    for step, deal in enumerate(deals):
        loads.append(
            [
                pltpu.make_async_copy(
                    weight.at[pl.ds(loaded + at, deal), pl.ds(own, half)],
                    rest_ref.at[pl.ds(at, deal), pl.ds(side * half, half)],
                    both_sems.at[step, side],
                )
                for side, weight in enumerate((gate_hbm, up_hbm))
            ]
        )
        at += deal
    pairs = len(loads)
    for step, at in enumerate(range(0, depth, chunk)):
        loads.append(
            [
                pltpu.make_async_copy(
                    down_hbm.at[pl.ds(own, half), pl.ds(at, chunk)],
                    down_ref.at[:, pl.ds(at, chunk)],
                    down_sems.at[step],
                )
            ]
        )

    waiting = list(loads)

    def start():
        if waiting:
            for copy in waiting.pop(0):
                copy.start()

    def wait(number):
        for copy in loads[number]:
            copy.wait()

    def multiply(at, count, ref, row, halfway):
        for column in range(0, 2 * half, tile):
            columns = pl.ds(column, min(tile, 2 * half - column))
            value = jnp.dot(
                rows_ref[:, at : at + count],
                ref[row : row + count, columns],
                preferred_element_type=jnp.float32,
            )
            if at == 0:
                product_ref[:, columns] = value
            else:
                product_ref[:, columns] += value
            if halfway and column == tile:
                start()

    start()
    rows_ref[: rows // 2] = near_ref[...]
    rows_ref[rows // 2 :] = far_ref[...]
    at = 0
    for ref in first_refs:
        multiply(at, ref.shape[0], ref, 0, False)
        if at == 0:
            start()
        at += ref.shape[0]
    row = 0
    for step, deal in enumerate(deals):
        wait(step)
        multiply(at, deal, rest_ref, row, True)
        start()
        at += deal
        row += deal
    while waiting:
        start()
    gate_out = product_ref[:, :half]
    up_out = product_ref[:, half:]
    hidden_ref[...] = (gate_out / (1.0 + jnp.exp(-gate_out)) * up_out).astype(jnp.bfloat16)
    zero = jnp.minimum(lax.axis_index("core"), 0)
    for step in range(depth // chunk):
        wait(pairs + step)
        for at in range(step * chunk, (step + 1) * chunk, tile):
            result = jnp.dot(
                hidden_ref[...], down_ref[:, pl.ds(at, tile)], preferred_element_type=jnp.float32
            )
            for line in range(tile // lanes):
                wide_ref[pl.ds(at // lanes + line, rows, stride=stride), :] = result[
                    :, line * lanes : (line + 1) * lanes
                ]
        done = step * chunk // lanes
        count = chunk // lanes
        for row in range(rows // 2):
            keep_ref[row + zero, done : done + count] = wide_ref[
                row * stride + done : row * stride + done + count
            ]
            at = (row + rows // 2) * stride + done
            send_ref[row + zero, done : done + count] = wide_ref[at : at + count].astype(
                jnp.bfloat16
            )


def block(near, far, firsts, w_gate, w_up, w_down, half):
    rows, depth = near.shape
    lines = depth // LANES
    rest = depth - sum(first.shape[0] for first in firsts)
    deals = (rest * 3 // 7, rest - rest * 3 // 7)

    def body(near_ref, far_ref, *refs):
        count = len(firsts)
        block_kernel(half, 2 * CHUNK, deals, near_ref, far_ref, refs[:count], *refs[count:])

    return pl.pallas_call(
        body,
        out_shape=(
            jax.ShapeDtypeStruct((rows, lines, LANES), jnp.float32),
            jax.ShapeDtypeStruct((rows, lines, LANES), jnp.bfloat16),
        ),
        in_specs=[VMEM] * (2 + len(firsts)) + [HBM] * 3,
        out_specs=(VMEM, VMEM),
        scratch_shapes=[
            pltpu.VMEM((2 * rows * (lines + 1), LANES), jnp.float32),
            pltpu.VMEM((2 * rows, depth), jnp.bfloat16),
            pltpu.VMEM((2 * rows, 2 * half), jnp.float32),
            pltpu.VMEM((2 * rows, half), jnp.bfloat16),
            pltpu.VMEM((rest, 2 * half), jnp.bfloat16),
            pltpu.VMEM((half, depth), jnp.bfloat16),
            pltpu.SemaphoreType.DMA((2, 2)),
            pltpu.SemaphoreType.DMA((depth // (2 * CHUNK),)),
        ],
        compiler_params=pltpu.CompilerParams(
            vmem_limit_bytes=(rest * 2 + depth) * half * 2 + (6 << 20)
        ),
        cost_estimate=pl.CostEstimate(
            flops=12 * rows * depth * half,
            bytes_accessed=(rest * 2 + depth) * half * 2,
            transcendentals=0,
        ),
        name="block",
    )(
        near,
        far,
        *(pltpu.with_memory_space_constraint(first, pltpu.VMEM) for first in firsts),
        w_gate,
        w_up,
        w_down,
    )


def finish_kernel(*refs):
    pieces, live_ref, out_ref = refs[:-2], refs[-2], refs[-1]
    totals = pieces[0][...].astype(jnp.float32)
    for piece in pieces[1:]:
        totals = totals + piece[...].astype(jnp.float32)
    totals = jnp.where(live_ref[:1] > 0, totals[0], jnp.zeros_like(totals[0]))
    for line in range(totals.shape[0]):
        out_ref[:, line * LANES : (line + 1) * LANES] = totals[line : line + 1].astype(jnp.bfloat16)


def finish(pieces, live):
    lines = pieces[0].shape[1]
    return pl.pallas_call(
        finish_kernel,
        out_shape=jax.ShapeDtypeStruct((1, lines * LANES), jnp.bfloat16),
        in_specs=[VMEM] * (len(pieces) + 1),
        out_specs=VMEM,
        compiler_params=pltpu.CompilerParams(vmem_limit_bytes=1 << 20),
        name="finish",
    )(*pieces, live)


def swap(value, axes, offset):
    places = range(lax.axis_size(axes))
    return lax.ppermute(value, axes, [(place, place ^ offset) for place in places])


def shared(tokens, norm_gain, w_gate, w_up, w_down, lengths, hit_lengths, start_positions):
    square = ("groups", "x")
    half = w_gate.shape[1] // lax.axis_size("groups")
    w_gate, w_up, w_down = (
        pltpu.with_memory_space_constraint(array, pltpu.HBM) for array in (w_gate, w_up, w_down)
    )
    requests = tuple(
        pltpu.with_memory_space_constraint(array, pltpu.HBM)
        for array in (lengths, hit_lengths, start_positions)
    )

    def place():
        return (lax.axis_index("z") * lax.axis_size("x") + lax.axis_index("x")) * lax.axis_size(
            "core"
        ) + lax.axis_index("core")

    deep = lax.axis_size("z")
    others = range(1, lax.axis_size(square))
    rows = [0] + list(range(2, deep)) + [1]
    column = [swap(tokens, "z", at) if at else tokens for at in rows]
    first, gain = load_first(w_gate, w_up, norm_gain.reshape(-1, LANES), half, 2 * CHUNK)
    column = stack(rows, column, gain)
    plane = [column] + [swap(column, square, at) for at in others]
    second, live = load_second(w_gate, w_up, half, 2 * CHUNK, 5 * CHUNK // 2, requests, place)
    near = pack(plane, gain, live)
    far = swap(near, "core", 1)
    kept, sent = block(near, far, (first, second), w_gate, w_up, w_down, half)
    plane = (kept + swap(sent, "core", 1).astype(jnp.float32)).astype(jnp.bfloat16)
    pieces = jnp.split(plane, lax.axis_size(square), axis=0)
    column = pieces[0].astype(jnp.float32)
    for piece in [swap(pieces[at], square, at) for at in reversed(others)]:
        column = column + piece.astype(jnp.float32)
    pieces = jnp.split(column.astype(jnp.bfloat16), deep, axis=0)
    return finish(
        pieces[:1] + [swap(piece, "z", at + 1) for at, piece in enumerate(pieces[1:])], live
    )


def solution(mesh):
    groups, members = mesh.shape["groups"], mesh.shape["tensor"]

    def placed(axes, whole):
        return (
            P(whole, None),
            P(),
            P(None, axes),
            P(None, axes),
            P(axes, None),
            P("groups"),
            P("groups"),
            P("groups"),
        )

    def run(*arrays):
        units = arrays[2].shape[1] // members
        if (
            units % (LANES * groups) == 0
            and arrays[0].shape[0] == groups * members
            and groups == 2
            and members >= 8
            and members & (members - 1) == 0
        ):
            body, axes, whole = shared, ("z", "x", "core"), ROW_LINES
            over = jax.sharding.Mesh(mesh.devices.reshape(groups, members // 4, 2, 2), ROW_LINES)
        else:
            body, axes, whole, over = local, "tensor", ("groups", "tensor"), mesh
        return jax.shard_map(
            body,
            mesh=over,
            in_specs=placed(axes, whole),
            out_specs=P(whole, None),
            check_vma=False,
        )(*arrays)

    return run
```

```python
import functools

import jax
import jax.numpy as jnp
from jax import lax
from jax.experimental import pallas as pl
from jax.experimental.pallas import tpu as pltpu
from jax.sharding import PartitionSpec as P

LANES = 128
ROW_LINES = ("groups", "z", "x", "core")


def normalize(tokens, norm_gain):
    values = tokens.astype(jnp.float32)
    mean_sq = jnp.mean(values * values, axis=-1, keepdims=True)
    return (values * lax.rsqrt(mean_sq + 1e-05) * norm_gain.astype(jnp.float32)).astype(
        jnp.bfloat16
    )


def live_rows(lengths, hit_lengths, start_positions, token_index):
    ends = jnp.cumsum(lengths)
    begins = ends - lengths
    member = (token_index[:, None] >= begins[None, :]) & (token_index[:, None] < ends[None, :])
    member_int = member.astype(jnp.int32)
    offsets = token_index - jnp.sum(member_int * begins[None, :], axis=1)
    position = jnp.sum(member_int * start_positions[None, :], axis=1) + offsets
    covered = jnp.sum(member_int * hit_lengths[None, :], axis=1)
    return position >= covered


def local(tokens, norm_gain, w_gate, w_up, w_down, lengths, hit_lengths, start_positions):
    row_count = tokens.shape[0]
    normed = normalize(tokens, norm_gain)
    piece_rows = lax.all_gather(normed, "tensor", axis=0, tiled=True)
    gate_out = jnp.dot(piece_rows, w_gate, preferred_element_type=jnp.float32)
    up_out = jnp.dot(piece_rows, w_up, preferred_element_type=jnp.float32)
    hidden = (jax.nn.silu(gate_out) * up_out).astype(jnp.bfloat16)
    partial_value = jnp.dot(hidden, w_down, preferred_element_type=jnp.float32)
    rounded = partial_value.astype(jnp.bfloat16)
    totals = jnp.sum(
        lax.all_to_all(rounded[None], "tensor", split_axis=1, concat_axis=0, tiled=True).astype(
            jnp.float32
        ),
        axis=0,
    )
    token_index = lax.axis_index("tensor") * row_count + jnp.arange(row_count, dtype=jnp.int32)
    live = live_rows(lengths, hit_lengths, start_positions, token_index)
    return jnp.where(live[:, None], totals, jnp.zeros_like(totals)).astype(jnp.bfloat16)


VMEM = pl.BlockSpec(memory_space=pltpu.VMEM)
HBM = pl.BlockSpec(memory_space=pltpu.HBM)
CHUNK = 1024


def live_flag(lengths, hit_lengths, start_positions, token):
    begin = 0
    live = False
    for request in range(lengths.shape[0]):
        end = begin + lengths[request]
        position = start_positions[request] + token - begin
        inside = (token >= begin) & (token < end)
        live = live | (inside & (position >= hit_lengths[request]))
        begin = end
    return live


def stack_kernel(rows, *refs):
    pieces, out_ref, wide_ref = refs[:-3], refs[-2], refs[-1]
    lines = out_ref.shape[1]
    for at, piece in zip(rows, pieces):
        values = piece[...].astype(jnp.float32)
        for line in range(lines):
            wide_ref[at, line : line + 1] = values[:, line * LANES : (line + 1) * LANES]
    out_ref[...] = wide_ref[...].astype(out_ref.dtype)


def stack(rows, pieces, gain):
    shape = (len(pieces), pieces[0].shape[1] // LANES, LANES)
    return pl.pallas_call(
        functools.partial(stack_kernel, rows),
        out_shape=jax.ShapeDtypeStruct(shape, pieces[0].dtype),
        in_specs=[VMEM] * len(pieces) + [pl.BlockSpec(memory_space=pl.ANY)],
        out_specs=VMEM,
        scratch_shapes=[pltpu.VMEM(shape, jnp.float32)],
        compiler_params=pltpu.CompilerParams(vmem_limit_bytes=2 << 20),
        name="stack",
    )(*pieces, gain)


def load_gain_kernel(half, gate_hbm, up_hbm, gain_hbm, both_vmem, gain_vmem, sems):
    own = pl.multiple_of(lax.axis_index("groups") * half, LANES)
    copies = [pltpu.make_async_copy(gain_hbm, gain_vmem, sems.at[2])] + [
        pltpu.make_async_copy(
            weight.at[pl.ds(0, both_vmem.shape[0]), pl.ds(own, half)],
            both_vmem.at[:, pl.ds(at * half, half)],
            sems.at[at],
        )
        for at, weight in enumerate((gate_hbm, up_hbm))
    ]
    for copy in copies:
        copy.start()
    for copy in copies:
        copy.wait()


def load_first(w_gate, w_up, gain, half, count):
    return pl.pallas_call(
        functools.partial(load_gain_kernel, half),
        out_shape=(
            pltpu.VMEM((count, 2 * half), w_gate.dtype),
            pltpu.VMEM(gain.shape, gain.dtype),
        ),
        in_specs=[HBM] * 3,
        out_specs=(VMEM, VMEM),
        scratch_shapes=[pltpu.SemaphoreType.DMA((3,))],
        compiler_params=pltpu.CompilerParams(vmem_limit_bytes=1 << 20),
        cost_estimate=pl.CostEstimate(
            flops=0, bytes_accessed=2 * count * half * 2, transcendentals=0
        ),
        name="load_first",
    )(w_gate, w_up, pltpu.with_memory_space_constraint(gain, pltpu.HBM))


def load_second_kernel(
    half,
    row,
    place,
    lengths,
    hit_lengths,
    start_positions,
    gate_hbm,
    up_hbm,
    both_vmem,
    mark_vmem,
    lengths_smem,
    hit_smem,
    start_smem,
    sems,
):
    own = pl.multiple_of(lax.axis_index("groups") * half, LANES)
    small = [
        pltpu.make_async_copy(source, target, sems.at[2 + at])
        for at, (source, target) in enumerate(
            ((lengths, lengths_smem), (hit_lengths, hit_smem), (start_positions, start_smem))
        )
    ]
    copies = [
        pltpu.make_async_copy(
            weight.at[pl.ds(row, both_vmem.shape[0]), pl.ds(own, half)],
            both_vmem.at[:, pl.ds(at * half, half)],
            sems.at[at],
        )
        for at, weight in enumerate((gate_hbm, up_hbm))
    ]
    for copy in small + copies:
        copy.start()
    for copy in small:
        copy.wait()
    live = live_flag(lengths_smem, hit_smem, start_smem, place())
    mark_vmem[...] = jnp.full(mark_vmem.shape, live.astype(jnp.float32), jnp.float32)
    for copy in copies:
        copy.wait()


def load_second(w_gate, w_up, half, row, count, requests, place):
    return pl.pallas_call(
        functools.partial(load_second_kernel, half, row, place),
        out_shape=(
            pltpu.VMEM((count, 2 * half), w_gate.dtype),
            jax.ShapeDtypeStruct((8, LANES), jnp.float32),
        ),
        in_specs=[HBM] * (2 + len(requests)),
        out_specs=(VMEM, VMEM),
        scratch_shapes=[pltpu.SMEM(array.shape, array.dtype) for array in requests]
        + [pltpu.SemaphoreType.DMA((5,))],
        compiler_params=pltpu.CompilerParams(vmem_limit_bytes=1 << 20),
        cost_estimate=pl.CostEstimate(
            flops=0, bytes_accessed=2 * count * half * 2, transcendentals=0
        ),
        name="load_second",
    )(*requests, w_gate, w_up)


def pack_kernel(*refs):
    pieces, gain_ref, out_ref, wide_ref = refs[:-4], refs[-4], refs[-2], refs[-1]
    rows = out_ref.shape[0]
    lines = out_ref.shape[1] // LANES
    stride = wide_ref.shape[0] // rows
    gain = gain_ref[...].astype(jnp.float32)
    row = 0
    for piece in pieces:
        values = piece[...].astype(jnp.float32)
        mean_sq = jnp.sum(values * values, axis=(1, 2), keepdims=True) * (1.0 / (lines * LANES))
        scaled = values * lax.rsqrt(mean_sq + 1e-05) * gain[None]
        for at in range(piece.shape[0]):
            wide_ref[row * stride : row * stride + lines] = scaled[at]
            row += 1
    for line in range(lines):
        out_ref[:, line * LANES : (line + 1) * LANES] = wide_ref[
            pl.ds(line, rows, stride=stride), :
        ].astype(jnp.bfloat16)


def pack(pieces, gain, mark):
    rows = sum(piece.shape[0] for piece in pieces)
    lines = pieces[0].shape[1]
    return pl.pallas_call(
        pack_kernel,
        out_shape=jax.ShapeDtypeStruct((rows, lines * LANES), jnp.bfloat16),
        in_specs=[VMEM] * (len(pieces) + 1) + [pl.BlockSpec(memory_space=pl.ANY)],
        out_specs=VMEM,
        scratch_shapes=[pltpu.VMEM((rows * (lines + 1), LANES), jnp.float32)],
        compiler_params=pltpu.CompilerParams(vmem_limit_bytes=4 << 20),
        name="pack",
    )(*pieces, pltpu.with_memory_space_constraint(gain, pltpu.VMEM), mark)


def block_kernel(
    half,
    chunk,
    deals,
    near_ref,
    far_ref,
    first_refs,
    gate_hbm,
    up_hbm,
    down_hbm,
    keep_ref,
    send_ref,
    wide_ref,
    rows_ref,
    product_ref,
    hidden_ref,
    rest_ref,
    down_ref,
    both_sems,
    down_sems,
):
    tile = 512
    rows, depth = rows_ref.shape
    lanes = LANES
    lines = depth // lanes
    stride = wide_ref.shape[0] // rows
    loaded = sum(ref.shape[0] for ref in first_refs)
    own = pl.multiple_of(lax.axis_index("groups") * half, LANES)
    loads = []
    at = 0
    for step, deal in enumerate(deals):
        loads.append(
            [
                pltpu.make_async_copy(
                    weight.at[pl.ds(loaded + at, deal), pl.ds(own, half)],
                    rest_ref.at[pl.ds(at, deal), pl.ds(side * half, half)],
                    both_sems.at[step, side],
                )
                for side, weight in enumerate((gate_hbm, up_hbm))
            ]
        )
        at += deal
    pairs = len(loads)
    spans = []
    while sum(width for _, width in spans) < depth:
        at = sum(width for _, width in spans)
        spans.append((at, chunk if depth - at > chunk else chunk // 2))
    for step, (at, width) in enumerate(spans):
        loads.append(
            [
                pltpu.make_async_copy(
                    down_hbm.at[pl.ds(own, half), pl.ds(at, width)],
                    down_ref.at[:, pl.ds(at, width)],
                    down_sems.at[step],
                )
            ]
        )

    waiting = list(loads)

    def start():
        if waiting:
            for copy in waiting.pop(0):
                copy.start()

    def wait(number):
        for copy in loads[number]:
            copy.wait()

    def multiply(at, count, ref, row, halfway):
        for column in range(0, 2 * half, tile):
            columns = pl.ds(column, min(tile, 2 * half - column))
            value = jnp.dot(
                rows_ref[:, at : at + count],
                ref[row : row + count, columns],
                preferred_element_type=jnp.float32,
            )
            if at == 0:
                product_ref[:, columns] = value
            else:
                product_ref[:, columns] += value
            if halfway and column == tile:
                start()

    start()
    rows_ref[: rows // 2] = near_ref[...]
    rows_ref[rows // 2 :] = far_ref[...]
    at = 0
    for ref in first_refs:
        multiply(at, ref.shape[0], ref, 0, False)
        start()
        at += ref.shape[0]
    row = 0
    for step, deal in enumerate(deals):
        wait(step)
        multiply(at, deal, rest_ref, row, True)
        start()
        at += deal
        row += deal
    while waiting:
        start()
    gate_out = product_ref[:, :half]
    up_out = product_ref[:, half:]
    hidden_ref[...] = (gate_out / (1.0 + jnp.exp(-gate_out)) * up_out).astype(jnp.bfloat16)
    zero = jnp.minimum(lax.axis_index("core"), 0)
    for step, (begin, width) in enumerate(spans):
        wait(pairs + step)
        for at in range(begin, begin + width, tile):
            result = jnp.dot(
                hidden_ref[...], down_ref[:, pl.ds(at, tile)], preferred_element_type=jnp.float32
            )
            for line in range(tile // lanes):
                wide_ref[pl.ds(at // lanes + line, rows, stride=stride), :] = result[
                    :, line * lanes : (line + 1) * lanes
                ]
        done = begin // lanes
        count = width // lanes
        for row in range(rows // 2):
            keep_ref[row + zero, done : done + count] = wide_ref[
                row * stride + done : row * stride + done + count
            ]
            at = (row + rows // 2) * stride + done
            send_ref[row + zero, done : done + count] = wide_ref[at : at + count].astype(
                jnp.bfloat16
            )


def block(near, far, firsts, w_gate, w_up, w_down, half):
    rows, depth = near.shape
    lines = depth // LANES
    rest = depth - sum(first.shape[0] for first in firsts)
    deals = (rest * 3 // 7, rest - rest * 3 // 7)

    def body(near_ref, far_ref, *refs):
        count = len(firsts)
        block_kernel(half, 2 * CHUNK, deals, near_ref, far_ref, refs[:count], *refs[count:])

    return pl.pallas_call(
        body,
        out_shape=(
            jax.ShapeDtypeStruct((rows, lines, LANES), jnp.float32),
            jax.ShapeDtypeStruct((rows, lines, LANES), jnp.bfloat16),
        ),
        in_specs=[VMEM] * (2 + len(firsts)) + [HBM] * 3,
        out_specs=(VMEM, VMEM),
        scratch_shapes=[
            pltpu.VMEM((2 * rows * (lines + 1), LANES), jnp.float32),
            pltpu.VMEM((2 * rows, depth), jnp.bfloat16),
            pltpu.VMEM((2 * rows, 2 * half), jnp.float32),
            pltpu.VMEM((2 * rows, half), jnp.bfloat16),
            pltpu.VMEM((rest, 2 * half), jnp.bfloat16),
            pltpu.VMEM((half, depth), jnp.bfloat16),
            pltpu.SemaphoreType.DMA((2, 2)),
            pltpu.SemaphoreType.DMA((depth // (2 * CHUNK) + 1,)),
        ],
        compiler_params=pltpu.CompilerParams(
            vmem_limit_bytes=(rest * 2 + depth) * half * 2 + (6 << 20)
        ),
        cost_estimate=pl.CostEstimate(
            flops=12 * rows * depth * half,
            bytes_accessed=(rest * 2 + depth) * half * 2,
            transcendentals=0,
        ),
        name="block",
    )(
        near,
        far,
        *(pltpu.with_memory_space_constraint(first, pltpu.VMEM) for first in firsts),
        w_gate,
        w_up,
        w_down,
    )


def finish_kernel(*refs):
    pieces, live_ref, out_ref = refs[:-2], refs[-2], refs[-1]
    totals = pieces[0][...].astype(jnp.float32)
    for piece in pieces[1:]:
        totals = totals + piece[...].astype(jnp.float32)
    totals = jnp.where(live_ref[:1] > 0, totals[0], jnp.zeros_like(totals[0]))
    for line in range(totals.shape[0]):
        out_ref[:, line * LANES : (line + 1) * LANES] = totals[line : line + 1].astype(jnp.bfloat16)


def finish(pieces, live):
    lines = pieces[0].shape[1]
    return pl.pallas_call(
        finish_kernel,
        out_shape=jax.ShapeDtypeStruct((1, lines * LANES), jnp.bfloat16),
        in_specs=[VMEM] * (len(pieces) + 1),
        out_specs=VMEM,
        compiler_params=pltpu.CompilerParams(vmem_limit_bytes=1 << 20),
        name="finish",
    )(*pieces, live)


def swap(value, axes, offset):
    places = range(lax.axis_size(axes))
    return lax.ppermute(value, axes, [(place, place ^ offset) for place in places])


def shared(tokens, norm_gain, w_gate, w_up, w_down, lengths, hit_lengths, start_positions):
    square = ("groups", "x")
    half = w_gate.shape[1] // lax.axis_size("groups")
    w_gate, w_up, w_down = (
        pltpu.with_memory_space_constraint(array, pltpu.HBM) for array in (w_gate, w_up, w_down)
    )
    requests = tuple(
        pltpu.with_memory_space_constraint(array, pltpu.HBM)
        for array in (lengths, hit_lengths, start_positions)
    )

    def place():
        return (lax.axis_index("z") * lax.axis_size("x") + lax.axis_index("x")) * lax.axis_size(
            "core"
        ) + lax.axis_index("core")

    deep = lax.axis_size("z")
    others = range(1, lax.axis_size(square))
    rows = [0] + list(range(2, deep)) + [1]
    column = [swap(tokens, "z", at) if at else tokens for at in rows]
    first, gain = load_first(w_gate, w_up, norm_gain.reshape(-1, LANES), half, 2 * CHUNK)
    column = stack(rows, column, gain)
    plane = [column] + [swap(column, square, at) for at in others]
    second, live = load_second(w_gate, w_up, half, 2 * CHUNK, 5 * CHUNK // 2, requests, place)
    near = pack(plane, gain, live)
    far = swap(near, "core", 1)
    kept, sent = block(near, far, (first, second), w_gate, w_up, w_down, half)
    plane = (kept + swap(sent, "core", 1).astype(jnp.float32)).astype(jnp.bfloat16)
    pieces = jnp.split(plane, lax.axis_size(square), axis=0)
    column = pieces[0].astype(jnp.float32)
    for piece in [swap(pieces[at], square, at) for at in reversed(others)]:
        column = column + piece.astype(jnp.float32)
    pieces = jnp.split(column.astype(jnp.bfloat16), deep, axis=0)
    return finish(
        pieces[:1] + [swap(piece, "z", at + 1) for at, piece in enumerate(pieces[1:])], live
    )


def solution(mesh):
    groups, members = mesh.shape["groups"], mesh.shape["tensor"]

    def placed(axes, whole):
        return (
            P(whole, None),
            P(),
            P(None, axes),
            P(None, axes),
            P(axes, None),
            P("groups"),
            P("groups"),
            P("groups"),
        )

    def run(*arrays):
        units = arrays[2].shape[1] // members
        if (
            units % (LANES * groups) == 0
            and arrays[0].shape[0] == groups * members
            and groups == 2
            and members >= 8
            and members & (members - 1) == 0
        ):
            body, axes, whole = shared, ("z", "x", "core"), ROW_LINES
            over = jax.sharding.Mesh(mesh.devices.reshape(groups, members // 4, 2, 2), ROW_LINES)
        else:
            body, axes, whole, over = local, "tensor", ("groups", "tensor"), mesh
        return jax.shard_map(
            body,
            mesh=over,
            in_specs=placed(axes, whole),
            out_specs=P(whole, None),
            check_vma=False,
        )(*arrays)

    return run
```

```python
import functools

import jax
import jax.numpy as jnp
from jax import lax
from jax.experimental import pallas as pl
from jax.experimental.pallas import tpu as pltpu
from jax.sharding import PartitionSpec as P

LANES = 128
ROW_LINES = ("groups", "z", "x", "core")


def normalize(tokens, norm_gain):
    values = tokens.astype(jnp.float32)
    mean_sq = jnp.mean(values * values, axis=-1, keepdims=True)
    return (values * lax.rsqrt(mean_sq + 1e-05) * norm_gain.astype(jnp.float32)).astype(
        jnp.bfloat16
    )


def live_rows(lengths, hit_lengths, start_positions, token_index):
    ends = jnp.cumsum(lengths)
    begins = ends - lengths
    member = (token_index[:, None] >= begins[None, :]) & (token_index[:, None] < ends[None, :])
    member_int = member.astype(jnp.int32)
    offsets = token_index - jnp.sum(member_int * begins[None, :], axis=1)
    position = jnp.sum(member_int * start_positions[None, :], axis=1) + offsets
    covered = jnp.sum(member_int * hit_lengths[None, :], axis=1)
    return position >= covered


def local(tokens, norm_gain, w_gate, w_up, w_down, lengths, hit_lengths, start_positions):
    row_count = tokens.shape[0]
    normed = normalize(tokens, norm_gain)
    piece_rows = lax.all_gather(normed, "tensor", axis=0, tiled=True)
    gate_out = jnp.dot(piece_rows, w_gate, preferred_element_type=jnp.float32)
    up_out = jnp.dot(piece_rows, w_up, preferred_element_type=jnp.float32)
    hidden = (jax.nn.silu(gate_out) * up_out).astype(jnp.bfloat16)
    partial_value = jnp.dot(hidden, w_down, preferred_element_type=jnp.float32)
    rounded = partial_value.astype(jnp.bfloat16)
    totals = jnp.sum(
        lax.all_to_all(rounded[None], "tensor", split_axis=1, concat_axis=0, tiled=True).astype(
            jnp.float32
        ),
        axis=0,
    )
    token_index = lax.axis_index("tensor") * row_count + jnp.arange(row_count, dtype=jnp.int32)
    live = live_rows(lengths, hit_lengths, start_positions, token_index)
    return jnp.where(live[:, None], totals, jnp.zeros_like(totals)).astype(jnp.bfloat16)


VMEM = pl.BlockSpec(memory_space=pltpu.VMEM)
HBM = pl.BlockSpec(memory_space=pltpu.HBM)
CHUNK = 1024


def live_flag(lengths, hit_lengths, start_positions, token):
    begin = 0
    live = False
    for request in range(lengths.shape[0]):
        end = begin + lengths[request]
        position = start_positions[request] + token - begin
        inside = (token >= begin) & (token < end)
        live = live | (inside & (position >= hit_lengths[request]))
        begin = end
    return live


def stack_kernel(rows, *refs):
    pieces, out_ref, wide_ref = refs[:-3], refs[-2], refs[-1]
    lines = out_ref.shape[1]
    for at, piece in zip(rows, pieces):
        values = piece[...].astype(jnp.float32)
        for line in range(lines):
            wide_ref[at, line : line + 1] = values[:, line * LANES : (line + 1) * LANES]
    out_ref[...] = wide_ref[...].astype(out_ref.dtype)


def stack(rows, pieces, gain):
    shape = (len(pieces), pieces[0].shape[1] // LANES, LANES)
    return pl.pallas_call(
        functools.partial(stack_kernel, rows),
        out_shape=jax.ShapeDtypeStruct(shape, pieces[0].dtype),
        in_specs=[VMEM] * len(pieces) + [pl.BlockSpec(memory_space=pl.ANY)],
        out_specs=VMEM,
        scratch_shapes=[pltpu.VMEM(shape, jnp.float32)],
        compiler_params=pltpu.CompilerParams(vmem_limit_bytes=2 << 20),
        name="stack",
    )(*pieces, gain)


def load_gain_kernel(half, gate_hbm, up_hbm, gain_hbm, both_vmem, gain_vmem, sems):
    own = pl.multiple_of(lax.axis_index("groups") * half, LANES)
    copies = [pltpu.make_async_copy(gain_hbm, gain_vmem, sems.at[2])] + [
        pltpu.make_async_copy(
            weight.at[pl.ds(0, both_vmem.shape[0]), pl.ds(own, half)],
            both_vmem.at[:, pl.ds(at * half, half)],
            sems.at[at],
        )
        for at, weight in enumerate((gate_hbm, up_hbm))
    ]
    for copy in copies:
        copy.start()
    for copy in copies:
        copy.wait()


def load_first(w_gate, w_up, gain, half, count):
    return pl.pallas_call(
        functools.partial(load_gain_kernel, half),
        out_shape=(
            pltpu.VMEM((count, 2 * half), w_gate.dtype),
            pltpu.VMEM(gain.shape, gain.dtype),
        ),
        in_specs=[HBM] * 3,
        out_specs=(VMEM, VMEM),
        scratch_shapes=[pltpu.SemaphoreType.DMA((3,))],
        compiler_params=pltpu.CompilerParams(vmem_limit_bytes=1 << 20),
        cost_estimate=pl.CostEstimate(
            flops=0, bytes_accessed=2 * count * half * 2, transcendentals=0
        ),
        name="load_first",
    )(w_gate, w_up, pltpu.with_memory_space_constraint(gain, pltpu.HBM))


def load_second_kernel(
    half,
    row,
    place,
    lengths,
    hit_lengths,
    start_positions,
    gate_hbm,
    up_hbm,
    both_vmem,
    mark_vmem,
    lengths_smem,
    hit_smem,
    start_smem,
    sems,
):
    own = pl.multiple_of(lax.axis_index("groups") * half, LANES)
    small = [
        pltpu.make_async_copy(source, target, sems.at[2 + at])
        for at, (source, target) in enumerate(
            ((lengths, lengths_smem), (hit_lengths, hit_smem), (start_positions, start_smem))
        )
    ]
    copies = [
        pltpu.make_async_copy(
            weight.at[pl.ds(row, both_vmem.shape[0]), pl.ds(own, half)],
            both_vmem.at[:, pl.ds(at * half, half)],
            sems.at[at],
        )
        for at, weight in enumerate((gate_hbm, up_hbm))
    ]
    for copy in small + copies:
        copy.start()
    for copy in small:
        copy.wait()
    live = live_flag(lengths_smem, hit_smem, start_smem, place())
    mark_vmem[...] = jnp.full(mark_vmem.shape, live.astype(jnp.float32), jnp.float32)
    for copy in copies:
        copy.wait()


def load_second(w_gate, w_up, half, row, count, requests, place):
    return pl.pallas_call(
        functools.partial(load_second_kernel, half, row, place),
        out_shape=(
            pltpu.VMEM((count, 2 * half), w_gate.dtype),
            jax.ShapeDtypeStruct((8, LANES), jnp.float32),
        ),
        in_specs=[HBM] * (2 + len(requests)),
        out_specs=(VMEM, VMEM),
        scratch_shapes=[pltpu.SMEM(array.shape, array.dtype) for array in requests]
        + [pltpu.SemaphoreType.DMA((5,))],
        compiler_params=pltpu.CompilerParams(vmem_limit_bytes=1 << 20),
        cost_estimate=pl.CostEstimate(
            flops=0, bytes_accessed=2 * count * half * 2, transcendentals=0
        ),
        name="load_second",
    )(*requests, w_gate, w_up)


def pack_kernel(*refs):
    pieces, gain_ref, out_ref, wide_ref = refs[:-4], refs[-4], refs[-2], refs[-1]
    rows = out_ref.shape[0]
    lines = out_ref.shape[1] // LANES
    stride = wide_ref.shape[0] // rows
    gain = gain_ref[...].astype(jnp.float32)
    row = 0
    for piece in pieces:
        values = piece[...].astype(jnp.float32)
        mean_sq = jnp.sum(values * values, axis=(1, 2), keepdims=True) * (1.0 / (lines * LANES))
        scaled = values * lax.rsqrt(mean_sq + 1e-05) * gain[None]
        for at in range(piece.shape[0]):
            wide_ref[row * stride : row * stride + lines] = scaled[at]
            row += 1
    for line in range(lines):
        out_ref[:, line * LANES : (line + 1) * LANES] = wide_ref[
            pl.ds(line, rows, stride=stride), :
        ].astype(jnp.bfloat16)


def pack(pieces, gain, mark):
    rows = sum(piece.shape[0] for piece in pieces)
    lines = pieces[0].shape[1]
    return pl.pallas_call(
        pack_kernel,
        out_shape=jax.ShapeDtypeStruct((rows, lines * LANES), jnp.bfloat16),
        in_specs=[VMEM] * (len(pieces) + 1) + [pl.BlockSpec(memory_space=pl.ANY)],
        out_specs=VMEM,
        scratch_shapes=[pltpu.VMEM((rows * (lines + 1), LANES), jnp.float32)],
        compiler_params=pltpu.CompilerParams(vmem_limit_bytes=4 << 20),
        name="pack",
    )(*pieces, pltpu.with_memory_space_constraint(gain, pltpu.VMEM), mark)


def block_kernel(
    half,
    chunk,
    deals,
    near_ref,
    far_ref,
    first_refs,
    gate_hbm,
    up_hbm,
    down_hbm,
    keep_ref,
    send_ref,
    wide_ref,
    rows_ref,
    product_ref,
    hidden_ref,
    rest_ref,
    down_ref,
    both_sems,
    down_sems,
):
    tile = 512
    rows, depth = rows_ref.shape
    lanes = LANES
    lines = depth // lanes
    stride = wide_ref.shape[0] // rows
    loaded = sum(ref.shape[0] for ref in first_refs)
    own = pl.multiple_of(lax.axis_index("groups") * half, LANES)
    loads = []
    at = 0
    for step, deal in enumerate(deals):
        loads.append(
            [
                pltpu.make_async_copy(
                    weight.at[pl.ds(loaded + at, deal), pl.ds(own, half)],
                    rest_ref.at[pl.ds(at, deal), pl.ds(side * half, half)],
                    both_sems.at[step, side],
                )
                for side, weight in enumerate((gate_hbm, up_hbm))
            ]
        )
        at += deal
    pairs = len(loads)
    spans = []
    while sum(width for _, width in spans) < depth:
        at = sum(width for _, width in spans)
        spans.append((at, chunk if depth - at > chunk else chunk // 2))
    for step, (at, width) in enumerate(spans):
        loads.append(
            [
                pltpu.make_async_copy(
                    down_hbm.at[pl.ds(own, half), pl.ds(at, width)],
                    down_ref.at[:, pl.ds(at, width)],
                    down_sems.at[step],
                )
            ]
        )

    waiting = list(loads)

    def start():
        if waiting:
            for copy in waiting.pop(0):
                copy.start()

    def wait(number):
        for copy in loads[number]:
            copy.wait()

    def multiply(at, count, ref, row, halfway):
        for column in range(0, 2 * half, tile):
            columns = pl.ds(column, min(tile, 2 * half - column))
            value = jnp.dot(
                rows_ref[:, at : at + count],
                ref[row : row + count, columns],
                preferred_element_type=jnp.float32,
            )
            if at == 0:
                product_ref[:, columns] = value
            else:
                product_ref[:, columns] += value
            if halfway and column == tile:
                start()

    start()
    rows_ref[: rows // 2] = near_ref[...]
    rows_ref[rows // 2 :] = far_ref[...]
    at = 0
    for ref in first_refs:
        multiply(at, ref.shape[0], ref, 0, False)
        start()
        at += ref.shape[0]
    row = 0
    for step, deal in enumerate(deals):
        wait(step)
        multiply(at, deal, rest_ref, row, step < pairs - 1)
        start()
        at += deal
        row += deal
    while waiting:
        start()
    gate_out = product_ref[:, :half]
    up_out = product_ref[:, half:]
    hidden_ref[...] = (gate_out / (1.0 + jnp.exp(-gate_out)) * up_out).astype(jnp.bfloat16)
    zero = jnp.minimum(lax.axis_index("core"), 0)
    for step, (begin, width) in enumerate(spans):
        wait(pairs + step)
        for at in range(begin, begin + width, tile):
            result = jnp.dot(
                hidden_ref[...], down_ref[:, pl.ds(at, tile)], preferred_element_type=jnp.float32
            )
            for line in range(tile // lanes):
                wide_ref[pl.ds(at // lanes + line, rows, stride=stride), :] = result[
                    :, line * lanes : (line + 1) * lanes
                ]
        done = begin // lanes
        count = width // lanes
        for row in range(rows // 2):
            keep_ref[row + zero, done : done + count] = wide_ref[
                row * stride + done : row * stride + done + count
            ]
            at = (row + rows // 2) * stride + done
            send_ref[row + zero, done : done + count] = wide_ref[at : at + count].astype(
                jnp.bfloat16
            )


def block(near, far, firsts, w_gate, w_up, w_down, half):
    rows, depth = near.shape
    lines = depth // LANES
    rest = depth - sum(first.shape[0] for first in firsts)
    deals = (rest * 3 // 8, rest * 3 // 8, rest // 4)

    def body(near_ref, far_ref, *refs):
        count = len(firsts)
        block_kernel(half, 2 * CHUNK, deals, near_ref, far_ref, refs[:count], *refs[count:])

    return pl.pallas_call(
        body,
        out_shape=(
            jax.ShapeDtypeStruct((rows, lines, LANES), jnp.float32),
            jax.ShapeDtypeStruct((rows, lines, LANES), jnp.bfloat16),
        ),
        in_specs=[VMEM] * (2 + len(firsts)) + [HBM] * 3,
        out_specs=(VMEM, VMEM),
        scratch_shapes=[
            pltpu.VMEM((2 * rows * (lines + 1), LANES), jnp.float32),
            pltpu.VMEM((2 * rows, depth), jnp.bfloat16),
            pltpu.VMEM((2 * rows, 2 * half), jnp.float32),
            pltpu.VMEM((2 * rows, half), jnp.bfloat16),
            pltpu.VMEM((rest, 2 * half), jnp.bfloat16),
            pltpu.VMEM((half, depth), jnp.bfloat16),
            pltpu.SemaphoreType.DMA((len(deals), 2)),
            pltpu.SemaphoreType.DMA((depth // (2 * CHUNK) + 1,)),
        ],
        compiler_params=pltpu.CompilerParams(
            vmem_limit_bytes=(rest * 2 + depth) * half * 2 + (6 << 20)
        ),
        cost_estimate=pl.CostEstimate(
            flops=12 * rows * depth * half,
            bytes_accessed=(rest * 2 + depth) * half * 2,
            transcendentals=0,
        ),
        name="block",
    )(
        near,
        far,
        *(pltpu.with_memory_space_constraint(first, pltpu.VMEM) for first in firsts),
        w_gate,
        w_up,
        w_down,
    )


def finish_kernel(*refs):
    pieces, live_ref, out_ref = refs[:-2], refs[-2], refs[-1]
    totals = pieces[0][...].astype(jnp.float32)
    for piece in pieces[1:]:
        totals = totals + piece[...].astype(jnp.float32)
    totals = jnp.where(live_ref[:1] > 0, totals[0], jnp.zeros_like(totals[0]))
    for line in range(totals.shape[0]):
        out_ref[:, line * LANES : (line + 1) * LANES] = totals[line : line + 1].astype(jnp.bfloat16)


def finish(pieces, live):
    lines = pieces[0].shape[1]
    return pl.pallas_call(
        finish_kernel,
        out_shape=jax.ShapeDtypeStruct((1, lines * LANES), jnp.bfloat16),
        in_specs=[VMEM] * (len(pieces) + 1),
        out_specs=VMEM,
        compiler_params=pltpu.CompilerParams(vmem_limit_bytes=1 << 20),
        name="finish",
    )(*pieces, live)


def swap(value, axes, offset):
    places = range(lax.axis_size(axes))
    return lax.ppermute(value, axes, [(place, place ^ offset) for place in places])


def shared(tokens, norm_gain, w_gate, w_up, w_down, lengths, hit_lengths, start_positions):
    square = ("groups", "x")
    half = w_gate.shape[1] // lax.axis_size("groups")
    w_gate, w_up, w_down = (
        pltpu.with_memory_space_constraint(array, pltpu.HBM) for array in (w_gate, w_up, w_down)
    )
    requests = tuple(
        pltpu.with_memory_space_constraint(array, pltpu.HBM)
        for array in (lengths, hit_lengths, start_positions)
    )

    def place():
        return (lax.axis_index("z") * lax.axis_size("x") + lax.axis_index("x")) * lax.axis_size(
            "core"
        ) + lax.axis_index("core")

    deep = lax.axis_size("z")
    others = range(1, lax.axis_size(square))
    rows = [0] + list(range(2, deep)) + [1]
    column = [swap(tokens, "z", at) if at else tokens for at in rows]
    first, gain = load_first(w_gate, w_up, norm_gain.reshape(-1, LANES), half, 3 * CHUNK // 2)
    column = stack(rows, column, gain)
    plane = [column] + [swap(column, square, at) for at in others]
    second, live = load_second(w_gate, w_up, half, 3 * CHUNK // 2, 5 * CHUNK // 2, requests, place)
    near = pack(plane, gain, live)
    far = swap(near, "core", 1)
    kept, sent = block(near, far, (first, second), w_gate, w_up, w_down, half)
    plane = (kept + swap(sent, "core", 1).astype(jnp.float32)).astype(jnp.bfloat16)
    pieces = jnp.split(plane, lax.axis_size(square), axis=0)
    column = pieces[0].astype(jnp.float32)
    for piece in [swap(pieces[at], square, at) for at in reversed(others)]:
        column = column + piece.astype(jnp.float32)
    pieces = jnp.split(column.astype(jnp.bfloat16), deep, axis=0)
    return finish(
        pieces[:1] + [swap(piece, "z", at + 1) for at, piece in enumerate(pieces[1:])], live
    )


def solution(mesh):
    groups, members = mesh.shape["groups"], mesh.shape["tensor"]

    def placed(axes, whole):
        return (
            P(whole, None),
            P(),
            P(None, axes),
            P(None, axes),
            P(axes, None),
            P("groups"),
            P("groups"),
            P("groups"),
        )

    def run(*arrays):
        units = arrays[2].shape[1] // members
        if (
            units % (LANES * groups) == 0
            and arrays[0].shape[0] == groups * members
            and groups == 2
            and members >= 8
            and members & (members - 1) == 0
        ):
            body, axes, whole = shared, ("z", "x", "core"), ROW_LINES
            over = jax.sharding.Mesh(mesh.devices.reshape(groups, members // 4, 2, 2), ROW_LINES)
        else:
            body, axes, whole, over = local, "tensor", ("groups", "tensor"), mesh
        return jax.shard_map(
            body,
            mesh=over,
            in_specs=placed(axes, whole),
            out_specs=P(whole, None),
            check_vma=False,
        )(*arrays)

    return run
```

```python
import functools

import jax
import jax.numpy as jnp
from jax import lax
from jax.experimental import pallas as pl
from jax.experimental.pallas import tpu as pltpu
from jax.sharding import PartitionSpec as P

LANES = 128
ROW_LINES = ("groups", "z", "x", "core")


def normalize(tokens, norm_gain):
    values = tokens.astype(jnp.float32)
    mean_sq = jnp.mean(values * values, axis=-1, keepdims=True)
    return (values * lax.rsqrt(mean_sq + 1e-05) * norm_gain.astype(jnp.float32)).astype(
        jnp.bfloat16
    )


def live_rows(lengths, hit_lengths, start_positions, token_index):
    ends = jnp.cumsum(lengths)
    begins = ends - lengths
    member = (token_index[:, None] >= begins[None, :]) & (token_index[:, None] < ends[None, :])
    member_int = member.astype(jnp.int32)
    offsets = token_index - jnp.sum(member_int * begins[None, :], axis=1)
    position = jnp.sum(member_int * start_positions[None, :], axis=1) + offsets
    covered = jnp.sum(member_int * hit_lengths[None, :], axis=1)
    return position >= covered


def local(tokens, norm_gain, w_gate, w_up, w_down, lengths, hit_lengths, start_positions):
    row_count = tokens.shape[0]
    normed = normalize(tokens, norm_gain)
    piece_rows = lax.all_gather(normed, "tensor", axis=0, tiled=True)
    gate_out = jnp.dot(piece_rows, w_gate, preferred_element_type=jnp.float32)
    up_out = jnp.dot(piece_rows, w_up, preferred_element_type=jnp.float32)
    hidden = (jax.nn.silu(gate_out) * up_out).astype(jnp.bfloat16)
    partial_value = jnp.dot(hidden, w_down, preferred_element_type=jnp.float32)
    rounded = partial_value.astype(jnp.bfloat16)
    totals = jnp.sum(
        lax.all_to_all(rounded[None], "tensor", split_axis=1, concat_axis=0, tiled=True).astype(
            jnp.float32
        ),
        axis=0,
    )
    token_index = lax.axis_index("tensor") * row_count + jnp.arange(row_count, dtype=jnp.int32)
    live = live_rows(lengths, hit_lengths, start_positions, token_index)
    return jnp.where(live[:, None], totals, jnp.zeros_like(totals)).astype(jnp.bfloat16)


VMEM = pl.BlockSpec(memory_space=pltpu.VMEM)
HBM = pl.BlockSpec(memory_space=pltpu.HBM)
CHUNK = 1024


def live_flag(lengths, hit_lengths, start_positions, token):
    begin = 0
    live = False
    for request in range(lengths.shape[0]):
        end = begin + lengths[request]
        position = start_positions[request] + token - begin
        inside = (token >= begin) & (token < end)
        live = live | (inside & (position >= hit_lengths[request]))
        begin = end
    return live


def stack_kernel(rows, *refs):
    pieces, out_ref, wide_ref = refs[:-3], refs[-2], refs[-1]
    lines = out_ref.shape[1]
    for at, piece in zip(rows, pieces):
        values = piece[...].astype(jnp.float32)
        for line in range(lines):
            wide_ref[at, line : line + 1] = values[:, line * LANES : (line + 1) * LANES]
    out_ref[...] = wide_ref[...].astype(out_ref.dtype)


def stack(rows, pieces, gain):
    shape = (len(pieces), pieces[0].shape[1] // LANES, LANES)
    return pl.pallas_call(
        functools.partial(stack_kernel, rows),
        out_shape=jax.ShapeDtypeStruct(shape, pieces[0].dtype),
        in_specs=[VMEM] * len(pieces) + [pl.BlockSpec(memory_space=pl.ANY)],
        out_specs=VMEM,
        scratch_shapes=[pltpu.VMEM(shape, jnp.float32)],
        compiler_params=pltpu.CompilerParams(vmem_limit_bytes=2 << 20),
        name="stack",
    )(*pieces, gain)


def load_gain_kernel(half, gate_hbm, up_hbm, gain_hbm, both_vmem, gain_vmem, sems):
    own = pl.multiple_of(lax.axis_index("groups") * half, LANES)
    copies = [pltpu.make_async_copy(gain_hbm, gain_vmem, sems.at[2])] + [
        pltpu.make_async_copy(
            weight.at[pl.ds(0, both_vmem.shape[0]), pl.ds(own, half)],
            both_vmem.at[:, pl.ds(at * half, half)],
            sems.at[at],
        )
        for at, weight in enumerate((gate_hbm, up_hbm))
    ]
    for copy in copies:
        copy.start()
    for copy in copies:
        copy.wait()


def load_first(w_gate, w_up, gain, half, count):
    return pl.pallas_call(
        functools.partial(load_gain_kernel, half),
        out_shape=(
            pltpu.VMEM((count, 2 * half), w_gate.dtype),
            pltpu.VMEM(gain.shape, gain.dtype),
        ),
        in_specs=[HBM] * 3,
        out_specs=(VMEM, VMEM),
        scratch_shapes=[pltpu.SemaphoreType.DMA((3,))],
        compiler_params=pltpu.CompilerParams(vmem_limit_bytes=1 << 20),
        cost_estimate=pl.CostEstimate(
            flops=0, bytes_accessed=2 * count * half * 2, transcendentals=0
        ),
        name="load_first",
    )(w_gate, w_up, pltpu.with_memory_space_constraint(gain, pltpu.HBM))


def load_second_kernel(
    half,
    row,
    place,
    lengths,
    hit_lengths,
    start_positions,
    gate_hbm,
    up_hbm,
    both_vmem,
    mark_vmem,
    lengths_smem,
    hit_smem,
    start_smem,
    sems,
):
    own = pl.multiple_of(lax.axis_index("groups") * half, LANES)
    small = [
        pltpu.make_async_copy(source, target, sems.at[2 + at])
        for at, (source, target) in enumerate(
            ((lengths, lengths_smem), (hit_lengths, hit_smem), (start_positions, start_smem))
        )
    ]
    copies = [
        pltpu.make_async_copy(
            weight.at[pl.ds(row, both_vmem.shape[0]), pl.ds(own, half)],
            both_vmem.at[:, pl.ds(at * half, half)],
            sems.at[at],
        )
        for at, weight in enumerate((gate_hbm, up_hbm))
    ]
    for copy in small + copies:
        copy.start()
    for copy in small:
        copy.wait()
    live = live_flag(lengths_smem, hit_smem, start_smem, place())
    mark_vmem[...] = jnp.full(mark_vmem.shape, live.astype(jnp.float32), jnp.float32)
    for copy in copies:
        copy.wait()


def load_second(w_gate, w_up, half, row, count, requests, place):
    return pl.pallas_call(
        functools.partial(load_second_kernel, half, row, place),
        out_shape=(
            pltpu.VMEM((count, 2 * half), w_gate.dtype),
            jax.ShapeDtypeStruct((8, LANES), jnp.float32),
        ),
        in_specs=[HBM] * (2 + len(requests)),
        out_specs=(VMEM, VMEM),
        scratch_shapes=[pltpu.SMEM(array.shape, array.dtype) for array in requests]
        + [pltpu.SemaphoreType.DMA((5,))],
        compiler_params=pltpu.CompilerParams(vmem_limit_bytes=1 << 20),
        cost_estimate=pl.CostEstimate(
            flops=0, bytes_accessed=2 * count * half * 2, transcendentals=0
        ),
        name="load_second",
    )(*requests, w_gate, w_up)


def pack_kernel(*refs):
    pieces, gain_ref, out_ref, wide_ref = refs[:-4], refs[-4], refs[-2], refs[-1]
    rows = out_ref.shape[0]
    lines = out_ref.shape[1] // LANES
    stride = wide_ref.shape[0] // rows
    gain = gain_ref[...].astype(jnp.float32)
    row = 0
    for piece in pieces:
        values = piece[...].astype(jnp.float32)
        mean_sq = jnp.sum(values * values, axis=(1, 2), keepdims=True) * (1.0 / (lines * LANES))
        scaled = values * lax.rsqrt(mean_sq + 1e-05) * gain[None]
        for at in range(piece.shape[0]):
            wide_ref[row * stride : row * stride + lines] = scaled[at]
            row += 1
    for line in range(lines):
        out_ref[:, line * LANES : (line + 1) * LANES] = wide_ref[
            pl.ds(line, rows, stride=stride), :
        ].astype(jnp.bfloat16)


def pack(pieces, gain, mark):
    rows = sum(piece.shape[0] for piece in pieces)
    lines = pieces[0].shape[1]
    return pl.pallas_call(
        pack_kernel,
        out_shape=jax.ShapeDtypeStruct((rows, lines * LANES), jnp.bfloat16),
        in_specs=[VMEM] * (len(pieces) + 1) + [pl.BlockSpec(memory_space=pl.ANY)],
        out_specs=VMEM,
        scratch_shapes=[pltpu.VMEM((rows * (lines + 1), LANES), jnp.float32)],
        compiler_params=pltpu.CompilerParams(vmem_limit_bytes=4 << 20),
        name="pack",
    )(*pieces, pltpu.with_memory_space_constraint(gain, pltpu.VMEM), mark)


def block_kernel(
    half,
    chunk,
    deals,
    near_ref,
    far_ref,
    first_refs,
    gate_hbm,
    up_hbm,
    down_hbm,
    keep_ref,
    send_ref,
    wide_ref,
    rows_ref,
    product_ref,
    hidden_ref,
    rest_ref,
    down_ref,
    both_sems,
    down_sems,
):
    tile = 512
    rows, depth = rows_ref.shape
    lanes = LANES
    lines = depth // lanes
    stride = wide_ref.shape[0] // rows
    loaded = sum(ref.shape[0] for ref in first_refs)
    own = pl.multiple_of(lax.axis_index("groups") * half, LANES)
    loads = []
    at = 0
    for step, deal in enumerate(deals):
        loads.append(
            [
                pltpu.make_async_copy(
                    weight.at[pl.ds(loaded + at, deal), pl.ds(own, half)],
                    rest_ref.at[pl.ds(at, deal), pl.ds(side * half, half)],
                    both_sems.at[step, side],
                )
                for side, weight in enumerate((gate_hbm, up_hbm))
            ]
        )
        at += deal
    pairs = len(loads)
    spans = []
    while sum(width for _, width in spans) < depth:
        at = sum(width for _, width in spans)
        spans.append((at, chunk if depth - at > chunk else chunk // 2))
    for step, (at, width) in enumerate(spans):
        loads.append(
            [
                pltpu.make_async_copy(
                    down_hbm.at[pl.ds(own, half), pl.ds(at, width)],
                    down_ref.at[:, pl.ds(at, width)],
                    down_sems.at[step],
                )
            ]
        )

    waiting = list(loads)

    def start():
        if waiting:
            for copy in waiting.pop(0):
                copy.start()

    def wait(number):
        for copy in loads[number]:
            copy.wait()

    def multiply(terms, first, halfway):
        for column in range(0, 2 * half, tile):
            columns = pl.ds(column, min(tile, 2 * half - column))
            value = None
            for at, count, ref, row in terms:
                term = jnp.dot(
                    rows_ref[:, at : at + count],
                    ref[row : row + count, columns],
                    preferred_element_type=jnp.float32,
                )
                value = term if value is None else value + term
            if first:
                product_ref[:, columns] = value
            else:
                product_ref[:, columns] += value
            if halfway and column == tile:
                start()

    start()
    rows_ref[: rows // 2] = near_ref[...]
    rows_ref[rows // 2 :] = far_ref[...]
    at = 0
    held = []
    for ref in first_refs:
        held.append((at, ref.shape[0], ref, 0))
        at += ref.shape[0]
    multiply(held, True, True)
    start()
    row = 0
    for step, deal in enumerate(deals):
        wait(step)
        multiply([(at, deal, rest_ref, row)], False, True)
        start()
        at += deal
        row += deal
    while waiting:
        start()
    gate_out = product_ref[:, :half]
    up_out = product_ref[:, half:]
    hidden_ref[...] = (gate_out / (1.0 + jnp.exp(-gate_out)) * up_out).astype(jnp.bfloat16)
    zero = jnp.minimum(lax.axis_index("core"), 0)
    for step, (begin, width) in enumerate(spans):
        wait(pairs + step)
        for at in range(begin, begin + width, tile):
            result = jnp.dot(
                hidden_ref[...], down_ref[:, pl.ds(at, tile)], preferred_element_type=jnp.float32
            )
            for line in range(tile // lanes):
                wide_ref[pl.ds(at // lanes + line, rows, stride=stride), :] = result[
                    :, line * lanes : (line + 1) * lanes
                ]
        done = begin // lanes
        count = width // lanes
        for row in range(rows // 2):
            keep_ref[row + zero, done : done + count] = wide_ref[
                row * stride + done : row * stride + done + count
            ]
            at = (row + rows // 2) * stride + done
            send_ref[row + zero, done : done + count] = wide_ref[at : at + count].astype(
                jnp.bfloat16
            )


def block(near, far, firsts, w_gate, w_up, w_down, half):
    rows, depth = near.shape
    lines = depth // LANES
    rest = depth - sum(first.shape[0] for first in firsts)
    deals = (rest * 3 // 7, rest - rest * 3 // 7)

    def body(near_ref, far_ref, *refs):
        count = len(firsts)
        block_kernel(half, 2 * CHUNK, deals, near_ref, far_ref, refs[:count], *refs[count:])

    return pl.pallas_call(
        body,
        out_shape=(
            jax.ShapeDtypeStruct((rows, lines, LANES), jnp.float32),
            jax.ShapeDtypeStruct((rows, lines, LANES), jnp.bfloat16),
        ),
        in_specs=[VMEM] * (2 + len(firsts)) + [HBM] * 3,
        out_specs=(VMEM, VMEM),
        scratch_shapes=[
            pltpu.VMEM((2 * rows * (lines + 1), LANES), jnp.float32),
            pltpu.VMEM((2 * rows, depth), jnp.bfloat16),
            pltpu.VMEM((2 * rows, 2 * half), jnp.float32),
            pltpu.VMEM((2 * rows, half), jnp.bfloat16),
            pltpu.VMEM((rest, 2 * half), jnp.bfloat16),
            pltpu.VMEM((half, depth), jnp.bfloat16),
            pltpu.SemaphoreType.DMA((2, 2)),
            pltpu.SemaphoreType.DMA((depth // (2 * CHUNK) + 1,)),
        ],
        compiler_params=pltpu.CompilerParams(
            vmem_limit_bytes=(rest * 2 + depth) * half * 2 + (6 << 20)
        ),
        cost_estimate=pl.CostEstimate(
            flops=12 * rows * depth * half,
            bytes_accessed=(rest * 2 + depth) * half * 2,
            transcendentals=0,
        ),
        name="block",
    )(
        near,
        far,
        *(pltpu.with_memory_space_constraint(first, pltpu.VMEM) for first in firsts),
        w_gate,
        w_up,
        w_down,
    )


def finish_kernel(*refs):
    pieces, live_ref, out_ref = refs[:-2], refs[-2], refs[-1]
    totals = pieces[0][...].astype(jnp.float32)
    for piece in pieces[1:]:
        totals = totals + piece[...].astype(jnp.float32)
    totals = jnp.where(live_ref[:1] > 0, totals[0], jnp.zeros_like(totals[0]))
    for line in range(totals.shape[0]):
        out_ref[:, line * LANES : (line + 1) * LANES] = totals[line : line + 1].astype(jnp.bfloat16)


def finish(pieces, live):
    lines = pieces[0].shape[1]
    return pl.pallas_call(
        finish_kernel,
        out_shape=jax.ShapeDtypeStruct((1, lines * LANES), jnp.bfloat16),
        in_specs=[VMEM] * (len(pieces) + 1),
        out_specs=VMEM,
        compiler_params=pltpu.CompilerParams(vmem_limit_bytes=1 << 20),
        name="finish",
    )(*pieces, live)


def swap(value, axes, offset):
    places = range(lax.axis_size(axes))
    return lax.ppermute(value, axes, [(place, place ^ offset) for place in places])


def shared(tokens, norm_gain, w_gate, w_up, w_down, lengths, hit_lengths, start_positions):
    square = ("groups", "x")
    half = w_gate.shape[1] // lax.axis_size("groups")
    w_gate, w_up, w_down = (
        pltpu.with_memory_space_constraint(array, pltpu.HBM) for array in (w_gate, w_up, w_down)
    )
    requests = tuple(
        pltpu.with_memory_space_constraint(array, pltpu.HBM)
        for array in (lengths, hit_lengths, start_positions)
    )

    def place():
        return (lax.axis_index("z") * lax.axis_size("x") + lax.axis_index("x")) * lax.axis_size(
            "core"
        ) + lax.axis_index("core")

    deep = lax.axis_size("z")
    others = range(1, lax.axis_size(square))
    rows = [0] + list(range(2, deep)) + [1]
    column = [swap(tokens, "z", at) if at else tokens for at in rows]
    first, gain = load_first(w_gate, w_up, norm_gain.reshape(-1, LANES), half, 2 * CHUNK)
    column = stack(rows, column, gain)
    plane = [column] + [swap(column, square, at) for at in others]
    second, live = load_second(w_gate, w_up, half, 2 * CHUNK, 5 * CHUNK // 2, requests, place)
    near = pack(plane, gain, live)
    far = swap(near, "core", 1)
    kept, sent = block(near, far, (first, second), w_gate, w_up, w_down, half)
    plane = (kept + swap(sent, "core", 1).astype(jnp.float32)).astype(jnp.bfloat16)
    pieces = jnp.split(plane, lax.axis_size(square), axis=0)
    column = pieces[0].astype(jnp.float32)
    for piece in [swap(pieces[at], square, at) for at in reversed(others)]:
        column = column + piece.astype(jnp.float32)
    pieces = jnp.split(column.astype(jnp.bfloat16), deep, axis=0)
    return finish(
        pieces[:1] + [swap(piece, "z", at + 1) for at, piece in enumerate(pieces[1:])], live
    )


def solution(mesh):
    groups, members = mesh.shape["groups"], mesh.shape["tensor"]

    def placed(axes, whole):
        return (
            P(whole, None),
            P(),
            P(None, axes),
            P(None, axes),
            P(axes, None),
            P("groups"),
            P("groups"),
            P("groups"),
        )

    def run(*arrays):
        units = arrays[2].shape[1] // members
        if (
            units % (LANES * groups) == 0
            and arrays[0].shape[0] == groups * members
            and groups == 2
            and members >= 8
            and members & (members - 1) == 0
        ):
            body, axes, whole = shared, ("z", "x", "core"), ROW_LINES
            over = jax.sharding.Mesh(mesh.devices.reshape(groups, members // 4, 2, 2), ROW_LINES)
        else:
            body, axes, whole, over = local, "tensor", ("groups", "tensor"), mesh
        return jax.shard_map(
            body,
            mesh=over,
            in_specs=placed(axes, whole),
            out_specs=P(whole, None),
            check_vma=False,
        )(*arrays)

    return run
```
